256 devices in a mesh: tm: 32 (over x, y, core), state: 8 (over z).
Axes of the slice: x: 4, y: 4, z: 8, core: 2. Of those that a mesh axis runs over, the one named last changes fastest.
Arguments:
- observations: float32 [128, 4096], P('tm'), may hold values from -6 to 6
- precisions: float32 [128, 4096], P('tm'), may hold values from 0.25 to 4
- blocks: bfloat16 [128, 256, 64, 64], P('tm', 'state'), may hold values from -0.09375 to 0.09375
- block_rows: int32 [128, 256], P('tm', 'state'), may hold values from 0 to 63
- block_cols: int32 [128, 256], P('tm', 'state'), may hold values from 0 to 15
- transition: bfloat16 [128, 1024, 1024], P('tm', 'state'), may hold values from -1 to 1
- prior: float32 [1024], replicated, may hold values from -8 to 8
Outputs:
- filtered: float32 [128, 1024], P('tm', 'state')
The draws below stay inside these ranges and needn't reach their ends.
All inputs are finite; a program needn't handle non-finite values.
Results may differ from the reference program's by a relative error of at most 0.014.
Values may be sent and summed in bfloat16 or wider, within the bound.
No kernel may reach another device: no remote copies, remote signals or barrier semaphores. Data moves between devices by JAX's collectives and lax.ppermute only.
A program may use at most 64 MiB of HBM per device.

```python
import math
import jax
import jax.numpy as jnp
from jax import lax

S = 1024
OBS = 4096
BLK = 64
NB = 256
K = 4
HORIZON_LENGTH = 128
N_TM = 32


def draw_transition(key, part):
    key = jax.random.fold_in(key, 11)
    seed_sequence = jax.random.split(key, 6)
    rate = jnp.exp(jax.random.uniform(seed_sequence[0], (S,), jnp.float32, jnp.log(0.004), jnp.log(0.06)))
    off = jnp.clip(jax.random.normal(seed_sequence[5], (HORIZON_LENGTH, S, S), jnp.float32), -5.0, 5.0)
    diagonal_nudge = jnp.exp(jax.random.uniform(seed_sequence[1], (HORIZON_LENGTH, S), jnp.float32, jnp.log(0.5), jnp.log(2.0)))
    keep = jnp.exp(-rate[None, :] * diagonal_nudge)
    spike_instant = jax.random.randint(seed_sequence[2], (4,), 0, HORIZON_LENGTH)
    agreement_indicator = jnp.any(jnp.arange(HORIZON_LENGTH)[:, None] == spike_instant[None, :], axis=1)
    loss = jax.random.uniform(seed_sequence[3], (HORIZON_LENGTH, S), jnp.float32, 0.5, 0.8)
    keep = jnp.where(agreement_indicator[:, None], keep * loss, keep)
    eye = jnp.eye(S, dtype=jnp.float32)
    mats = off * (0.15 / jnp.sqrt(S * 1.0)) * (1.0 - eye)[None] + eye[None] * keep[:, :, None]
    return mats.astype(jnp.bfloat16)


def set_ends(drawn, key, least, largest):
    place = [jax.random.randint(jax.random.fold_in(key, axis), (), 0, length) for axis, length in enumerate(drawn.shape)]
    main_axis = drawn.shape.index(max(drawn.shape))
    neighbour = place[:main_axis] + [(place[main_axis] + 1) % drawn.shape[main_axis]] + place[main_axis + 1:]
    return drawn.at[tuple(place)].set(least).at[tuple(neighbour)].set(largest)


def block_levels(stream_key, shape, cuts, smallest, largest):
    def one(axis_at, blocks):
        heights = jax.random.uniform(jax.random.fold_in(jax.random.fold_in(stream_key, 6), axis_at), (blocks,), jnp.float32, smallest / len(cuts), largest / len(cuts))
        return jnp.repeat(jnp.exp(heights), shape[axis_at] // blocks).reshape((-1,) + (1,) * (len(shape) - axis_at - 1))

    loudness = one(*cuts[0])
    for cut in cuts[1:]:
        loudness = loudness * one(*cut)
    return loudness


def scatter_about(stream_key, extent, width, bound, cuts=(), held_as=jnp.bfloat16):
    drawn = jax.random.normal(stream_key, extent, jnp.float32) * width
    if len(cuts) > 0:
        drawn = block_levels(stream_key, extent, cuts, -0.22, 0.18) * drawn
    return jnp.clip(drawn, min=-bound, max=bound).astype(held_as)


def setup_inputs(seed: int = 0) -> dict:
    arg_keys = jax.random.split(jax.random.key(seed), 8)
    return {
        "observations": scatter_about(arg_keys[0], (HORIZON_LENGTH, OBS), 1.0, 6.0, ((0, 32),), jnp.float32),
        "precisions": jnp.clip(jnp.exp(math.log(4.0) - 2.7725887 * jax.random.uniform(arg_keys[1], (HORIZON_LENGTH, OBS), jnp.float32) ** block_levels(arg_keys[1], (HORIZON_LENGTH, OBS), ((0, 32),), -0.2, 0.2)), 0.25, 4.0),
        "blocks": scatter_about(arg_keys[2], (HORIZON_LENGTH, NB, BLK, BLK), (4 * NB * BLK * BLK // S) ** -0.5, 0.09375, ((0, 32), (1, 8))),
        "block_rows": set_ends(jax.random.randint(arg_keys[3], (HORIZON_LENGTH, NB), 0, OBS // BLK), jax.random.fold_in(arg_keys[3], 1), 0, (OBS // BLK) - 1).astype(jnp.int32),
        "block_cols": set_ends(jax.random.randint(arg_keys[4], (HORIZON_LENGTH, NB), 0, S // BLK), jax.random.fold_in(arg_keys[4], 1), 0, (S // BLK) - 1).astype(jnp.int32),
        "transition": draw_transition(jax.random.fold_in(arg_keys[7], 71), 0),
        "prior": scatter_about(arg_keys[6], (S,), 2.0, 8.0, (), jnp.float32),
    }


def assemble(weighted_step, blocks_step, lines_per_interval, cols_step):
    pieces = weighted_step.reshape(OBS // BLK, BLK)
    selected_entry = pieces[lines_per_interval].astype(jnp.float32)
    terms = jnp.einsum("bi,bij->bj", selected_entry, blocks_step.astype(jnp.float32))
    onehot = (cols_step[:, None] == jnp.arange(S // BLK, dtype=jnp.int32)[None, :]).astype(jnp.float32)
    return jnp.einsum("bc,bj->cj", onehot, terms).reshape(S)


def block_products(args):
    mats, drives = args
    prod = mats[0]
    local = drives[0].astype(jnp.bfloat16)
    prods = [prod]
    locals_list = [local]
    for j in range(1, K):
        prod = jnp.dot(mats[j], prod, preferred_element_type=jnp.float32).astype(jnp.bfloat16)
        local = (jnp.dot(mats[j], local, preferred_element_type=jnp.float32) + drives[j]).astype(jnp.bfloat16)
        prods.append(prod)
        locals_list.append(local)
    return jnp.stack(prods), jnp.stack(locals_list)


def reference(observations, precisions, blocks, block_rows, block_cols, transition, prior):
    weighted = (precisions * observations).astype(jnp.bfloat16)
    drive = lax.map(lambda a: assemble(*a), (weighted, blocks, block_rows, block_cols))
    mats = transition.reshape(N_TM, K, S, S)
    drives = drive.reshape(N_TM, K, S)
    prods, locals_all = lax.map(block_products, (mats, drives))

    def advance(start, item):
        last_prod, last_local = item
        nxt = jnp.dot(last_prod.astype(jnp.float32), start, precision=lax.Precision.HIGHEST) + last_local.astype(jnp.float32)
        return nxt, start

    first = prior.astype(jnp.float32)
    _, starts = lax.scan(advance, first, (prods[:, K - 1], locals_all[:, K - 1]))

    def apply_block(item):
        block_prods, block_locals, start = item
        out = jnp.einsum("kij,j->ki", block_prods.astype(jnp.float32), start, precision=lax.Precision.HIGHEST)
        return out + block_locals.astype(jnp.float32)

    filtered = lax.map(apply_block, (prods, locals_all, starts))
    return filtered.reshape(HORIZON_LENGTH, S)
```

```python
import functools

import jax
import jax.numpy as jnp
from jax import lax
from jax.experimental import pallas as pl
from jax.experimental.pallas import tpu as pltpu
from jax.sharding import PartitionSpec as P

F32 = jnp.float32
BF16 = jnp.bfloat16
VMEM_LIMIT = 40 * 1024 * 1024
ROWS = 256


def split_rows(x):
    hi = x.astype(BF16).astype(F32)
    rest = x - hi
    mid = rest.astype(BF16).astype(F32)
    lo = rest - mid
    row = lax.broadcasted_iota(jnp.int32, (16, x.shape[1]), 0)
    zero = jnp.zeros((16, x.shape[1]), F32)
    out = jnp.where(row == 0, hi, jnp.where(row == 1, mid, jnp.where(row == 2, lo, zero)))
    return out.astype(BF16)


def joined(rows):
    return jnp.sum(rows.astype(F32), axis=0, keepdims=True)


def times_t(x, matrix):
    out = lax.dot_general(split_rows(x), matrix, (((1,), (1,)), ((), ())), preferred_element_type=F32)
    return joined(out)


def times(x, matrix):
    return joined(jnp.dot(split_rows(x), matrix, preferred_element_type=F32))


def matmul_into(left, right, store, size):
    def block(i, carry):
        at = pl.multiple_of(i * ROWS, ROWS)
        out = jnp.dot(left(pl.ds(at, ROWS)), right(), preferred_element_type=F32)
        store(pl.ds(at, ROWS), out.astype(BF16))
        return carry

    lax.fori_loop(0, size // ROWS, block, 0)


def products_kernel(count, place_ref, drive_ref, *refs):
    pieces = refs[: 2 * count]
    sum_ref, slabs_ref, locals_ref, t_ref, m_ref, n_ref, sems = refs[2 * count:]
    size = t_ref.shape[1]
    width = size // count
    place = place_ref[0]
    copies = []
    for half in range(2):
        for r in range(count):
            at = pl.multiple_of(lax.rem(place + r, count) * width, width)
            copy = pltpu.make_async_copy(
                pieces[half * count + r],
                t_ref.at[pl.ds(2 * half, 2), pl.ds(at, width), :],
                sems.at[half * count + r],
            )
            copy.start()
            copies.append(copy)
    for copy in copies[:count]:
        copy.wait()
    mine = pl.ds(pl.multiple_of(place * width, width), width)
    slabs_ref[0] = t_ref[0, mine, :]

    def put(ref):
        def store(rows, value):
            ref[rows, :] = value

        return store

    matmul_into(lambda rows: t_ref[1, rows, :], lambda: t_ref[0], put(m_ref), size)
    slabs_ref[1] = m_ref[mine, :]
    for copy in copies[count:]:
        copy.wait()
    matmul_into(lambda rows: t_ref[2, rows, :], lambda: m_ref[...], put(n_ref), size)
    slabs_ref[2] = n_ref[mine, :]
    matmul_into(lambda rows: t_ref[3, rows, :], lambda: n_ref[...], put(sum_ref), size)
    slabs_ref[3] = sum_ref[mine, :]
    local = drive_ref[0:1, :]
    locals_ref[0:1, :] = local
    for j in range(1, 4):
        local = times_t(local, t_ref[j]) + drive_ref[j:j + 1, :]
        locals_ref[j:j + 1, :] = local
    sum_ref[size:, :] = split_rows(local)


def pair_kernel(core_ref, own_ref, other_ref, qt_ref, q_ref, first_ref, second_ref):
    size = qt_ref.shape[0]

    @pl.when(core_ref[0] == 0)
    def _():
        first_ref[...] = own_ref[...]
        second_ref[...] = other_ref[...]

    @pl.when(core_ref[0] != 0)
    def _():
        first_ref[...] = other_ref[...]
        second_ref[...] = own_ref[...]

    def block(i, carry):
        at = pl.multiple_of(i * ROWS, ROWS)
        out = jnp.dot(second_ref[pl.ds(at, ROWS), :], first_ref[:size, :], preferred_element_type=F32)
        qt_ref[:, pl.ds(at, ROWS)] = out.T.astype(BF16)
        return carry

    lax.fori_loop(0, size // ROWS, block, 0)
    q_ref[...] = times_t(joined(first_ref[size:, :]), second_ref[:size, :]) + joined(second_ref[size:, :])


def hop_kernel(turn, chip_ref, begin_ref, came_ref, qt_ref, q_ref, held_ref, value_ref):
    here = chip_ref[0] == turn

    @pl.when(here)
    def _():
        begin = came_ref[...] if turn > 0 else begin_ref[...]
        held_ref[...] = begin
        value_ref[...] = times(begin, qt_ref[...]) + q_ref[...]

    @pl.when(jnp.logical_not(here))
    def _():
        held_ref[...] = begin_ref[...]
        value_ref[...] = begin_ref[...]


def out_kernel(core_ref, begin_ref, other_ref, slabs_ref, locals_ref, out_ref):
    steps, width, size = slabs_ref.shape

    def write(begin):
        flat = slabs_ref[...].reshape(steps * width, size)
        row = times_t(begin, flat)
        for j in range(steps):
            out_ref[j:j + 1, :] = row[:, j * width:(j + 1) * width] + locals_ref[j:j + 1, :]

    @pl.when(core_ref[0] == 0)
    def _():
        write(begin_ref[...])

    @pl.when(core_ref[0] != 0)
    def _():
        write(times_t(begin_ref[...], other_ref[:size, :]) + joined(other_ref[size:, :]))


def call(kernel, out_shape, spaces, scratch=(), flops=0, moved=0):
    return pl.pallas_call(
        kernel,
        out_shape=out_shape,
        in_specs=[pl.BlockSpec(memory_space=s) for s in spaces],
        out_specs=jax.tree.map(lambda _: pl.BlockSpec(memory_space=pltpu.VMEM), out_shape),
        scratch_shapes=list(scratch),
        compiler_params=pltpu.CompilerParams(vmem_limit_bytes=VMEM_LIMIT),
        cost_estimate=pl.CostEstimate(flops=flops, bytes_accessed=moved, transcendentals=0),
    )


def gathered(part, axis, last_forward):
    count = lax.axis_size(axis)
    forward = [(i, (i + 1) % count) for i in range(count)]
    backward = [((i + 1) % count, i) for i in range(count)]
    pieces = {0: part}
    for r in range(1, count // 2):
        pieces[count - r] = lax.ppermute(pieces[(count - r + 1) % count], axis, forward)
        pieces[r] = lax.ppermute(pieces[r - 1], axis, backward)
    half = count // 2
    if last_forward:
        pieces[half] = lax.ppermute(pieces[half + 1], axis, forward)
    else:
        pieces[half] = lax.ppermute(pieces[half - 1], axis, backward)
    return [pieces[r] for r in range(count)]


def partial_drive_of(observations, precisions, blocks, block_rows, block_cols, width):
    steps_here = blocks.shape[0]
    side = blocks.shape[2]
    weighted = (precisions * observations).astype(BF16)
    pieces = weighted.reshape(steps_here, weighted.shape[1] // side, side)
    selected_entry = jnp.take_along_axis(pieces, block_rows[:, :, None], axis=1)
    terms = jnp.einsum("tbi,tbij->tbj", selected_entry, blocks, preferred_element_type=F32)
    onehot = (
        block_cols[:, :, None] == jnp.arange(width // side, dtype=jnp.int32)[None, None, :]
    ).astype(F32)
    return jnp.einsum("tbc,tbj->tcj", onehot, terms, precision=lax.Precision.HIGHEST).reshape(steps_here, width)


def shards(observations, precisions, blocks, block_rows, block_cols, transition, prior):
    steps_here, width, size = transition.shape
    count = lax.axis_size("state")
    place = lax.axis_index("state")
    position = lax.axis_index("tm")
    blocks_of_time = lax.axis_size("tm")
    core = (position % 2).astype(jnp.int32).reshape(1)
    chip = (position // 2).astype(jnp.int32).reshape(1)
    V, S, A = pltpu.VMEM, pltpu.SMEM, pl.ANY

    drive = partial_drive_of(observations, precisions, blocks, block_rows, block_cols, size)
    for bit in (1, 2, 4):
        drive = drive + lax.ppermute(drive, "state", [(i, i ^ bit) for i in range(count)])

    first = gathered(transition[:2], "state", True)
    second = gathered(transition[2:], "state", False)

    summed, slabs, locals_ = call(
        functools.partial(products_kernel, count),
        (
            jax.ShapeDtypeStruct((size + 16, size), BF16),
            jax.ShapeDtypeStruct((steps_here, width, size), BF16),
            jax.ShapeDtypeStruct((steps_here, size), F32),
        ),
        [S, V] + [A] * (2 * count),
        [
            pltpu.VMEM((steps_here, size, size), BF16),
            pltpu.VMEM((size, size), BF16),
            pltpu.VMEM((size, size), BF16),
            pltpu.SemaphoreType.DMA((2 * count,)),
        ],
        flops=6 * size ** 3,
        moved=12 * size ** 2,
    )(place.astype(jnp.int32).reshape(1), drive, *first, *second)

    swap = [(i, i ^ 1) for i in range(blocks_of_time)]
    other = lax.ppermute(summed, "tm", swap)
    turned, term = call(
        pair_kernel,
        (jax.ShapeDtypeStruct((size, size), BF16), jax.ShapeDtypeStruct((1, size), F32)),
        [S, V, V],
        [pltpu.VMEM((size + 16, size), BF16)] * 2,
        flops=2 * size ** 3,
        moved=6 * size ** 2,
    )(core, summed, other)

    begin = prior.reshape(1, size)
    came = begin
    chips = blocks_of_time // 2
    for turn in range(chips):
        begin, value = call(
            functools.partial(hop_kernel, turn),
            (jax.ShapeDtypeStruct((1, size), F32),) * 2,
            [S, V, V, V, V],
            flops=32 * size ** 2,
            moved=2 * size ** 2,
        )(chip, begin, came, turned, term)
        if turn + 1 < chips:
            came = lax.ppermute(value, "tm", [(2 * turn + c, 2 * turn + 2 + c) for c in (0, 1)])

    mine = lax.dynamic_slice_in_dim(locals_, place * width, width, axis=1)
    return call(
        out_kernel,
        jax.ShapeDtypeStruct((steps_here, width), F32),
        [S, V, V, V, V],
        flops=32 * size ** 2,
        moved=4 * size ** 2,
    )(core, begin, other, slabs, mine)


def solution(mesh):
    return jax.shard_map(
        shards,
        mesh=mesh,
        in_specs=(
            P("tm", None),
            P("tm", None),
            P("tm", "state", None, None),
            P("tm", "state"),
            P("tm", "state"),
            P("tm", "state", None),
            P(),
        ),
        out_specs=P("tm", "state"),
        check_vma=False,
    )
```

```python
import functools

import jax
import jax.numpy as jnp
from jax import lax
from jax.experimental import pallas as pl
from jax.experimental.pallas import tpu as pltpu
from jax.sharding import PartitionSpec as P

F32 = jnp.float32
BF16 = jnp.bfloat16
VMEM_LIMIT = 24 * 1024 * 1024
COLUMNS = 256
LANES = 128


def three_parts(x):
    hi = x.astype(BF16).astype(F32)
    rest = x - hi
    mid = rest.astype(BF16).astype(F32)
    return hi, mid, rest - mid


def split_rows(x):
    hi, mid, lo = three_parts(x)
    row = lax.broadcasted_iota(jnp.int32, (16, x.shape[1]), 0)
    out = jnp.where(row == 0, hi, jnp.where(row == 1, mid, jnp.where(row == 2, lo, 0.0)))
    return out.astype(BF16)


def split_columns(x):
    hi, mid, lo = three_parts(x)
    column = lax.broadcasted_iota(jnp.int32, (x.shape[0], LANES), 1)
    out = jnp.where(column == 0, hi, jnp.where(column == 1, mid, jnp.where(column == 2, lo, 0.0)))
    return out.astype(BF16)


def joined(rows):
    return jnp.sum(rows.astype(F32), axis=0, keepdims=True)


def times_t(x, matrix):
    out = lax.dot_general(split_rows(x), matrix, (((1,), (1,)), ((), ())), preferred_element_type=F32)
    return joined(out)


def times(x, matrix):
    return joined(jnp.dot(split_rows(x), matrix, preferred_element_type=F32))


def times_column(matrix, x):
    out = jnp.dot(matrix, split_columns(x), preferred_element_type=F32)
    return jnp.sum(out, axis=1, keepdims=True)


def matmul(left_ref, right_ref, out_ref):
    size = left_ref.shape[0]

    def block(i, carry):
        at = pl.ds(pl.multiple_of(i * COLUMNS, COLUMNS), COLUMNS)
        out = jnp.dot(left_ref[...], right_ref[:, at], preferred_element_type=F32)
        out_ref[:size, at] = out.astype(BF16)
        return carry

    lax.fori_loop(0, right_ref.shape[1] // COLUMNS, block, 0)


def fetched(count, place, pieces, j, whole_ref, sems, first):
    width = pieces[0].shape[1]
    copies = []
    for r in range(count):
        at = pl.multiple_of(lax.rem(place + r, count) * width, width)
        copy = pltpu.make_async_copy(pieces[r].at[j], whole_ref.at[pl.ds(at, width), :], sems.at[first + r])
        copy.start()
        copies.append(copy)
    return copies


def two_kernel(count, place_ref, drive_ref, *refs):
    pieces, (two_ref, slab_ref, local_ref, one_ref, next_ref, sems) = refs[:count], refs[count:]
    width = slab_ref.shape[0]
    place = place_ref[0]
    copies = fetched(count, place, pieces, 0, one_ref, sems, 0)
    copies += fetched(count, place, pieces, 1, next_ref, sems, count)
    for copy in copies:
        copy.wait()
    matmul(next_ref, one_ref, two_ref)
    slab_ref[...] = two_ref[pl.ds(pl.multiple_of(place * width, width), width), :]
    local_ref[...] = times_column(next_ref[...], drive_ref[:, 0:1]) + drive_ref[:, 1:2]


def four_kernel(count, place_ref, drive_ref, local_ref, two_ref, *refs):
    pieces = refs[:count]
    sum_ref, slab3_ref, slab4_ref, locals_ref, three_ref, third_ref, fourth_ref, sems = refs[count:]
    width, size = slab3_ref.shape
    place = place_ref[0]
    thirds = fetched(count, place, pieces, 0, third_ref, sems, 0)
    fourths = fetched(count, place, pieces, 1, fourth_ref, sems, count)
    mine = pl.ds(pl.multiple_of(place * width, width), width)
    for copy in thirds:
        copy.wait()
    matmul(third_ref, two_ref, three_ref)
    slab3_ref[...] = three_ref[mine, :]
    local2 = local_ref[...]
    local3 = times_column(third_ref[...], local2) + drive_ref[:, 2:3]
    for copy in fourths:
        copy.wait()
    matmul(fourth_ref, three_ref, sum_ref)
    slab4_ref[...] = sum_ref[mine, :]
    local4 = times_column(fourth_ref[...], local3) + drive_ref[:, 3:4]
    column = lax.broadcasted_iota(jnp.int32, (size, LANES), 1)
    first = jnp.broadcast_to(drive_ref[:, 0:1], (size, LANES))
    side = jnp.where(column == 0, first, jnp.where(column == 1, local2, jnp.where(column == 2, local3, local4)))
    rows = side.T
    locals_ref[...] = rows[:8, :]
    sum_ref[size:, :] = split_rows(rows[3:4, :])


def both(core_ref, own_ref, other_ref, write):
    @pl.when(core_ref[0] == 0)
    def _():
        write(own_ref, other_ref)

    @pl.when(core_ref[0] != 0)
    def _():
        write(other_ref, own_ref)


def pair_kernel(core_ref, own_ref, other_ref, after_ref, qt_ref, q_ref):
    size = qt_ref.shape[0]

    @pl.when(core_ref[0] != 0)
    def _():
        def block(i, carry):
            at = pl.ds(pl.multiple_of(i * COLUMNS, COLUMNS), COLUMNS)
            out = jnp.dot(own_ref[at, :], other_ref[:size, :], preferred_element_type=F32)
            qt_ref[:, at] = out.T.astype(BF16)
            return carry

        lax.fori_loop(0, size // COLUMNS, block, 0)
        q_ref[...] = times_t(joined(other_ref[size:, :]), own_ref[:size, :]) + joined(own_ref[size:, :])


def early_hop_kernel(turn, core_ref, chip_ref, begin_ref, came_ref, own_ref, other_ref, held_ref, value_ref):
    size = begin_ref.shape[1]
    held_ref[...] = begin_ref[...]
    value_ref[...] = begin_ref[...]

    @pl.when(jnp.logical_and(chip_ref[0] == turn, core_ref[0] != 0))
    def _():
        begin = came_ref[...] if turn > 0 else begin_ref[...]
        held_ref[...] = begin
        between = times_t(begin, other_ref[:size, :]) + joined(other_ref[size:, :])
        value_ref[...] = times_t(between, own_ref[:size, :]) + joined(own_ref[size:, :])


def hop_kernel(turn, core_ref, chip_ref, begin_ref, came_ref, qt_ref, q_ref, held_ref, value_ref):
    here = jnp.logical_and(chip_ref[0] == turn, core_ref[0] != 0)

    @pl.when(here)
    def _():
        begin = came_ref[...]
        held_ref[...] = begin
        value_ref[...] = times(begin, qt_ref[...]) + q_ref[...]

    @pl.when(jnp.logical_not(here))
    def _():
        held_ref[...] = begin_ref[...]
        value_ref[...] = begin_ref[...]


def ready_kernel(core_ref, place_ref, other_ref, locals_ref, after_ref, *refs):
    slabs, (maps_ref, terms_ref) = refs[:-2], refs[-2:]
    width, size = slabs[0].shape
    mine = pl.ds(pl.multiple_of(place_ref[0] * width, width), width)
    for j, slab_ref in enumerate(slabs):
        at = slice(j * width, (j + 1) * width)

        @pl.when(core_ref[0] == 0)
        def _():
            maps_ref[:, at] = slab_ref[...].astype(F32).T.astype(BF16)
            terms_ref[j:j + 1, :] = locals_ref[j:j + 1, mine]

        @pl.when(core_ref[0] != 0)
        def _():
            out = jnp.dot(slab_ref[...], other_ref[:size, :], preferred_element_type=F32)
            maps_ref[:, at] = out.T.astype(BF16)
            term = times_t(joined(other_ref[size:, :]), slab_ref[...])
            terms_ref[j:j + 1, :] = term + locals_ref[j:j + 1, mine]


def out_kernel(core_ref, begin_ref, got_ref, maps_ref, terms_ref, out_ref):
    steps, width = out_ref.shape
    begin = jnp.where(core_ref[0] == 0, got_ref[...], begin_ref[...])
    row = times(begin, maps_ref[...])
    for j in range(steps):
        out_ref[j:j + 1, :] = row[:, j * width:(j + 1) * width] + terms_ref[j:j + 1, :]


def call(kernel, out_shape, spaces, scratch=(), flops=0, moved=0):
    return pl.pallas_call(
        kernel,
        out_shape=out_shape,
        in_specs=[pl.BlockSpec(memory_space=s) for s in spaces],
        out_specs=jax.tree.map(lambda _: pl.BlockSpec(memory_space=pltpu.VMEM), out_shape),
        scratch_shapes=list(scratch),
        compiler_params=pltpu.CompilerParams(vmem_limit_bytes=VMEM_LIMIT),
        cost_estimate=pl.CostEstimate(flops=flops, bytes_accessed=moved, transcendentals=0),
    )


def after(value, *needed):
    return lax.optimization_barrier((value, needed))[0]


def ring_rounds(parts, axis, needed):
    count = lax.axis_size(axis)
    forward = [(i, (i + 1) % count) for i in range(count)]
    backward = [((i + 1) % count, i) for i in range(count)]
    half = count // 2
    found = [{0: part} for part in parts]
    for r in range(1, half + 1):
        for i, pieces in enumerate(found):
            left, right = pieces[(count - r + 1) % count], pieces[r - 1]
            more = needed(r, i, found)
            if more:
                left, right = after((left, right), *more)
            if r < half or i % 2 == 0:
                pieces[count - r] = lax.ppermute(left, axis, forward)
            if r < half or i % 2 == 1:
                pieces[r] = lax.ppermute(right, axis, backward)
    return [[pieces[r] for r in range(count)] for pieces in found]


def partial_drive_of(observations, precisions, blocks, block_rows, block_cols, width):
    steps_here = blocks.shape[0]
    side = blocks.shape[2]
    weighted = (precisions * observations).astype(BF16)
    pieces = weighted.reshape(steps_here, weighted.shape[1] // side, side)
    selected_entry = jnp.take_along_axis(pieces, block_rows[:, :, None], axis=1)
    terms = jnp.einsum("tbi,tbij->tbj", selected_entry, blocks, preferred_element_type=F32)
    onehot = (
        block_cols[:, :, None] == jnp.arange(width // side, dtype=jnp.int32)[None, None, :]
    ).astype(F32)
    return jnp.einsum("tbc,tbj->tcj", onehot, terms, precision=lax.Precision.HIGHEST).reshape(steps_here, width)


def shards(observations, precisions, blocks, block_rows, block_cols, transition, prior):
    steps_here, width, size = transition.shape
    count = lax.axis_size("state")
    place = lax.axis_index("state")
    position = lax.axis_index("tm")
    blocks_of_time = lax.axis_size("tm")
    core = (position % 2).astype(jnp.int32).reshape(1)
    chip = (position // 2).astype(jnp.int32).reshape(1)
    at = place.astype(jnp.int32).reshape(1)
    V, S, H = pltpu.VMEM, pltpu.SMEM, pltpu.HBM

    def added(drive, bit):
        return drive + lax.ppermute(drive, "state", [(i, i ^ bit) for i in range(count)])

    drive = partial_drive_of(observations, precisions, blocks, block_rows, block_cols, size)
    drive1 = added(drive, 1)
    drive2 = added(drive1, 2)
    drive4 = added(drive2, 4)
    needs = {(2, 0): drive, (3, 0): drive1, (4, 0): drive2}

    def needed(r, i, found):
        return (needs[r, i],) if (r, i) in needs else ()

    early, late = ring_rounds([transition[:2], transition[2:]], "state", needed)
    columns = jnp.pad(drive4.T, ((0, 0), (0, LANES - steps_here)))

    matrix = jax.ShapeDtypeStruct((size, size), BF16)
    longer = jax.ShapeDtypeStruct((size + 16, size), BF16)
    slab = jax.ShapeDtypeStruct((width, size), BF16)
    column = jax.ShapeDtypeStruct((size, 1), F32)
    row = jax.ShapeDtypeStruct((1, size), F32)
    whole = pltpu.VMEM((size, size), BF16)
    semaphores = pltpu.SemaphoreType.DMA((2 * count,))
    two, slab2, local2 = call(
        functools.partial(two_kernel, count), (matrix, slab, column), [S, V] + [H] * count,
        [whole, whole, semaphores], flops=2 * size ** 3, moved=6 * size ** 2,
    )(at, columns, *early)
    own, slab3, slab4, locals_ = call(
        functools.partial(four_kernel, count),
        (longer, slab, slab, jax.ShapeDtypeStruct((8, size), F32)),
        [S, V, V, V] + [H] * count,
        [whole, whole, whole, semaphores], flops=4 * size ** 3, moved=8 * size ** 2,
    )(at, columns, local2, two, *late)

    other = lax.ppermute(own, "tm", [(i, i + 1) for i in range(0, blocks_of_time, 2)])

    def hop(value, turn):
        return lax.ppermute(value, "tm", [(2 * turn + 1, 2 * turn + 3)])

    begin = prior.reshape(1, size)
    came = begin
    chips = blocks_of_time // 2
    for turn in range(2):
        begin, value = call(
            functools.partial(early_hop_kernel, turn), (row, row), [S, S] + [V] * 4,
            flops=64 * size ** 2, moved=4 * size ** 2,
        )(core, chip, begin, came, own, other)
        came = hop(value, turn)
    turned, term = call(
        pair_kernel, (matrix, row), [S, V, V, V], flops=2 * size ** 3, moved=6 * size ** 2
    )(core, own, other, value)
    for turn in range(2, chips):
        begin, value = call(
            functools.partial(hop_kernel, turn), (row, row), [S, S, V, V, V, V],
            flops=32 * size ** 2, moved=2 * size ** 2,
        )(core, chip, begin, came, turned, term)
        if turn == 2:
            maps, terms = call(
                ready_kernel,
                (jax.ShapeDtypeStruct((size, steps_here * width), BF16), jax.ShapeDtypeStruct((steps_here, width), F32)),
                [S, S] + [V] * 7, flops=size ** 3, moved=4 * size ** 2,
            )(core, at, other, locals_, value, transition[0], slab2, slab3, slab4)
        if turn + 1 < chips:
            came = hop(value, turn)
    got = lax.ppermute(begin, "tm", [(i + 1, i) for i in range(0, blocks_of_time, 2)])
    return call(
        out_kernel, jax.ShapeDtypeStruct((steps_here, width), F32), [S, V, V, V, V],
        flops=16 * size ** 2, moved=size ** 2,
    )(core, begin, got, maps, terms)


def solution(mesh):
    return jax.shard_map(
        shards,
        mesh=mesh,
        in_specs=(
            P("tm", None),
            P("tm", None),
            P("tm", "state", None, None),
            P("tm", "state"),
            P("tm", "state"),
            P("tm", "state", None),
            P(),
        ),
        out_specs=P("tm", "state"),
        check_vma=False,
    )
```

```python
import functools

import jax
import jax.numpy as jnp
from jax import lax
from jax.experimental import pallas as pl
from jax.experimental.pallas import tpu as pltpu
from jax.sharding import PartitionSpec as P

F32 = jnp.float32
BF16 = jnp.bfloat16
VMEM_LIMIT = 24 * 1024 * 1024
ROWS = 512


def three_parts(x):
    hi = x.astype(BF16).astype(F32)
    rest = x - hi
    mid = rest.astype(BF16).astype(F32)
    return hi, mid, rest - mid


def split_rows(x):
    hi, mid, lo = three_parts(x)
    row = lax.broadcasted_iota(jnp.int32, (16, x.shape[1]), 0)
    out = jnp.where(row == 0, hi, jnp.where(row == 1, mid, jnp.where(row == 2, lo, 0.0)))
    return out.astype(BF16)


def joined(rows):
    return jnp.sum(rows.astype(F32), axis=0, keepdims=True)


def times_t(x, matrix):
    out = lax.dot_general(split_rows(x), matrix, (((1,), (1,)), ((), ())), preferred_element_type=F32)
    return joined(out)


def times(x, matrix):
    return joined(jnp.dot(split_rows(x), matrix, preferred_element_type=F32))


def matmul(left_ref, right_ref, out_ref):
    def block(i, carry):
        at = pl.ds(pl.multiple_of(i * ROWS, ROWS), ROWS)
        out_ref[at, :] = jnp.dot(left_ref[at, :], right_ref[...], preferred_element_type=F32).astype(BF16)
        return carry

    lax.fori_loop(0, left_ref.shape[0] // ROWS, block, 0)


def core_here():
    return lax.rem(lax.axis_index("tm"), 2)


def chip_here():
    return lax.div(lax.axis_index("tm"), 2)


def drive_kernel(rows_ref, cols_ref, observations_ref, precisions_ref, blocks_ref, drive_ref, weighted_ref):
    steps, count, side, _ = blocks_ref.shape
    weighted_ref[...] = (precisions_ref[...] * observations_ref[...]).astype(BF16).astype(F32)
    drive_ref[...] = jnp.zeros_like(drive_ref)
    for t in range(steps):
        def block(b, carry):
            left = jnp.broadcast_to(weighted_ref[t, pl.ds(rows_ref[t, b], 1), :], (16, side)).astype(BF16)
            term = jnp.dot(left, blocks_ref[t, b], preferred_element_type=F32)
            at = pl.ds(cols_ref[t, b], 1)
            drive_ref[t, at, :] = drive_ref[t, at, :] + term[0:1, :]
            return carry

        lax.fori_loop(0, count, block, 0, unroll=4)


def add_kernel(one_ref, other_ref, out_ref):
    out_ref[...] = one_ref[...] + other_ref[...]


def row_of(drive_ref, j, row_ref):
    side = drive_ref.shape[2]
    for c in range(drive_ref.shape[1]):
        row_ref[0:1, c * side:(c + 1) * side] = drive_ref[j, c:c + 1, :]
    return row_ref[0:1, :]


def fetched(count, place, pieces, j, whole_ref, sems, first):
    width = pieces[0].shape[1]
    copies = []
    for r in range(count):
        at = pl.multiple_of(lax.rem(place + r, count) * width, width)
        copy = pltpu.make_async_copy(pieces[r].at[j], whole_ref.at[pl.ds(at, width), :], sems.at[first + r])
        copy.start()
        copies.append(copy)
    return copies


def two_kernel(count, drive_ref, *refs):
    pieces = refs[:count]
    two_ref, slab_ref, locals_ref, one_ref, next_ref, row_ref, sems = refs[count:]
    width = slab_ref.shape[0]
    place = lax.axis_index("state")
    ones = fetched(count, place, pieces, 0, one_ref, sems, 0)
    nexts = fetched(count, place, pieces, 1, next_ref, sems, count)
    for copy in ones + nexts:
        copy.wait()
    matmul(next_ref, one_ref, two_ref)
    slab_ref[...] = two_ref[pl.ds(pl.multiple_of(place * width, width), width), :]
    first = row_of(drive_ref, 0, row_ref)
    locals_ref[0:1, :] = first
    locals_ref[1:2, :] = times_t(first, next_ref[...]) + row_of(drive_ref, 1, row_ref)


def four_kernel(count, two_ref, *refs):
    pieces = refs[:count]
    four_ref, slab3_ref, slab4_ref, third_ref, fourth_ref, three_ref, sems = refs[count:]
    width = slab3_ref.shape[0]
    place = lax.axis_index("state")
    thirds = fetched(count, place, pieces, 0, third_ref, sems, 0)
    fourths = fetched(count, place, pieces, 1, fourth_ref, sems, count)
    mine = pl.ds(pl.multiple_of(place * width, width), width)
    for copy in thirds:
        copy.wait()
    matmul(third_ref, two_ref, three_ref)
    slab3_ref[...] = three_ref[mine, :]
    for copy in fourths:
        copy.wait()
    matmul(fourth_ref, three_ref, four_ref)
    slab4_ref[...] = four_ref[mine, :]


def local_kernel(drive_ref, before_ref, third_ref, fourth_ref, locals_ref, term_ref, row_ref):
    locals_ref[0:2, :] = before_ref[0:2, :]
    local = times_t(before_ref[1:2, :], third_ref[...]) + row_of(drive_ref, 2, row_ref)
    locals_ref[2:3, :] = local
    local = times_t(local, fourth_ref[...]) + row_of(drive_ref, 3, row_ref)
    locals_ref[3:4, :] = local
    term_ref[...] = split_rows(local)


def pair_kernel(own_ref, own_term_ref, other_ref, other_term_ref, after_ref, qt_ref, q_ref):
    @pl.when(core_here() != 0)
    def _():
        def block(i, carry):
            at = pl.ds(pl.multiple_of(i * ROWS, ROWS), ROWS)
            out = jnp.dot(own_ref[at, :], other_ref[...], preferred_element_type=F32)
            qt_ref[:, at] = out.T.astype(BF16)
            return carry

        lax.fori_loop(0, own_ref.shape[0] // ROWS, block, 0)
        q_ref[...] = times_t(joined(other_term_ref[...]), own_ref[...]) + joined(own_term_ref[...])


def early_hop_kernel(
    turn, begin_ref, came_ref, own_ref, own_term_ref, other_ref, other_term_ref, held_ref, value_ref
):
    held_ref[...] = begin_ref[...]
    value_ref[...] = begin_ref[...]

    @pl.when(jnp.logical_and(chip_here() == turn, core_here() != 0))
    def _():
        begin = came_ref[...] if turn > 0 else begin_ref[...]
        held_ref[...] = begin
        between = times_t(begin, other_ref[...]) + joined(other_term_ref[...])
        value_ref[...] = times_t(between, own_ref[...]) + joined(own_term_ref[...])


def hop_kernel(turn, begin_ref, came_ref, qt_ref, q_ref, held_ref, value_ref):
    here = jnp.logical_and(chip_here() == turn, core_here() != 0)

    @pl.when(here)
    def _():
        begin = came_ref[...]
        held_ref[...] = begin
        value_ref[...] = times(begin, qt_ref[...]) + q_ref[...]

    @pl.when(jnp.logical_not(here))
    def _():
        held_ref[...] = begin_ref[...]
        value_ref[...] = begin_ref[...]


def ready_kernel(other_ref, other_term_ref, locals_ref, after_ref, maps0_ref, *refs):
    slabs, (maps_ref, terms_ref) = (maps0_ref.at[0],) + refs[:-2], refs[-2:]
    width = slabs[0].shape[0]
    mine = pl.ds(pl.multiple_of(lax.axis_index("state") * width, width), width)
    for j, slab_ref in enumerate(slabs):
        at = slice(j * width, (j + 1) * width)

        @pl.when(core_here() == 0)
        def _():
            maps_ref[:, at] = slab_ref[...].astype(F32).T.astype(BF16)
            terms_ref[j:j + 1, :] = locals_ref[j:j + 1, mine]

        @pl.when(core_here() != 0)
        def _():
            out = jnp.dot(slab_ref[...], other_ref[...], preferred_element_type=F32)
            maps_ref[:, at] = out.T.astype(BF16)
            term = times_t(joined(other_term_ref[...]), slab_ref[...])
            terms_ref[j:j + 1, :] = term + locals_ref[j:j + 1, mine]


def out_kernel(begin_ref, got_ref, maps_ref, terms_ref, out_ref):
    steps, width = out_ref.shape
    begin = jnp.where(core_here() == 0, got_ref[...], begin_ref[...])
    row = times(begin, maps_ref[...])
    for j in range(steps):
        out_ref[j:j + 1, :] = row[:, j * width:(j + 1) * width] + terms_ref[j:j + 1, :]


def call(kernel, out_shape, spaces, scratch=(), flops=0, moved=0):
    return pl.pallas_call(
        kernel,
        out_shape=out_shape,
        in_specs=[pl.BlockSpec(memory_space=s) for s in spaces],
        out_specs=jax.tree.map(lambda _: pl.BlockSpec(memory_space=pltpu.VMEM), out_shape),
        scratch_shapes=list(scratch),
        compiler_params=pltpu.CompilerParams(vmem_limit_bytes=VMEM_LIMIT),
        cost_estimate=pl.CostEstimate(flops=flops, bytes_accessed=moved, transcendentals=0),
    )


def after(value, *needed):
    return lax.optimization_barrier((value, needed))[0]


def ring_rounds(parts, axis, needed):
    count = lax.axis_size(axis)
    forward = [(i, (i + 1) % count) for i in range(count)]
    backward = [((i + 1) % count, i) for i in range(count)]
    half = count // 2
    found = [{0: part} for part in parts]
    for r in range(1, half + 1):
        for i, pieces in enumerate(found):
            left, right = pieces[(count - r + 1) % count], pieces[r - 1]
            more = needed(r, i, found)
            if more:
                left, right = after((left, right), *more)
            if r < half or i % 2 == 0:
                pieces[count - r] = lax.ppermute(left, axis, forward)
            if r < half or i % 2 == 1:
                pieces[r] = lax.ppermute(right, axis, backward)
    return [[pieces[r] for r in range(count)] for pieces in found]


def shards(observations, precisions, blocks, block_rows, block_cols, transition, prior):
    steps_here, width, size = transition.shape
    side = blocks.shape[2]
    count = lax.axis_size("state")
    blocks_of_time = lax.axis_size("tm")
    V, S, A = pltpu.VMEM, pltpu.SMEM, pl.ANY

    matrix = jax.ShapeDtypeStruct((size, size), BF16)
    slab = jax.ShapeDtypeStruct((width, size), BF16)
    rows = jax.ShapeDtypeStruct((16, size), BF16)
    steps = jax.ShapeDtypeStruct((steps_here, size), F32)
    row = jax.ShapeDtypeStruct((1, size), F32)
    whole = pltpu.VMEM((size, size), BF16)
    single = pltpu.VMEM((1, size), F32)
    semaphores = pltpu.SemaphoreType.DMA((2 * count,))

    pieces = (steps_here, observations.shape[1] // side, side)
    parts = jax.ShapeDtypeStruct((steps_here, size // side, side), F32)
    drive = call(
        drive_kernel, parts, [S, S, V, V, V], [pltpu.VMEM(pieces, F32)], flops=10 ** 7, moved=2 ** 21
    )(block_rows, block_cols, observations.reshape(pieces), precisions.reshape(pieces), blocks)

    def added(drive, bit):
        came = lax.ppermute(drive, "state", [(i, i ^ bit) for i in range(count)])
        return call(add_kernel, parts, [V, V], flops=4096, moved=2 ** 16)(drive, came)

    drive1 = added(drive, 1)
    drive2 = added(drive1, 2)
    drive4 = added(drive2, 4)
    needs = {(2, 0): drive, (3, 0): drive1, (4, 0): drive2}

    def needed(r, i, found):
        return (needs[r, i],) if (r, i) in needs else ()

    early, late = ring_rounds([transition[:2], transition[2:]], "state", needed)
    two, slab2, before = call(
        functools.partial(two_kernel, count), (matrix, slab, steps), [V] + [A] * count,
        [whole, whole, single, semaphores], flops=2 * size ** 3, moved=6 * size ** 2,
    )(drive4, *early)
    own, slab3, slab4, third, fourth = call(
        functools.partial(four_kernel, count), (matrix, slab, slab, matrix, matrix), [V] + [A] * count,
        [whole, semaphores], flops=4 * size ** 3, moved=8 * size ** 2,
    )(two, *late)

    swap = [(i, i + 1) for i in range(0, blocks_of_time, 2)]
    other = lax.ppermute(own, "tm", swap)
    locals_, own_term = call(
        local_kernel, (steps, rows), [V] * 4, [single], flops=64 * size ** 2, moved=4 * size ** 2
    )(drive4, before, third, fourth)
    other_term = lax.ppermute(own_term, "tm", swap)

    def hop(value, turn):
        return lax.ppermute(value, "tm", [(2 * turn + 1, 2 * turn + 3)])

    begin = prior.reshape(1, size)
    came = begin
    chips = blocks_of_time // 2
    for turn in range(2):
        begin, value = call(
            functools.partial(early_hop_kernel, turn), (row, row), [V] * 6,
            flops=64 * size ** 2, moved=4 * size ** 2,
        )(begin, came, own, own_term, other, other_term)
        came = hop(value, turn)
    turned, term = call(
        pair_kernel, (matrix, row), [V] * 5, flops=2 * size ** 3, moved=6 * size ** 2
    )(own, own_term, other, other_term, value)
    for turn in range(2, chips):
        begin, value = call(
            functools.partial(hop_kernel, turn), (row, row), [V] * 4,
            flops=32 * size ** 2, moved=2 * size ** 2,
        )(begin, came, turned, term)
        if turn == 2:
            maps, terms = call(
                ready_kernel,
                (jax.ShapeDtypeStruct((size, steps_here * width), BF16), jax.ShapeDtypeStruct((steps_here, width), F32)),
                [V] * 8, flops=size ** 3, moved=4 * size ** 2,
            )(other, other_term, locals_, value, early[0], slab2, slab3, slab4)
        if turn + 1 < chips:
            came = hop(value, turn)
    got = lax.ppermute(begin, "tm", [(i + 1, i) for i in range(0, blocks_of_time, 2)])
    return call(
        out_kernel, jax.ShapeDtypeStruct((steps_here, width), F32), [V] * 4,
        flops=16 * size ** 2, moved=size ** 2,
    )(begin, got, maps, terms)


def solution(mesh):
    return jax.shard_map(
        shards,
        mesh=mesh,
        in_specs=(
            P("tm", None),
            P("tm", None),
            P("tm", "state", None, None),
            P("tm", "state"),
            P("tm", "state"),
            P("tm", "state", None),
            P(),
        ),
        out_specs=P("tm", "state"),
        check_vma=False,
    )
```

```python
import functools

import jax
import jax.numpy as jnp
from jax import lax
from jax.experimental import pallas as pl
from jax.experimental.pallas import tpu as pltpu
from jax.sharding import PartitionSpec as P

F32 = jnp.float32
BF16 = jnp.bfloat16
VMEM_LIMIT = 24 * 1024 * 1024
ROWS = 512


def three_parts(x):
    hi = x.astype(BF16).astype(F32)
    rest = x - hi
    mid = rest.astype(BF16).astype(F32)
    return hi, mid, rest - mid


def split_rows(x):
    hi, mid, lo = three_parts(x)
    row = lax.broadcasted_iota(jnp.int32, (16, x.shape[1]), 0)
    out = jnp.where(row == 0, hi, jnp.where(row == 1, mid, jnp.where(row == 2, lo, 0.0)))
    return out.astype(BF16)


def joined(rows):
    return jnp.sum(rows.astype(F32), axis=0, keepdims=True)


def times_t(x, matrix):
    out = lax.dot_general(split_rows(x), matrix, (((1,), (1,)), ((), ())), preferred_element_type=F32)
    return joined(out)


def times(x, matrix):
    return joined(jnp.dot(split_rows(x), matrix, preferred_element_type=F32))


def matmul(left_ref, right_ref, out_ref):
    def block(i, carry):
        at = pl.ds(pl.multiple_of(i * ROWS, ROWS), ROWS)
        out_ref[at, :] = jnp.dot(left_ref[at, :], right_ref[...], preferred_element_type=F32).astype(BF16)
        return carry

    lax.fori_loop(0, left_ref.shape[0] // ROWS, block, 0)


def core_here():
    return lax.rem(lax.axis_index("tm"), 2)


def chip_here():
    return lax.div(lax.axis_index("tm"), 2)


def drive_kernel(
    rows_ref, cols_ref, observations_ref, precisions_ref, blocks_ref, maps_ref, out_ref, weighted_ref, drive_ref, parts_ref, sems
):
    steps, count, side, _ = blocks_ref.shape
    width = maps_ref.shape[1]
    copies = []
    for j in range(steps // 2):
        rows = pl.ds(j * width, width)
        copies.append(pltpu.make_async_copy(maps_ref.at[steps // 2 + j], out_ref.at[rows, :], sems.at[j]))
        copies[j].start()
    weighted_ref[...] = (precisions_ref[...] * observations_ref[...]).astype(BF16).astype(F32)
    drive_ref[...] = jnp.zeros_like(drive_ref)
    parts_ref[...] = jnp.zeros_like(parts_ref)
    for t in range(steps):
        def block(b, carry):
            left = jnp.broadcast_to(weighted_ref[t, pl.ds(rows_ref[t, b], 1), :], (16, side)).astype(BF16)
            term = jnp.dot(left, blocks_ref[t, b], preferred_element_type=F32)
            at = pl.ds(cols_ref[t, b], 1)
            drive_ref[t, at, :] = drive_ref[t, at, :] + term[0:1, :]
            return carry

        lax.fori_loop(0, count, block, 0, unroll=4)
    for t in range(steps):
        for c in range(drive_ref.shape[1]):
            for i, part in enumerate(three_parts(drive_ref[t, c:c + 1, :])):
                parts_ref[3 * t + i:3 * t + i + 1, c * side:(c + 1) * side] = part
    out_ref[(steps // 2) * width:, :] = parts_ref[...].astype(BF16)
    for copy in copies:
        copy.wait()


def fetched(count, place, pieces, j, whole_ref, sems, first):
    width = whole_ref.shape[0] // count
    copies = []
    for r in range(count):
        at = pl.multiple_of(lax.rem(place + r, count) * width, width)
        copy = pltpu.make_async_copy(
            pieces[r].at[pl.ds(j * width, width), :], whole_ref.at[pl.ds(at, width), :], sems.at[first + r]
        )
        copy.start()
        copies.append(copy)
    return copies


def two_kernel(count, *refs):
    pieces, (two_ref, slab_ref, next_ref, one_ref, sems) = refs[:count], refs[count:]
    width = slab_ref.shape[0]
    place = lax.axis_index("state")
    ones = fetched(count, place, pieces, 0, one_ref, sems, 0)
    nexts = fetched(count, place, pieces, 1, next_ref, sems, count)
    for copy in ones + nexts:
        copy.wait()
    matmul(next_ref, one_ref, two_ref)
    slab_ref[...] = two_ref[pl.ds(pl.multiple_of(place * width, width), width), :]


def four_kernel(count, two_ref, *refs):
    pieces = refs[:count]
    four_ref, slab3_ref, slab4_ref, third_ref, fourth_ref, drive_ref, three_ref, parts_ref, sems = refs[count:]
    width = slab3_ref.shape[0]
    place = lax.axis_index("state")
    thirds = fetched(count, place, pieces, 0, third_ref, sems, 0)
    fourths = fetched(count, place, pieces, 1, fourth_ref, sems, count)
    parts = []
    for r in range(count):
        parts.append(pltpu.make_async_copy(pieces[r].at[pl.ds(2 * width, 16), :], parts_ref.at[r], sems.at[2 * count + r]))
        parts[r].start()
    mine = pl.ds(pl.multiple_of(place * width, width), width)
    for copy in thirds:
        copy.wait()
    matmul(third_ref, two_ref, three_ref)
    slab3_ref[...] = three_ref[mine, :]
    for copy in fourths:
        copy.wait()
    matmul(fourth_ref, three_ref, four_ref)
    slab4_ref[...] = four_ref[mine, :]
    for copy in parts:
        copy.wait()
    drive_ref[...] = jnp.sum(parts_ref[...].astype(F32), axis=0)


def local_kernel(drive_ref, prior_ref, second_ref, third_ref, fourth_ref, four_ref, locals_ref, term_ref, mean_ref):
    local = joined(drive_ref[0:3, :])
    locals_ref[0:1, :] = local
    for j, map_ref in enumerate((second_ref, third_ref, fourth_ref)):
        local = times_t(local, map_ref[...]) + joined(drive_ref[3 * j + 3:3 * j + 6, :])
        locals_ref[j + 1:j + 2, :] = local
    term_ref[...] = split_rows(local)
    mean_ref[...] = local

    @pl.when(lax.axis_index("tm") == 0)
    def _():
        mean_ref[...] = times_t(prior_ref[...], four_ref[...]) + local


def pair_kernel(own_ref, own_term_ref, other_ref, other_term_ref, after_ref, qt_ref, q_ref):
    @pl.when(core_here() != 0)
    def _():
        def block(i, carry):
            at = pl.ds(pl.multiple_of(i * ROWS, ROWS), ROWS)
            out = jnp.dot(own_ref[at, :], other_ref[...], preferred_element_type=F32)
            qt_ref[:, at] = out.T.astype(BF16)
            return carry

        lax.fori_loop(0, own_ref.shape[0] // ROWS, block, 0)
        q_ref[...] = times_t(joined(other_term_ref[...]), own_ref[...]) + joined(own_term_ref[...])


def first_hop_kernel(mean_ref, own_ref, term_ref, value_ref):
    value_ref[...] = mean_ref[...]

    @pl.when(lax.axis_index("tm") == 1)
    def _():
        value_ref[...] = times_t(mean_ref[...], own_ref[...]) + joined(term_ref[...])


def second_hop_kernel(begin_ref, came_ref, own_ref, own_term_ref, other_ref, other_term_ref, held_ref, value_ref):
    held_ref[...] = begin_ref[...]
    value_ref[...] = begin_ref[...]

    @pl.when(lax.axis_index("tm") == 3)
    def _():
        begin = came_ref[...]
        held_ref[...] = begin
        between = times_t(begin, other_ref[...]) + joined(other_term_ref[...])
        value_ref[...] = times_t(between, own_ref[...]) + joined(own_term_ref[...])


def hop_kernel(turn, begin_ref, came_ref, qt_ref, q_ref, held_ref, value_ref):
    here = jnp.logical_and(chip_here() == turn, core_here() != 0)

    @pl.when(here)
    def _():
        begin = came_ref[...]
        held_ref[...] = begin
        value_ref[...] = times(begin, qt_ref[...]) + q_ref[...]

    @pl.when(jnp.logical_not(here))
    def _():
        held_ref[...] = begin_ref[...]
        value_ref[...] = begin_ref[...]


def ready_kernel(other_ref, other_term_ref, other0_ref, other0_term_ref, locals_ref, after_ref, *refs):
    slabs, (maps_ref, terms_ref) = refs[:-2], refs[-2:]
    width, size = slabs[1].shape
    mine = pl.ds(pl.multiple_of(lax.axis_index("state") * width, width), width)

    def write(whole_ref, term_ref):
        for j, slab_ref in enumerate(slabs):
            at = slice(j * width, (j + 1) * width)
            out = jnp.dot(slab_ref[:width, :], whole_ref[...], preferred_element_type=F32)
            maps_ref[:, at] = out.T.astype(BF16)
            term = times_t(joined(term_ref[...]), slab_ref[:width, :])
            terms_ref[j:j + 1, :] = term + locals_ref[j:j + 1, mine]

    @pl.when(core_here() == 0)
    def _():
        for j, slab_ref in enumerate(slabs):
            maps_ref[:, j * width:(j + 1) * width] = slab_ref[:width, :].astype(F32).T.astype(BF16)
            terms_ref[j:j + 1, :] = locals_ref[j:j + 1, mine]

    @pl.when(lax.axis_index("tm") == 1)
    def _():
        write(other0_ref, other0_term_ref)

    @pl.when(jnp.logical_and(core_here() != 0, lax.axis_index("tm") != 1))
    def _():
        write(other_ref, other_term_ref)


def out_kernel(last, begin_ref, came_ref, got_ref, last_ref, maps_ref, terms_ref, out_ref):
    steps, width = out_ref.shape
    first, second = (got_ref[...], last_ref[...]), (begin_ref[...], came_ref[...])
    at_last = chip_here() == last
    begin = jnp.where(
        core_here() == 0, jnp.where(at_last, first[1], first[0]), jnp.where(at_last, second[1], second[0])
    )
    row = times(begin, maps_ref[...])
    for j in range(steps):
        out_ref[j:j + 1, :] = row[:, j * width:(j + 1) * width] + terms_ref[j:j + 1, :]


def call(kernel, out_shape, spaces, scratch=(), flops=0, moved=0):
    return pl.pallas_call(
        kernel,
        out_shape=out_shape,
        in_specs=[pl.BlockSpec(memory_space=s) for s in spaces],
        out_specs=jax.tree.map(lambda _: pl.BlockSpec(memory_space=pltpu.VMEM), out_shape),
        scratch_shapes=list(scratch),
        compiler_params=pltpu.CompilerParams(vmem_limit_bytes=VMEM_LIMIT),
        cost_estimate=pl.CostEstimate(flops=flops, bytes_accessed=moved, transcendentals=0),
    )


def after(value, *needed):
    return lax.optimization_barrier((value, needed))[0]


def ring_rounds(parts, axis, needed):
    count = lax.axis_size(axis)
    forward = [(i, (i + 1) % count) for i in range(count)]
    backward = [((i + 1) % count, i) for i in range(count)]
    half = count // 2
    found = [{0: part} for part in parts]
    for r in range(1, half + 1):
        for i, pieces in enumerate(found):
            left, right = pieces[(count - r + 1) % count], pieces[r - 1]
            more = needed(r, i, found)
            if more:
                left, right = after((left, right), *more)
            if r < half or i % 2 == 0:
                pieces[count - r] = lax.ppermute(left, axis, forward)
            if r < half or i % 2 == 1:
                pieces[r] = lax.ppermute(right, axis, backward)
    return [[pieces[r] for r in range(count)] for pieces in found]


def shards(observations, precisions, blocks, block_rows, block_cols, transition, prior):
    steps_here, width, size = transition.shape
    side = blocks.shape[2]
    count = lax.axis_size("state")
    blocks_of_time = lax.axis_size("tm")
    V, S, A = pltpu.VMEM, pltpu.SMEM, pl.ANY

    matrix = jax.ShapeDtypeStruct((size, size), BF16)
    slab = jax.ShapeDtypeStruct((width, size), BF16)
    rows = jax.ShapeDtypeStruct((16, size), BF16)
    steps = jax.ShapeDtypeStruct((steps_here, size), F32)
    row = jax.ShapeDtypeStruct((1, size), F32)
    whole = pltpu.VMEM((size, size), BF16)

    half = steps_here // 2
    pieces = (steps_here, observations.shape[1] // side, side)
    packed = call(
        drive_kernel, jax.ShapeDtypeStruct((half * width + 16, size), BF16), [S, S, V, V, V, A],
        [
            pltpu.VMEM(pieces, F32),
            pltpu.VMEM((steps_here, size // side, side), F32),
            pltpu.VMEM((16, size), F32),
            pltpu.SemaphoreType.DMA((half,)),
        ],
        flops=10 ** 7, moved=2 ** 21,
    )(block_rows, block_cols, observations.reshape(pieces), precisions.reshape(pieces), blocks, transition)
    early, late = ring_rounds(
        [transition[:half].reshape(half * width, size), packed], "state",
        lambda r, i, found: (packed,) if (r, i) == (2, 0) else (),
    )
    two, slab2, second = call(
        functools.partial(two_kernel, count), (matrix, slab, matrix), [A] * count,
        [whole, pltpu.SemaphoreType.DMA((2 * count,))], flops=2 * size ** 3, moved=6 * size ** 2,
    )(*early)
    own, slab3, slab4, third, fourth, drive = call(
        functools.partial(four_kernel, count),
        (matrix, slab, slab, matrix, matrix, jax.ShapeDtypeStruct((16, size), F32)),
        [V] + [A] * count,
        [whole, pltpu.VMEM((count, 16, size), BF16), pltpu.SemaphoreType.DMA((3 * count,))],
        flops=4 * size ** 3, moved=8 * size ** 2,
    )(two, *late)

    begin = prior.reshape(1, size)
    pairs = [(i, i + 1) for i in range(0, blocks_of_time, 2)]
    other = lax.ppermute(own, "tm", pairs[1:])
    locals_, own_term, mean = call(
        local_kernel, (steps, rows, row), [V] * 6, flops=128 * size ** 2, moved=8 * size ** 2
    )(drive, begin, second, third, fourth, own)
    mean = lax.ppermute(mean, "tm", pairs[:1])
    other_term = lax.ppermute(own_term, "tm", pairs[1:])

    def hop(value, turn):
        return lax.ppermute(value, "tm", [(2 * turn + 1, 2 * turn + 3)])

    chips = blocks_of_time // 2
    value = call(first_hop_kernel, row, [V] * 3, flops=32 * size ** 2, moved=2 * size ** 2)(mean, own, own_term)
    came = hop(value, 0)
    begin, value = call(
        second_hop_kernel, (row, row), [V] * 6, flops=64 * size ** 2, moved=4 * size ** 2
    )(begin, came, own, own_term, other, other_term)
    came = hop(value, 1)
    turned, term = call(
        pair_kernel, (matrix, row), [V] * 5, flops=2 * size ** 3, moved=6 * size ** 2
    )(own, own_term, other, other_term, value)
    for turn in range(2, chips - 1):
        begin, value = call(
            functools.partial(hop_kernel, turn), (row, row), [V] * 4,
            flops=32 * size ** 2, moved=2 * size ** 2,
        )(begin, came, turned, term)
        came = hop(value, turn)
        if turn == 2:
            other0, other0_term = lax.ppermute(after((own, own_term), value), "tm", pairs[:1])
        if turn == 3:
            maps, terms = call(
                ready_kernel,
                (jax.ShapeDtypeStruct((size, steps_here * width), BF16), jax.ShapeDtypeStruct((steps_here, width), F32)),
                [V] * 10, flops=size ** 3, moved=4 * size ** 2,
            )(other, other_term, other0, other0_term, locals_, value, early[0], slab2, slab3, slab4)
        if turn == 4:
            came = after(came, maps)
    got = lax.ppermute(begin, "tm", [(b, a) for a, b in pairs[:-1]])
    last = lax.ppermute(came, "tm", [(b, a) for a, b in pairs[-1:]])
    return call(
        functools.partial(out_kernel, chips - 1), jax.ShapeDtypeStruct((steps_here, width), F32), [V] * 6,
        flops=16 * size ** 2, moved=size ** 2,
    )(begin, came, got, last, maps, terms)


def solution(mesh):
    return jax.shard_map(
        shards,
        mesh=mesh,
        in_specs=(
            P("tm", None),
            P("tm", None),
            P("tm", "state", None, None),
            P("tm", "state"),
            P("tm", "state"),
            P("tm", "state", None),
            P(),
        ),
        out_specs=P("tm", "state"),
        check_vma=False,
    )
```

```python
import functools

import jax
import jax.numpy as jnp
from jax import lax
from jax.experimental import pallas as pl
from jax.experimental.pallas import tpu as pltpu
from jax.sharding import PartitionSpec as P

F32 = jnp.float32
BF16 = jnp.bfloat16
VMEM_LIMIT = 24 * 1024 * 1024
ROWS = 512


def three_parts(x):
    hi = x.astype(BF16).astype(F32)
    rest = x - hi
    mid = rest.astype(BF16).astype(F32)
    return hi, mid, rest - mid


def split_rows(x):
    hi, mid, lo = three_parts(x)
    row = lax.broadcasted_iota(jnp.int32, (16, x.shape[1]), 0)
    out = jnp.where(row == 0, hi, jnp.where(row == 1, mid, jnp.where(row == 2, lo, 0.0)))
    return out.astype(BF16)


def joined(rows):
    return jnp.sum(rows.astype(F32), axis=0, keepdims=True)


def times_t(x, matrix):
    out = lax.dot_general(split_rows(x), matrix, (((1,), (1,)), ((), ())), preferred_element_type=F32)
    return joined(out)


def times(x, matrix):
    return joined(jnp.dot(split_rows(x), matrix, preferred_element_type=F32))


def matmul(left_ref, right_ref, out_ref):
    def block(i, carry):
        at = pl.ds(pl.multiple_of(i * ROWS, ROWS), ROWS)
        out_ref[at, :] = jnp.dot(left_ref[at, :], right_ref[...], preferred_element_type=F32).astype(BF16)
        return carry

    lax.fori_loop(0, left_ref.shape[0] // ROWS, block, 0)


def core_here():
    return lax.rem(lax.axis_index("tm"), 2)


def chip_here():
    return lax.div(lax.axis_index("tm"), 2)


def drive_kernel(
    rows_ref, cols_ref, values_ref, blocks_ref, maps_ref, out_ref, weighted_ref, parts_ref, sems
):
    steps, count, side, _ = blocks_ref.shape
    later, width, size = maps_ref.shape
    copies = []
    for j in range(later):
        copies.append(pltpu.make_async_copy(maps_ref.at[j], out_ref.at[pl.ds(j * width, width), :], sems.at[j]))
        copies[j].start()
    weighted = values_ref[...].astype(F32)
    pieces = weighted_ref.shape[0]
    for r in range(pieces):
        weighted_ref[r] = weighted[:, r * side:(r + 1) * side]
    parts_ref[...] = jnp.zeros_like(parts_ref)
    piece = lax.broadcasted_iota(jnp.int32, (pieces, count), 0)
    column = lax.broadcasted_iota(jnp.int32, (size // side, count), 0)
    own = lax.broadcasted_iota(jnp.int32, (count, count * side), 0) == (
        lax.broadcasted_iota(jnp.int32, (count, count * side), 1) // side
    )
    for t in range(steps):
        chosen = (piece == rows_ref[t:t + 1, :]).astype(F32).astype(BF16)
        left = lax.dot_general(
            chosen, weighted_ref[:, t, :].astype(BF16), (((0,), (0,)), ((), ())), preferred_element_type=F32
        )
        left = jnp.concatenate([left] * count, axis=1)
        left = jnp.where(own, left, 0.0).astype(BF16)
        terms = jnp.dot(left, blocks_ref[t].reshape(count * side, side), preferred_element_type=F32)
        chosen = (column == cols_ref[t:t + 1, :]).astype(F32).astype(BF16)
        drive = sum(jnp.dot(chosen, part.astype(BF16), preferred_element_type=F32) for part in three_parts(terms))
        for i, part in enumerate(three_parts(drive)):
            for c in range(size // side):
                parts_ref[3 * t + i:3 * t + i + 1, c * side:(c + 1) * side] = part[c:c + 1, :]
    out_ref[later * width:, :] = parts_ref[...].astype(BF16)
    for copy in copies:
        copy.wait()


def fetched(count, place, pieces, j, whole_ref, sems, first):
    width = whole_ref.shape[0] // count
    copies = []
    for r in range(count):
        at = pl.multiple_of(lax.rem(place + r, count) * width, width)
        copy = pltpu.make_async_copy(
            pieces[r].at[pl.ds(j * width, width), :], whole_ref.at[pl.ds(at, width), :], sems.at[first + r]
        )
        copy.start()
        copies.append(copy)
    return copies


def two_kernel(count, *refs):
    pieces, (two_ref, slab_ref, one_ref, next_ref, sems) = refs[:count], refs[count:]
    width = slab_ref.shape[0]
    place = lax.axis_index("state")
    ones = fetched(count, place, pieces, 0, one_ref, sems, 0)
    nexts = fetched(count, place, pieces, 1, next_ref, sems, count)
    for copy in ones + nexts:
        copy.wait()
    matmul(next_ref, one_ref, two_ref)
    slab_ref[...] = two_ref[pl.ds(pl.multiple_of(place * width, width), width), :]


def gather_kernel(count, prior_ref, first_ref, second_ref, *refs):
    pieces = refs[:count]
    third_ref, fourth_ref, drive_ref, mean_ref, parts_ref, sems = refs[count:]
    width = third_ref.shape[0] // count
    place = lax.axis_index("state")
    copies = fetched(count, place, pieces, 0, third_ref, sems, 0)
    copies += fetched(count, place, pieces, 1, fourth_ref, sems, count)
    parts = []
    for r in range(count):
        parts.append(pltpu.make_async_copy(pieces[r].at[pl.ds(2 * width, 16), :], parts_ref.at[r], sems.at[2 * count + r]))
        parts[r].start()
    for copy in copies + parts:
        copy.wait()
    drive_ref[...] = jnp.sum(parts_ref[...].astype(F32), axis=0)
    mean_ref[...] = prior_ref[...]

    @pl.when(lax.axis_index("tm") == 0)
    def _():
        mean = prior_ref[...]
        for j, map_ref in enumerate((first_ref, second_ref, third_ref, fourth_ref)):
            mean = times_t(mean, map_ref[...]) + joined(drive_ref[3 * j:3 * j + 3, :])
        mean_ref[...] = mean


def four_kernel(two_ref, third_ref, fourth_ref, four_ref, slab3_ref, slab4_ref, three_ref):
    width = slab3_ref.shape[0]
    mine = pl.ds(pl.multiple_of(lax.axis_index("state") * width, width), width)
    matmul(third_ref, two_ref, three_ref)
    slab3_ref[...] = three_ref[mine, :]
    matmul(fourth_ref, three_ref, four_ref)
    slab4_ref[...] = four_ref[mine, :]


def local_kernel(drive_ref, second_ref, third_ref, fourth_ref, locals_ref, term_ref):
    local = joined(drive_ref[0:3, :])
    locals_ref[0:1, :] = local
    for j, map_ref in enumerate((second_ref, third_ref, fourth_ref)):
        local = times_t(local, map_ref[...]) + joined(drive_ref[3 * j + 3:3 * j + 6, :])
        locals_ref[j + 1:j + 2, :] = local
    term_ref[...] = split_rows(local)


def pair_kernel(own_ref, own_term_ref, other_ref, other_term_ref, after_ref, qt_ref, q_ref):
    @pl.when(core_here() != 0)
    def _():
        def block(i, carry):
            at = pl.ds(pl.multiple_of(i * ROWS, ROWS), ROWS)
            out = jnp.dot(own_ref[at, :], other_ref[...], preferred_element_type=F32)
            qt_ref[:, at] = out.T.astype(BF16)
            return carry

        lax.fori_loop(0, own_ref.shape[0] // ROWS, block, 0)
        q_ref[...] = times_t(joined(other_term_ref[...]), own_ref[...]) + joined(own_term_ref[...])


def first_hop_kernel(mean_ref, own_ref, term_ref, value_ref):
    value_ref[...] = mean_ref[...]

    @pl.when(lax.axis_index("tm") == 1)
    def _():
        value_ref[...] = times_t(mean_ref[...], own_ref[...]) + joined(term_ref[...])


def second_hop_kernel(begin_ref, came_ref, own_ref, own_term_ref, other_ref, other_term_ref, held_ref, value_ref):
    held_ref[...] = begin_ref[...]
    value_ref[...] = begin_ref[...]

    @pl.when(lax.axis_index("tm") == 3)
    def _():
        begin = came_ref[...]
        held_ref[...] = begin
        between = times_t(begin, other_ref[...]) + joined(other_term_ref[...])
        value_ref[...] = times_t(between, own_ref[...]) + joined(own_term_ref[...])


def hop_kernel(turn, begin_ref, came_ref, qt_ref, q_ref, held_ref, value_ref):
    here = jnp.logical_and(chip_here() == turn, core_here() != 0)

    @pl.when(here)
    def _():
        begin = came_ref[...]
        held_ref[...] = begin
        value_ref[...] = times(begin, qt_ref[...]) + q_ref[...]

    @pl.when(jnp.logical_not(here))
    def _():
        held_ref[...] = begin_ref[...]
        value_ref[...] = begin_ref[...]


def ready_kernel(other_ref, other_term_ref, other0_ref, other0_term_ref, locals_ref, after_ref, *refs):
    slabs, (maps_ref, terms_ref) = refs[:-2], refs[-2:]
    width, size = slabs[1].shape
    mine = pl.ds(pl.multiple_of(lax.axis_index("state") * width, width), width)

    def write(whole_ref, term_ref):
        for j, slab_ref in enumerate(slabs):
            at = slice(j * width, (j + 1) * width)
            out = jnp.dot(slab_ref[:width, :], whole_ref[...], preferred_element_type=F32)
            maps_ref[:, at] = out.T.astype(BF16)
            term = times_t(joined(term_ref[...]), slab_ref[:width, :])
            terms_ref[j:j + 1, :] = term + locals_ref[j:j + 1, mine]

    @pl.when(core_here() == 0)
    def _():
        for j, slab_ref in enumerate(slabs):
            maps_ref[:, j * width:(j + 1) * width] = slab_ref[:width, :].astype(F32).T.astype(BF16)
            terms_ref[j:j + 1, :] = locals_ref[j:j + 1, mine]

    @pl.when(lax.axis_index("tm") == 1)
    def _():
        write(other0_ref, other0_term_ref)

    @pl.when(jnp.logical_and(core_here() != 0, lax.axis_index("tm") != 1))
    def _():
        write(other_ref, other_term_ref)


def out_kernel(last, begin_ref, came_ref, got_ref, last_ref, maps_ref, terms_ref, out_ref):
    steps, width = out_ref.shape
    first, second = (got_ref[...], last_ref[...]), (begin_ref[...], came_ref[...])
    at_last = chip_here() == last
    begin = jnp.where(
        core_here() == 0, jnp.where(at_last, first[1], first[0]), jnp.where(at_last, second[1], second[0])
    )
    row = times(begin, maps_ref[...])
    for j in range(steps):
        out_ref[j:j + 1, :] = row[:, j * width:(j + 1) * width] + terms_ref[j:j + 1, :]


def call(kernel, out_shape, spaces, scratch=(), flops=0, moved=0):
    return pl.pallas_call(
        kernel,
        out_shape=out_shape,
        in_specs=[pl.BlockSpec(memory_space=s) for s in spaces],
        out_specs=jax.tree.map(lambda _: pl.BlockSpec(memory_space=pltpu.VMEM), out_shape),
        scratch_shapes=list(scratch),
        compiler_params=pltpu.CompilerParams(vmem_limit_bytes=VMEM_LIMIT),
        cost_estimate=pl.CostEstimate(flops=flops, bytes_accessed=moved, transcendentals=0),
    )


def after(value, *needed):
    return lax.optimization_barrier((value, needed))[0]


def ring_rounds(parts, axis, needed):
    count = lax.axis_size(axis)
    forward = [(i, (i + 1) % count) for i in range(count)]
    backward = [((i + 1) % count, i) for i in range(count)]
    half = count // 2
    found = [{0: part} for part in parts]
    for r in range(1, half + 1):
        for i, pieces in enumerate(found):
            left, right = pieces[(count - r + 1) % count], pieces[r - 1]
            more = needed(r, i, found)
            if more:
                left, right = after((left, right), *more)
            if r < half or i % 2 == 0:
                pieces[count - r] = lax.ppermute(left, axis, forward)
            if r < half or i % 2 == 1:
                pieces[r] = lax.ppermute(right, axis, backward)
    return [[pieces[r] for r in range(count)] for pieces in found]


def shards(observations, precisions, blocks, block_rows, block_cols, transition, prior):
    steps_here, width, size = transition.shape
    side = blocks.shape[2]
    count = lax.axis_size("state")
    blocks_of_time = lax.axis_size("tm")
    V, S, A = pltpu.VMEM, pltpu.SMEM, pl.ANY

    matrix = jax.ShapeDtypeStruct((size, size), BF16)
    slab = jax.ShapeDtypeStruct((width, size), BF16)
    rows = jax.ShapeDtypeStruct((16, size), BF16)
    steps = jax.ShapeDtypeStruct((steps_here, size), F32)
    row = jax.ShapeDtypeStruct((1, size), F32)
    whole = pltpu.VMEM((size, size), BF16)

    half = steps_here // 2
    pieces = observations.shape[1] // side
    packed = call(
        drive_kernel, jax.ShapeDtypeStruct((half * width + 16, size), BF16), [V] * 4 + [A],
        [
            pltpu.VMEM((pieces, steps_here, side), F32),
            pltpu.VMEM((16, size), F32),
            pltpu.SemaphoreType.DMA((half,)),
        ],
        flops=10 ** 7, moved=2 ** 21,
    )(block_rows, block_cols, (precisions * observations).astype(BF16), blocks, transition[half:])
    early, late = ring_rounds(
        [transition[:half].reshape(half * width, size), packed], "state",
        lambda r, i, found: (packed,) if (r, i) == (2, 0) else (),
    )
    begin = prior.reshape(1, size)
    two, slab2, first, second = call(
        functools.partial(two_kernel, count), (matrix, slab, matrix, matrix), [A] * count,
        [pltpu.SemaphoreType.DMA((2 * count,))], flops=2 * size ** 3, moved=6 * size ** 2,
    )(*early)
    third, fourth, drive, mean = call(
        functools.partial(gather_kernel, count),
        (matrix, matrix, jax.ShapeDtypeStruct((16, size), F32), row),
        [V] * 3 + [A] * count,
        [pltpu.VMEM((count, 16, size), BF16), pltpu.SemaphoreType.DMA((3 * count,))],
        flops=128 * size ** 2, moved=8 * size ** 2,
    )(begin, first, second, *late)
    pairs = [(i, i + 1) for i in range(0, blocks_of_time, 2)]
    mean = lax.ppermute(mean, "tm", pairs[:1])
    own, slab3, slab4 = call(
        four_kernel, (matrix, slab, slab), [V] * 3, [whole], flops=4 * size ** 3, moved=8 * size ** 2,
    )(two, third, fourth)
    other = lax.ppermute(own, "tm", pairs[1:])
    locals_, own_term = call(
        local_kernel, (steps, rows), [V] * 4, flops=96 * size ** 2, moved=6 * size ** 2
    )(drive, second, third, fourth)
    other_term = lax.ppermute(own_term, "tm", pairs[1:])

    def hop(value, turn):
        return lax.ppermute(value, "tm", [(2 * turn + 1, 2 * turn + 3)])

    chips = blocks_of_time // 2
    value = call(first_hop_kernel, row, [V] * 3, flops=32 * size ** 2, moved=2 * size ** 2)(mean, own, own_term)
    came = hop(value, 0)
    begin, value = call(
        second_hop_kernel, (row, row), [V] * 6, flops=64 * size ** 2, moved=4 * size ** 2
    )(begin, came, own, own_term, other, other_term)
    came = hop(value, 1)
    turned, term = call(
        pair_kernel, (matrix, row), [V] * 5, flops=2 * size ** 3, moved=6 * size ** 2
    )(own, own_term, other, other_term, value)
    other0, other0_term = lax.ppermute(after((own, own_term), turned), "tm", pairs[:1])
    for turn in range(2, chips - 1):
        begin, value = call(
            functools.partial(hop_kernel, turn), (row, row), [V] * 4,
            flops=32 * size ** 2, moved=2 * size ** 2,
        )(begin, came, turned, term)
        came = hop(value, turn)
        if turn == 3:
            maps, terms = call(
                ready_kernel,
                (jax.ShapeDtypeStruct((size, steps_here * width), BF16), jax.ShapeDtypeStruct((steps_here, width), F32)),
                [V] * 10, flops=size ** 3, moved=4 * size ** 2,
            )(other, other_term, other0, other0_term, locals_, value, early[0], slab2, slab3, slab4)
        if turn == 4:
            came = after(came, maps)
    got = lax.ppermute(begin, "tm", [(b, a) for a, b in pairs[:-1]])
    last = lax.ppermute(came, "tm", [(b, a) for a, b in pairs[-1:]])
    return call(
        functools.partial(out_kernel, chips - 1), jax.ShapeDtypeStruct((steps_here, width), F32), [V] * 6,
        flops=16 * size ** 2, moved=size ** 2,
    )(begin, came, got, last, maps, terms)


def solution(mesh):
    return jax.shard_map(
        shards,
        mesh=mesh,
        in_specs=(
            P("tm", None),
            P("tm", None),
            P("tm", "state", None, None),
            P("tm", "state"),
            P("tm", "state"),
            P("tm", "state", None),
            P(),
        ),
        out_specs=P("tm", "state"),
        check_vma=False,
    )
```

```python
import functools

import jax
import jax.numpy as jnp
from jax import lax
from jax.experimental import pallas as pl
from jax.experimental.pallas import tpu as pltpu
from jax.sharding import PartitionSpec as P

F32 = jnp.float32
BF16 = jnp.bfloat16
VMEM_LIMIT = 24 * 1024 * 1024
ROWS = 512


def three_parts(x):
    hi = x.astype(BF16).astype(F32)
    rest = x - hi
    mid = rest.astype(BF16).astype(F32)
    return hi, mid, rest - mid


def split_rows(x):
    hi, mid, lo = three_parts(x)
    row = lax.broadcasted_iota(jnp.int32, (16, x.shape[1]), 0)
    out = jnp.where(row == 0, hi, jnp.where(row == 1, mid, jnp.where(row == 2, lo, 0.0)))
    return out.astype(BF16)


def joined(rows):
    return jnp.sum(rows.astype(F32), axis=0, keepdims=True)


def times_t(x, matrix):
    out = lax.dot_general(split_rows(x), matrix, (((1,), (1,)), ((), ())), preferred_element_type=F32)
    return joined(out)


def times(x, matrix):
    return joined(jnp.dot(split_rows(x), matrix, preferred_element_type=F32))


def matmul(left_ref, right_ref, out_ref):
    def block(i, carry):
        at = pl.ds(pl.multiple_of(i * ROWS, ROWS), ROWS)
        out_ref[at, :] = jnp.dot(left_ref[at, :], right_ref[...], preferred_element_type=F32).astype(BF16)
        return carry

    lax.fori_loop(0, left_ref.shape[0] // ROWS, block, 0)


def core_here():
    return lax.rem(lax.axis_index("tm"), 2)


def chip_here():
    return lax.div(lax.axis_index("tm"), 2)


def drive_kernel(
    rows_ref, cols_ref, values_ref, blocks_ref, maps_ref, out_ref, weighted_ref, parts_ref, sems
):
    steps, count, side, _ = blocks_ref.shape
    later, width, size = maps_ref.shape
    copies = []
    for j in range(later):
        copies.append(pltpu.make_async_copy(maps_ref.at[j], out_ref.at[pl.ds(j * width, width), :], sems.at[j]))
        copies[j].start()
    weighted = values_ref[...].astype(F32)
    pieces = weighted_ref.shape[0]
    for r in range(pieces):
        weighted_ref[r] = weighted[:, r * side:(r + 1) * side]
    parts_ref[...] = jnp.zeros_like(parts_ref)
    piece = lax.broadcasted_iota(jnp.int32, (pieces, count), 0)
    column = lax.broadcasted_iota(jnp.int32, (size // side, count), 0)
    own = lax.broadcasted_iota(jnp.int32, (count, count * side), 0) == (
        lax.broadcasted_iota(jnp.int32, (count, count * side), 1) // side
    )
    for t in range(steps):
        chosen = (piece == rows_ref[t:t + 1, :]).astype(F32).astype(BF16)
        left = lax.dot_general(
            chosen, weighted_ref[:, t, :].astype(BF16), (((0,), (0,)), ((), ())), preferred_element_type=F32
        )
        left = jnp.concatenate([left] * count, axis=1)
        left = jnp.where(own, left, 0.0).astype(BF16)
        terms = jnp.dot(left, blocks_ref[t].reshape(count * side, side), preferred_element_type=F32)
        chosen = (column == cols_ref[t:t + 1, :]).astype(F32).astype(BF16)
        drive = sum(jnp.dot(chosen, part.astype(BF16), preferred_element_type=F32) for part in three_parts(terms))
        for i, part in enumerate(three_parts(drive)):
            for c in range(size // side):
                parts_ref[3 * t + i:3 * t + i + 1, c * side:(c + 1) * side] = part[c:c + 1, :]
    out_ref[later * width:, :] = parts_ref[...].astype(BF16)
    for copy in copies:
        copy.wait()


def fetched(count, place, pieces, j, whole_ref, sems, first):
    width = whole_ref.shape[0] // count
    copies = []
    for r in range(count):
        at = pl.multiple_of(lax.rem(place + r, count) * width, width)
        copy = pltpu.make_async_copy(
            pieces[r].at[pl.ds(j * width, width), :], whole_ref.at[pl.ds(at, width), :], sems.at[first + r]
        )
        copy.start()
        copies.append(copy)
    return copies


def two_kernel(count, *refs):
    pieces, (two_ref, slab_ref, next_ref, one_ref, sems) = refs[:count], refs[count:]
    width = slab_ref.shape[0]
    place = lax.axis_index("state")
    ones = fetched(count, place, pieces, 0, one_ref, sems, 0)
    nexts = fetched(count, place, pieces, 1, next_ref, sems, count)
    for copy in ones + nexts:
        copy.wait()
    matmul(next_ref, one_ref, two_ref)
    slab_ref[...] = two_ref[pl.ds(pl.multiple_of(place * width, width), width), :]


def four_kernel(count, two_ref, *refs):
    pieces = refs[:count]
    four_ref, slab3_ref, slab4_ref, third_ref, fourth_ref, drive_ref, three_ref, parts_ref, sems = refs[count:]
    width = slab3_ref.shape[0]
    place = lax.axis_index("state")
    thirds = fetched(count, place, pieces, 0, third_ref, sems, 0)
    fourths = fetched(count, place, pieces, 1, fourth_ref, sems, count)
    parts = []
    for r in range(count):
        parts.append(pltpu.make_async_copy(pieces[r].at[pl.ds(2 * width, 16), :], parts_ref.at[r], sems.at[2 * count + r]))
        parts[r].start()
    mine = pl.ds(pl.multiple_of(place * width, width), width)
    for copy in thirds:
        copy.wait()
    matmul(third_ref, two_ref, three_ref)
    slab3_ref[...] = three_ref[mine, :]
    for copy in fourths:
        copy.wait()
    matmul(fourth_ref, three_ref, four_ref)
    slab4_ref[...] = four_ref[mine, :]
    for copy in parts:
        copy.wait()
    drive_ref[...] = jnp.sum(parts_ref[...].astype(F32), axis=0)


def local_kernel(drive_ref, second_ref, third_ref, fourth_ref, locals_ref, term_ref):
    local = joined(drive_ref[0:3, :])
    locals_ref[0:1, :] = local
    for j, map_ref in enumerate((second_ref, third_ref, fourth_ref)):
        local = times_t(local, map_ref[...]) + joined(drive_ref[3 * j + 3:3 * j + 6, :])
        locals_ref[j + 1:j + 2, :] = local
    term_ref[...] = split_rows(local)


DIRECT = 3


def pair_kernel(own_ref, own_term_ref, other_ref, other_term_ref, turned_ref):
    size = own_ref.shape[0]

    @pl.when(jnp.logical_and(core_here() != 0, chip_here() >= DIRECT))
    def _():
        def block(i, carry):
            at = pl.ds(pl.multiple_of(i * ROWS, ROWS), ROWS)
            out = jnp.dot(own_ref[at, :], other_ref[...], preferred_element_type=F32)
            turned_ref[:size, at] = out.T.astype(BF16)
            return carry

        lax.fori_loop(0, size // ROWS, block, 0)
        term = times_t(joined(other_term_ref[...]), own_ref[...]) + joined(own_term_ref[...])
        turned_ref[size:, :] = split_rows(term)


def applied(x, turned_ref):
    size = x.shape[1]
    return times(x, turned_ref[:size, :]) + joined(turned_ref[size:, :])


def direct_kernel(turn, begin_ref, came_ref, own_ref, own_term_ref, other_ref, other_term_ref, held_ref, value_ref):
    held_ref[...] = begin_ref[...]
    value_ref[...] = begin_ref[...]

    @pl.when(lax.axis_index("tm") == 2 * turn + 1)
    def _():
        begin = came_ref[...]
        held_ref[...] = begin
        between = times_t(begin, other_ref[...]) + joined(other_term_ref[...])
        value_ref[...] = times_t(between, own_ref[...]) + joined(own_term_ref[...])


def hop_kernel(turn, begin_ref, came_ref, turned_ref, held_ref, value_ref):
    here = lax.axis_index("tm") == 2 * turn + 1

    @pl.when(here)
    def _():
        begin = came_ref[...]
        held_ref[...] = begin
        value_ref[...] = applied(begin, turned_ref)

    @pl.when(jnp.logical_not(here))
    def _():
        held_ref[...] = begin_ref[...]
        value_ref[...] = begin_ref[...]


def double_kernel(firsts, came_ref, turned_ref, double_ref):
    size = turned_ref.shape[1]
    chip = chip_here()

    @pl.when((core_here() != 0) & (chip > firsts) & (lax.rem(chip, 2) == 1) & (chip < 2 * firsts - 1))
    def _():
        matmul(came_ref.at[:size, :], turned_ref.at[:size, :], double_ref)
        double_ref[size:, :] = split_rows(applied(joined(came_ref[size:, :]), turned_ref))


def far_kernel(chip, last, begin_ref, came_ref, before_ref, map_ref, double_ref, held_ref, value_ref):
    here = lax.axis_index("tm") == 2 * chip + 1

    @pl.when(here)
    def _():
        if last:
            value_ref[...] = before_ref[...]
        else:
            value_ref[...] = applied(came_ref[...], double_ref)
        held_ref[...] = applied(came_ref[...], map_ref)

    @pl.when(jnp.logical_not(here))
    def _():
        held_ref[...] = begin_ref[...]
        value_ref[...] = before_ref[...]


def final_kernel(firsts, held_ref, handed_ref, begin_ref):
    chip = chip_here()
    handed = jnp.logical_and(chip >= firsts, lax.rem(chip, 2) == 0)
    begin_ref[...] = jnp.where(handed, handed_ref[...], held_ref[...])


def ready_kernel(other_ref, other_term_ref, locals_ref, after_ref, *refs):
    slabs, (maps_ref, terms_ref) = refs[:-2], refs[-2:]
    width, size = slabs[1].shape
    mine = pl.ds(pl.multiple_of(lax.axis_index("state") * width, width), width)

    @pl.when(core_here() == 0)
    def _():
        for j, slab_ref in enumerate(slabs):
            maps_ref[:, j * width:(j + 1) * width] = slab_ref[:width, :].astype(F32).T.astype(BF16)
            terms_ref[j:j + 1, :] = locals_ref[j:j + 1, mine]

    @pl.when(core_here() != 0)
    def _():
        for j, slab_ref in enumerate(slabs):
            at = slice(j * width, (j + 1) * width)
            out = jnp.dot(slab_ref[:width, :], other_ref[...], preferred_element_type=F32)
            maps_ref[:, at] = out.T.astype(BF16)
            term = times_t(joined(other_term_ref[...]), slab_ref[:width, :])
            terms_ref[j:j + 1, :] = term + locals_ref[j:j + 1, mine]


def out_kernel(begin_ref, got_ref, maps_ref, terms_ref, out_ref):
    steps, width = out_ref.shape
    begin = jnp.where(core_here() == 0, got_ref[...], begin_ref[...])
    row = times(begin, maps_ref[...])
    for j in range(steps):
        out_ref[j:j + 1, :] = row[:, j * width:(j + 1) * width] + terms_ref[j:j + 1, :]


def call(kernel, out_shape, spaces, scratch=(), flops=0, moved=0):
    return pl.pallas_call(
        kernel,
        out_shape=out_shape,
        in_specs=[pl.BlockSpec(memory_space=s) for s in spaces],
        out_specs=jax.tree.map(lambda _: pl.BlockSpec(memory_space=pltpu.VMEM), out_shape),
        scratch_shapes=list(scratch),
        compiler_params=pltpu.CompilerParams(vmem_limit_bytes=VMEM_LIMIT),
        cost_estimate=pl.CostEstimate(flops=flops, bytes_accessed=moved, transcendentals=0),
    )


def after(value, *needed):
    return lax.optimization_barrier((value, needed))[0]


def ring_rounds(parts, axis, needed):
    count = lax.axis_size(axis)
    forward = [(i, (i + 1) % count) for i in range(count)]
    backward = [((i + 1) % count, i) for i in range(count)]
    half = count // 2
    found = [{0: part} for part in parts]
    for r in range(1, half + 1):
        for i, pieces in enumerate(found):
            left, right = pieces[(count - r + 1) % count], pieces[r - 1]
            more = needed(r, i, found)
            if more:
                left, right = after((left, right), *more)
            if r < half or i % 2 == 0:
                pieces[count - r] = lax.ppermute(left, axis, forward)
            if r < half or i % 2 == 1:
                pieces[r] = lax.ppermute(right, axis, backward)
    return [[pieces[r] for r in range(count)] for pieces in found]


def shards(observations, precisions, blocks, block_rows, block_cols, transition, prior):
    steps_here, width, size = transition.shape
    side = blocks.shape[2]
    count = lax.axis_size("state")
    blocks_of_time = lax.axis_size("tm")
    V, S, A = pltpu.VMEM, pltpu.SMEM, pl.ANY

    matrix = jax.ShapeDtypeStruct((size, size), BF16)
    slab = jax.ShapeDtypeStruct((width, size), BF16)
    rows = jax.ShapeDtypeStruct((16, size), BF16)
    steps = jax.ShapeDtypeStruct((steps_here, size), F32)
    row = jax.ShapeDtypeStruct((1, size), F32)
    whole = pltpu.VMEM((size, size), BF16)

    half = steps_here // 2
    pieces = observations.shape[1] // side
    packed = call(
        drive_kernel, jax.ShapeDtypeStruct((half * width + 16, size), BF16), [V] * 4 + [A],
        [
            pltpu.VMEM((pieces, steps_here, side), F32),
            pltpu.VMEM((16, size), F32),
            pltpu.SemaphoreType.DMA((half,)),
        ],
        flops=10 ** 7, moved=2 ** 21,
    )(block_rows, block_cols, (precisions * observations).astype(BF16), blocks, transition[half:])
    early, late = ring_rounds(
        [transition[:half].reshape(half * width, size), packed], "state",
        lambda r, i, found: (packed,) if (r, i) == (2, 0) else (),
    )
    two, slab2, second = call(
        functools.partial(two_kernel, count), (matrix, slab, matrix), [A] * count,
        [whole, pltpu.SemaphoreType.DMA((2 * count,))], flops=2 * size ** 3, moved=6 * size ** 2,
    )(*early)
    own, slab3, slab4, third, fourth, drive = call(
        functools.partial(four_kernel, count),
        (matrix, slab, slab, matrix, matrix, jax.ShapeDtypeStruct((16, size), F32)),
        [V] + [A] * count,
        [whole, pltpu.VMEM((count, 16, size), BF16), pltpu.SemaphoreType.DMA((3 * count,))],
        flops=4 * size ** 3, moved=8 * size ** 2,
    )(two, *late)
    pairs = [(i, i + 1) for i in range(0, blocks_of_time, 2)]
    other = lax.ppermute(own, "tm", pairs)
    locals_, own_term = call(
        local_kernel, (steps, rows), [V] * 4, flops=96 * size ** 2, moved=6 * size ** 2
    )(drive, second, third, fourth)
    other_term = lax.ppermute(own_term, "tm", pairs)

    chips = blocks_of_time // 2
    firsts = chips // 2
    longer = jax.ShapeDtypeStruct((size + 16, size), BF16)
    turned = call(
        pair_kernel, longer, [V] * 4, flops=2 * size ** 3, moved=6 * size ** 2
    )(own, own_term, other, other_term)
    before = lax.ppermute(turned, "tm", [(2 * c + 1, 2 * c + 3) for c in range(firsts, chips, 2)])

    begin = after(prior.reshape(1, size), turned)
    came = begin
    for turn in range(firsts):
        if turn < DIRECT:
            begin, value = call(
                functools.partial(direct_kernel, turn), (row, row), [V] * 6,
                flops=64 * size ** 2, moved=4 * size ** 2,
            )(begin, came, own, own_term, other, other_term)
        else:
            begin, value = call(
                functools.partial(hop_kernel, turn), (row, row), [V] * 3,
                flops=32 * size ** 2, moved=2 * size ** 2,
            )(begin, came, turned)
        came = lax.ppermute(value, "tm", [(2 * turn + 1, 2 * turn + (3 if turn + 1 < firsts else 5))])
        if turn == DIRECT:
            maps, terms = call(
                ready_kernel,
                (jax.ShapeDtypeStruct((size, steps_here * width), BF16), jax.ShapeDtypeStruct((steps_here, width), F32)),
                [V] * 8, flops=size ** 3, moved=4 * size ** 2,
            )(other, other_term, locals_, value, early[0], slab2, slab3, slab4)
        if turn == DIRECT + 1:
            came = after(came, maps)
    double = call(
        functools.partial(double_kernel, firsts), longer, [V, V], flops=2 * size ** 3, moved=6 * size ** 2
    )(before, turned)
    for chip in range(firsts + 1, chips, 2):
        begin, value = call(
            functools.partial(far_kernel, chip, chip == chips - 1), (row, row), [V] * 5,
            flops=64 * size ** 2, moved=4 * size ** 2,
        )(begin, came, value, before, double)
        if chip < chips - 1:
            came = lax.ppermute(value, "tm", [(2 * chip + 1, 2 * chip + 5)])
    handed = lax.ppermute(value, "tm", [(2 * c - 1, 2 * c + 1) for c in range(firsts, chips, 2)])
    begin = call(functools.partial(final_kernel, firsts), row, [V, V])(begin, handed)
    got = lax.ppermute(begin, "tm", [(b, a) for a, b in pairs])
    return call(
        out_kernel, jax.ShapeDtypeStruct((steps_here, width), F32), [V] * 4,
        flops=16 * size ** 2, moved=size ** 2,
    )(begin, got, maps, terms)


def solution(mesh):
    return jax.shard_map(
        shards,
        mesh=mesh,
        in_specs=(
            P("tm", None),
            P("tm", None),
            P("tm", "state", None, None),
            P("tm", "state"),
            P("tm", "state"),
            P("tm", "state", None),
            P(),
        ),
        out_specs=P("tm", "state"),
        check_vma=False,
    )
```

```python
import functools

import jax
import jax.numpy as jnp
from jax import lax
from jax.experimental import pallas as pl
from jax.experimental.pallas import tpu as pltpu
from jax.sharding import PartitionSpec as P

F32 = jnp.float32
BF16 = jnp.bfloat16
VMEM_LIMIT = 24 * 1024 * 1024
ROWS = 512


def three_parts(x):
    hi = x.astype(BF16).astype(F32)
    rest = x - hi
    mid = rest.astype(BF16).astype(F32)
    return hi, mid, rest - mid


def split_rows(x):
    hi, mid, lo = three_parts(x)
    row = lax.broadcasted_iota(jnp.int32, (16, x.shape[1]), 0)
    out = jnp.where(row == 0, hi, jnp.where(row == 1, mid, jnp.where(row == 2, lo, 0.0)))
    return out.astype(BF16)


def joined(rows):
    return jnp.sum(rows.astype(F32), axis=0, keepdims=True)


def times_t(x, *parts):
    left = split_rows(x)
    out = [
        joined(lax.dot_general(left, part, (((1,), (1,)), ((), ())), preferred_element_type=F32)) for part in parts
    ]
    return out[0] if len(out) == 1 else jnp.concatenate(out, axis=1)


def times(x, *parts):
    left = split_rows(x)
    return joined(product(left, *parts))


def product(left, *parts):
    rows = parts[0].shape[0]
    out = [
        jnp.dot(left[:, i * rows:(i + 1) * rows], part, preferred_element_type=F32) for i, part in enumerate(parts)
    ]
    return sum(out[1:], out[0])


def matmul(left_ref, right_ref, out_ref):
    def block(i, carry):
        at = pl.ds(pl.multiple_of(i * ROWS, ROWS), ROWS)
        out_ref[at, :] = jnp.dot(left_ref[at, :], right_ref[...], preferred_element_type=F32).astype(BF16)
        return carry

    lax.fori_loop(0, left_ref.shape[0] // ROWS, block, 0)


def core_here():
    return lax.rem(lax.axis_index("tm"), 2)


def chip_here():
    return lax.div(lax.axis_index("tm"), 2)


def drive_kernel(
    rows_ref, cols_ref, values_ref, blocks_ref, maps_ref, out_ref, weighted_ref, parts_ref, sems
):
    steps, count, side, _ = blocks_ref.shape
    later, width, size = maps_ref.shape
    copies = []
    for j in range(later):
        copies.append(pltpu.make_async_copy(maps_ref.at[j], out_ref.at[pl.ds(j * width, width), :], sems.at[j]))
        copies[j].start()
    weighted = values_ref[...].astype(F32)
    pieces = weighted_ref.shape[0]
    for r in range(pieces):
        weighted_ref[r] = weighted[:, r * side:(r + 1) * side]
    parts_ref[...] = jnp.zeros_like(parts_ref)
    piece = lax.broadcasted_iota(jnp.int32, (pieces, count), 0)
    column = lax.broadcasted_iota(jnp.int32, (size // side, count), 0)
    own = lax.broadcasted_iota(jnp.int32, (count, count * side), 0) == (
        lax.broadcasted_iota(jnp.int32, (count, count * side), 1) // side
    )
    for t in range(steps):
        chosen = (piece == rows_ref[t:t + 1, :]).astype(F32).astype(BF16)
        left = lax.dot_general(
            chosen, weighted_ref[:, t, :].astype(BF16), (((0,), (0,)), ((), ())), preferred_element_type=F32
        )
        left = jnp.concatenate([left] * count, axis=1)
        left = jnp.where(own, left, 0.0).astype(BF16)
        terms = jnp.dot(left, blocks_ref[t].reshape(count * side, side), preferred_element_type=F32)
        chosen = (column == cols_ref[t:t + 1, :]).astype(F32).astype(BF16)
        drive = sum(jnp.dot(chosen, part.astype(BF16), preferred_element_type=F32) for part in three_parts(terms))
        for i, part in enumerate(three_parts(drive)):
            for c in range(size // side):
                parts_ref[3 * t + i:3 * t + i + 1, c * side:(c + 1) * side] = part[c:c + 1, :]
    out_ref[later * width:, :] = parts_ref[...].astype(BF16)
    for copy in copies:
        copy.wait()


def fetched(count, place, pieces, j, whole_ref, sems, first):
    width = whole_ref.shape[0] // count
    copies = []
    for i, (r, piece) in enumerate(pieces):
        at = pl.multiple_of(lax.rem(place + r, count) * width, width)
        copy = pltpu.make_async_copy(
            piece.at[pl.ds(j * width, width), :], whole_ref.at[pl.ds(at, width), :], sems.at[first + i]
        )
        copy.start()
        copies.append(copy)
    return copies


def two_kernel(count, *refs):
    pieces, (two_ref, slab_ref, next_ref, one_ref, sems) = list(enumerate(refs[:count])), refs[count:]
    width = slab_ref.shape[0]
    place = lax.axis_index("state")
    ones = fetched(count, place, pieces, 0, one_ref, sems, 0)
    nexts = fetched(count, place, pieces, 1, next_ref, sems, count)
    for copy in ones + nexts:
        copy.wait()
    matmul(next_ref, one_ref, two_ref)
    slab_ref[...] = two_ref[pl.ds(pl.multiple_of(place * width, width), width), :]


def three_kernel(count, have, two_ref, *refs):
    pieces = list(zip(have, refs[:len(have)]))
    three_ref, third_ref, fourth_ref, sems = refs[len(have):]
    width = third_ref.shape[0] // count
    place = lax.axis_index("state")
    copies = fetched(count, place, pieces, 0, third_ref, sems, 0)
    copies += fetched(count, place, pieces, 1, fourth_ref, sems, len(have))
    for copy in copies:
        copy.wait()
    for r in have:
        at = pl.ds(pl.multiple_of(lax.rem(place + r, count) * width, width), width)
        three_ref[at, :] = jnp.dot(third_ref[at, :], two_ref[...], preferred_element_type=F32).astype(BF16)


def four_kernel(count, have, two_ref, threes_ref, thirds_ref, fourths_ref, *refs):
    missing = [(r, refs[r]) for r in range(count) if r not in have]
    four_ref, slab3_ref, slab4_ref, three_ref, third_ref, fourth_ref, drive_ref, parts_ref, sems = refs[count:]
    width = slab3_ref.shape[0]
    place = lax.axis_index("state")
    thirds = fetched(count, place, missing, 0, third_ref, sems, 0)
    fourths = fetched(count, place, missing, 1, fourth_ref, sems, len(missing))
    parts = []
    for r in range(count):
        at = 2 * len(missing) + r
        parts.append(pltpu.make_async_copy(refs[r].at[pl.ds(2 * width, 16), :], parts_ref.at[r], sems.at[at]))
        parts[r].start()
    for copy in thirds:
        copy.wait()
    for r, _ in missing:
        at = pl.ds(pl.multiple_of(lax.rem(place + r, count) * width, width), width)
        three_ref[at, :] = jnp.dot(third_ref[at, :], two_ref[...], preferred_element_type=F32).astype(BF16)
    for copy in fourths:
        copy.wait()
    matmul(fourth_ref, three_ref, four_ref)
    mine = pl.ds(pl.multiple_of(place * width, width), width)
    slab3_ref[...] = three_ref[mine, :]
    slab4_ref[...] = four_ref[mine, :]
    for copy in parts:
        copy.wait()
    drive_ref[...] = jnp.sum(parts_ref[...].astype(F32), axis=0)


def local_kernel(drive_ref, second_ref, third_ref, fourth_ref, locals_ref, term_ref):
    local = joined(drive_ref[0:3, :])
    locals_ref[0:1, :] = local
    for j, map_ref in enumerate((second_ref, third_ref, fourth_ref)):
        local = times_t(local, map_ref[...]) + joined(drive_ref[3 * j + 3:3 * j + 6, :])
        locals_ref[j + 1:j + 2, :] = local
    term_ref[...] = split_rows(local)


DIRECT = 3


def pair_kernel(half, own_ref, own_term_ref, other_ref, other_term_ref, turned_ref):
    rows = own_ref.shape[0] // 2
    at = slice(half * rows, (half + 1) * rows)

    @pl.when(jnp.logical_and(core_here() != 0, chip_here() >= DIRECT))
    def _():
        for i in range(2):
            out = jnp.dot(own_ref[i * rows:(i + 1) * rows, :], other_ref[:, at], preferred_element_type=F32)
            turned_ref[:rows, i * rows:(i + 1) * rows] = out.T.astype(BF16)
        if half == 1:
            term = times_t(joined(other_term_ref[...]), own_ref[...]) + joined(own_term_ref[...])
            turned_ref[rows:, :] = split_rows(term)


def applied(x, turned0_ref, turned1_ref):
    rows = turned0_ref.shape[0]
    return times(x, turned0_ref[...], turned1_ref[:rows, :]) + joined(turned1_ref[rows:, :])


def direct_kernel(turn, begin_ref, came_ref, own_ref, own_term_ref, other_ref, other_term_ref, held_ref, value_ref):
    held_ref[...] = begin_ref[...]
    value_ref[...] = begin_ref[...]

    @pl.when(lax.axis_index("tm") == 2 * turn + 1)
    def _():
        begin = came_ref[...]
        held_ref[...] = begin
        between = times_t(begin, other_ref[...]) + joined(other_term_ref[...])
        value_ref[...] = times_t(between, own_ref[...]) + joined(own_term_ref[...])


def hop_kernel(turn, begin_ref, came_ref, turned0_ref, turned1_ref, held_ref, value_ref):
    here = lax.axis_index("tm") == 2 * turn + 1

    @pl.when(here)
    def _():
        begin = came_ref[...]
        held_ref[...] = begin
        value_ref[...] = applied(begin, turned0_ref, turned1_ref)

    @pl.when(jnp.logical_not(here))
    def _():
        held_ref[...] = begin_ref[...]
        value_ref[...] = begin_ref[...]


def double_kernel(half, firsts, came_ref, turned0_ref, turned1_ref, double_ref):
    rows = turned0_ref.shape[0]
    chip = chip_here()

    @pl.when((core_here() != 0) & (chip > firsts) & (lax.rem(chip, 2) == 1) & (chip < 2 * firsts - 1))
    def _():
        double_ref[:rows, :] = product(came_ref[:rows, :], turned0_ref[...], turned1_ref[:rows, :]).astype(BF16)
        if half == 1:
            double_ref[rows:, :] = split_rows(applied(joined(came_ref[rows:, :]), turned0_ref, turned1_ref))


def far_kernel(
    chip, last, begin_ref, came_ref, before_ref, map0_ref, map1_ref, double0_ref, double1_ref, held_ref, value_ref
):
    here = lax.axis_index("tm") == 2 * chip + 1

    @pl.when(here)
    def _():
        if last:
            value_ref[...] = before_ref[...]
        else:
            value_ref[...] = applied(came_ref[...], double0_ref, double1_ref)
        held_ref[...] = applied(came_ref[...], map0_ref, map1_ref)

    @pl.when(jnp.logical_not(here))
    def _():
        held_ref[...] = begin_ref[...]
        value_ref[...] = before_ref[...]


def final_kernel(firsts, held_ref, handed_ref, begin_ref):
    chip = chip_here()
    handed = jnp.logical_and(chip >= firsts, lax.rem(chip, 2) == 0)
    begin_ref[...] = jnp.where(handed, handed_ref[...], held_ref[...])


def ready_kernel(other_ref, other_term_ref, locals_ref, after_ref, *refs):
    slabs, (maps_ref, terms_ref) = refs[:-2], refs[-2:]
    width, size = slabs[1].shape
    mine = pl.ds(pl.multiple_of(lax.axis_index("state") * width, width), width)

    @pl.when(core_here() == 0)
    def _():
        for j, slab_ref in enumerate(slabs):
            maps_ref[:, j * width:(j + 1) * width] = slab_ref[:width, :].astype(F32).T.astype(BF16)
            terms_ref[j:j + 1, :] = locals_ref[j:j + 1, mine]

    @pl.when(core_here() != 0)
    def _():
        for j, slab_ref in enumerate(slabs):
            at = slice(j * width, (j + 1) * width)
            out = jnp.dot(slab_ref[:width, :], other_ref[...], preferred_element_type=F32)
            maps_ref[:, at] = out.T.astype(BF16)
            term = times_t(joined(other_term_ref[...]), slab_ref[:width, :])
            terms_ref[j:j + 1, :] = term + locals_ref[j:j + 1, mine]


def out_kernel(begin_ref, got_ref, maps_ref, terms_ref, out_ref):
    steps, width = out_ref.shape
    begin = jnp.where(core_here() == 0, got_ref[...], begin_ref[...])
    row = times(begin, maps_ref[...])
    for j in range(steps):
        out_ref[j:j + 1, :] = row[:, j * width:(j + 1) * width] + terms_ref[j:j + 1, :]


def call(kernel, out_shape, spaces, scratch=(), flops=0, moved=0, aliases={}):
    return pl.pallas_call(
        kernel,
        out_shape=out_shape,
        in_specs=[pl.BlockSpec(memory_space=s) for s in spaces],
        out_specs=jax.tree.map(lambda _: pl.BlockSpec(memory_space=pltpu.VMEM), out_shape),
        scratch_shapes=list(scratch),
        input_output_aliases=aliases,
        compiler_params=pltpu.CompilerParams(vmem_limit_bytes=VMEM_LIMIT),
        cost_estimate=pl.CostEstimate(flops=flops, bytes_accessed=moved, transcendentals=0),
    )


def after(value, *needed):
    return lax.optimization_barrier((value, needed))[0]


def ring_rounds(parts, axis, needed):
    count = lax.axis_size(axis)
    forward = [(i, (i + 1) % count) for i in range(count)]
    backward = [((i + 1) % count, i) for i in range(count)]
    half = count // 2
    found = [{0: part} for part in parts]
    for r in range(1, half + 1):
        for i, pieces in enumerate(found):
            left, right = pieces[(count - r + 1) % count], pieces[r - 1]
            more = needed(r, i, found)
            if more:
                left, right = after((left, right), *more)
            if r < half or i % 2 == 0:
                pieces[count - r] = lax.ppermute(left, axis, forward)
            if r < half or i % 2 == 1:
                pieces[r] = lax.ppermute(right, axis, backward)
    return [[pieces[r] for r in range(count)] for pieces in found]


def shards(observations, precisions, blocks, block_rows, block_cols, transition, prior):
    steps_here, width, size = transition.shape
    side = blocks.shape[2]
    count = lax.axis_size("state")
    blocks_of_time = lax.axis_size("tm")
    V, S, A = pltpu.VMEM, pltpu.SMEM, pl.ANY

    matrix = jax.ShapeDtypeStruct((size, size), BF16)
    slab = jax.ShapeDtypeStruct((width, size), BF16)
    rows = jax.ShapeDtypeStruct((16, size), BF16)
    steps = jax.ShapeDtypeStruct((steps_here, size), F32)
    row = jax.ShapeDtypeStruct((1, size), F32)
    whole = pltpu.VMEM((size, size), BF16)

    half = steps_here // 2
    pieces = observations.shape[1] // side
    packed = call(
        drive_kernel, jax.ShapeDtypeStruct((half * width + 16, size), BF16), [V] * 4 + [A],
        [
            pltpu.VMEM((pieces, steps_here, side), F32),
            pltpu.VMEM((16, size), F32),
            pltpu.SemaphoreType.DMA((half,)),
        ],
        flops=10 ** 7, moved=2 ** 21,
    )(block_rows, block_cols, (precisions * observations).astype(BF16), blocks, transition[half:])
    early, late = ring_rounds(
        [transition[:half].reshape(half * width, size), packed], "state",
        lambda r, i, found: (packed,) if (r, i) == (2, 0) else (),
    )
    two, slab2, second = call(
        functools.partial(two_kernel, count), (matrix, slab, matrix), [A] * count,
        [whole, pltpu.SemaphoreType.DMA((2 * count,))], flops=2 * size ** 3, moved=6 * size ** 2,
    )(*early)
    have = [r for r in range(count) if r not in (count // 2, count // 2 + 1)]
    three, third, fourth = call(
        functools.partial(three_kernel, count, have), (matrix, matrix, matrix), [V] + [A] * len(have),
        [pltpu.SemaphoreType.DMA((2 * len(have),))], flops=2 * size ** 3, moved=6 * size ** 2,
    )(two, *[late[r] for r in have])
    own, slab3, slab4, _, third, fourth, drive = call(
        functools.partial(four_kernel, count, have),
        (matrix, slab, slab, matrix, matrix, matrix, jax.ShapeDtypeStruct((16, size), F32)),
        [V] * 4 + [A] * count,
        [pltpu.VMEM((count, 16, size), BF16), pltpu.SemaphoreType.DMA((3 * count,))],
        flops=2 * size ** 3, moved=6 * size ** 2, aliases={1: 3, 2: 4, 3: 5},
    )(two, three, third, fourth, *late)
    pairs = [(i, i + 1) for i in range(0, blocks_of_time, 2)]
    other = lax.ppermute(own, "tm", pairs)
    locals_, own_term = call(
        local_kernel, (steps, rows), [V] * 4, flops=96 * size ** 2, moved=6 * size ** 2
    )(drive, second, third, fourth)
    other_term = lax.ppermute(own_term, "tm", pairs)

    chips = blocks_of_time // 2
    firsts = chips // 2
    part = jax.ShapeDtypeStruct((size // 2, size), BF16)
    longer = jax.ShapeDtypeStruct((size // 2 + 16, size), BF16)
    blocks_here = (own, own_term, other, other_term)
    onward = [(2 * c + 1, 2 * c + 3) for c in range(firsts, chips, 2)]
    half_cost = dict(flops=size ** 3, moved=6 * size ** 2)
    turned0 = call(functools.partial(pair_kernel, 0), part, [V] * 4, **half_cost)(*blocks_here)
    before0 = lax.ppermute(turned0, "tm", onward)
    turned1 = call(functools.partial(pair_kernel, 1), longer, [V] * 4, **half_cost)(*blocks_here)
    before1 = lax.ppermute(turned1, "tm", onward)

    begin = after(prior.reshape(1, size), turned1)
    came = begin
    for turn in range(firsts):
        if turn < DIRECT:
            begin, value = call(
                functools.partial(direct_kernel, turn), (row, row), [V] * 6,
                flops=64 * size ** 2, moved=4 * size ** 2,
            )(begin, came, *blocks_here)
        else:
            begin, value = call(
                functools.partial(hop_kernel, turn), (row, row), [V] * 4,
                flops=32 * size ** 2, moved=2 * size ** 2,
            )(begin, came, turned0, turned1)
        came = lax.ppermute(value, "tm", [(2 * turn + 1, 2 * turn + (3 if turn + 1 < firsts else 5))])
        if turn == DIRECT:
            maps, terms = call(
                ready_kernel,
                (jax.ShapeDtypeStruct((size, steps_here * width), BF16), jax.ShapeDtypeStruct((steps_here, width), F32)),
                [V] * 8, flops=size ** 3, moved=4 * size ** 2,
            )(other, other_term, locals_, value, early[0], slab2, slab3, slab4)
        if turn == DIRECT + 1:
            came = after(came, maps)
    double0 = call(functools.partial(double_kernel, 0, firsts), part, [V] * 3, **half_cost)(before0, turned0, turned1)
    double1 = call(functools.partial(double_kernel, 1, firsts), longer, [V] * 3, **half_cost)(before1, turned0, turned1)
    for chip in range(firsts + 1, chips, 2):
        begin, value = call(
            functools.partial(far_kernel, chip, chip == chips - 1), (row, row), [V] * 7,
            flops=64 * size ** 2, moved=4 * size ** 2,
        )(begin, came, value, before0, before1, double0, double1)
        if chip < chips - 1:
            came = lax.ppermute(value, "tm", [(2 * chip + 1, 2 * chip + 5)])
    handed = lax.ppermute(value, "tm", [(2 * c - 1, 2 * c + 1) for c in range(firsts, chips, 2)])
    begin = call(functools.partial(final_kernel, firsts), row, [V, V])(begin, handed)
    got = lax.ppermute(begin, "tm", [(b, a) for a, b in pairs])
    return call(
        out_kernel, jax.ShapeDtypeStruct((steps_here, width), F32), [V] * 4,
        flops=16 * size ** 2, moved=size ** 2,
    )(begin, got, maps, terms)


def solution(mesh):
    return jax.shard_map(
        shards,
        mesh=mesh,
        in_specs=(
            P("tm", None),
            P("tm", None),
            P("tm", "state", None, None),
            P("tm", "state"),
            P("tm", "state"),
            P("tm", "state", None),
            P(),
        ),
        out_specs=P("tm", "state"),
        check_vma=False,
    )
```

```python
import functools

import jax
import jax.numpy as jnp
from jax import lax
from jax.experimental import pallas as pl
from jax.experimental.pallas import tpu as pltpu
from jax.sharding import PartitionSpec as P

F32 = jnp.float32
BF16 = jnp.bfloat16
VMEM_LIMIT = 24 * 1024 * 1024
ROWS = 512


def three_parts(x):
    hi = x.astype(BF16).astype(F32)
    rest = x - hi
    mid = rest.astype(BF16).astype(F32)
    return hi, mid, rest - mid


def split_rows(x):
    hi, mid, lo = three_parts(x)
    row = lax.broadcasted_iota(jnp.int32, (16, x.shape[1]), 0)
    out = jnp.where(row == 0, hi, jnp.where(row == 1, mid, jnp.where(row == 2, lo, 0.0)))
    return out.astype(BF16)


def joined(rows):
    return jnp.sum(rows.astype(F32), axis=0, keepdims=True)


def times_t(x, *parts):
    left = split_rows(x)
    out = [
        joined(lax.dot_general(left, part, (((1,), (1,)), ((), ())), preferred_element_type=F32)) for part in parts
    ]
    return out[0] if len(out) == 1 else jnp.concatenate(out, axis=1)


def times(x, *parts):
    left = split_rows(x)
    return joined(product(left, *parts))


def product(left, *parts):
    rows = parts[0].shape[0]
    out = [
        jnp.dot(left[:, i * rows:(i + 1) * rows], part, preferred_element_type=F32) for i, part in enumerate(parts)
    ]
    return sum(out[1:], out[0])


def matmul(left_ref, right_ref, out_ref):
    def block(i, carry):
        at = pl.ds(pl.multiple_of(i * ROWS, ROWS), ROWS)
        out_ref[at, :] = jnp.dot(left_ref[at, :], right_ref[...], preferred_element_type=F32).astype(BF16)
        return carry

    lax.fori_loop(0, left_ref.shape[0] // ROWS, block, 0)


def core_here():
    return lax.rem(lax.axis_index("tm"), 2)


def chip_here():
    return lax.div(lax.axis_index("tm"), 2)


def drive_kernel(
    rows_ref, cols_ref, values_ref, blocks_ref, maps_ref, out_ref, weighted_ref, parts_ref, sems
):
    steps, count, side, _ = blocks_ref.shape
    later, width, size = maps_ref.shape
    copies = []
    for j in range(later):
        copies.append(pltpu.make_async_copy(maps_ref.at[j], out_ref.at[pl.ds(j * width, width), :], sems.at[j]))
        copies[j].start()
    weighted = values_ref[...].astype(F32)
    pieces = weighted_ref.shape[0]
    for r in range(pieces):
        weighted_ref[r] = weighted[:, r * side:(r + 1) * side]
    parts_ref[...] = jnp.zeros_like(parts_ref)
    piece = lax.broadcasted_iota(jnp.int32, (pieces, count), 0)
    column = lax.broadcasted_iota(jnp.int32, (size // side, count), 0)
    own = lax.broadcasted_iota(jnp.int32, (count, count * side), 0) == (
        lax.broadcasted_iota(jnp.int32, (count, count * side), 1) // side
    )
    for t in range(steps):
        chosen = (piece == rows_ref[t:t + 1, :]).astype(F32).astype(BF16)
        left = lax.dot_general(
            chosen, weighted_ref[:, t, :].astype(BF16), (((0,), (0,)), ((), ())), preferred_element_type=F32
        )
        left = jnp.concatenate([left] * count, axis=1)
        left = jnp.where(own, left, 0.0).astype(BF16)
        terms = jnp.dot(left, blocks_ref[t].reshape(count * side, side), preferred_element_type=F32)
        chosen = (column == cols_ref[t:t + 1, :]).astype(F32).astype(BF16)
        drive = sum(jnp.dot(chosen, part.astype(BF16), preferred_element_type=F32) for part in three_parts(terms))
        for i, part in enumerate(three_parts(drive)):
            for c in range(size // side):
                parts_ref[3 * t + i:3 * t + i + 1, c * side:(c + 1) * side] = part[c:c + 1, :]
    out_ref[later * width:, :] = parts_ref[...].astype(BF16)
    for copy in copies:
        copy.wait()


def fetched(count, place, pieces, j, whole_ref, sems, first):
    width = whole_ref.shape[0] // count
    copies = []
    for i, (r, piece) in enumerate(pieces):
        at = pl.multiple_of(lax.rem(place + r, count) * width, width)
        copy = pltpu.make_async_copy(
            piece.at[pl.ds(j * width, width), :], whole_ref.at[pl.ds(at, width), :], sems.at[first + i]
        )
        copy.start()
        copies.append(copy)
    return copies


def two_kernel(count, *refs):
    pieces, (two_ref, slab_ref, next_ref, one_ref, sems) = list(enumerate(refs[:count])), refs[count:]
    width = slab_ref.shape[0]
    place = lax.axis_index("state")
    ones = fetched(count, place, pieces, 0, one_ref, sems, 0)
    nexts = fetched(count, place, pieces, 1, next_ref, sems, count)
    for copy in ones + nexts:
        copy.wait()
    matmul(next_ref, one_ref, two_ref)
    slab_ref[...] = two_ref[pl.ds(pl.multiple_of(place * width, width), width), :]


def three_kernel(count, have, two_ref, *refs):
    pieces = list(zip(have, refs[:len(have)]))
    three_ref, third_ref, fourth_ref, sems = refs[len(have):]
    width = third_ref.shape[0] // count
    place = lax.axis_index("state")
    copies = fetched(count, place, pieces, 0, third_ref, sems, 0)
    copies += fetched(count, place, pieces, 1, fourth_ref, sems, len(have))
    for copy in copies:
        copy.wait()
    for r in have:
        at = pl.ds(pl.multiple_of(lax.rem(place + r, count) * width, width), width)
        three_ref[at, :] = jnp.dot(third_ref[at, :], two_ref[...], preferred_element_type=F32).astype(BF16)


def four_kernel(count, have, two_ref, threes_ref, thirds_ref, fourths_ref, *refs):
    missing = [(r, refs[r]) for r in range(count) if r not in have]
    four_ref, slab3_ref, slab4_ref, three_ref, third_ref, fourth_ref, drive_ref, parts_ref, sems = refs[count:]
    width = slab3_ref.shape[0]
    place = lax.axis_index("state")
    thirds = fetched(count, place, missing, 0, third_ref, sems, 0)
    fourths = fetched(count, place, missing, 1, fourth_ref, sems, len(missing))
    parts = []
    for r in range(count):
        at = 2 * len(missing) + r
        parts.append(pltpu.make_async_copy(refs[r].at[pl.ds(2 * width, 16), :], parts_ref.at[r], sems.at[at]))
        parts[r].start()
    for copy in thirds:
        copy.wait()
    for r, _ in missing:
        at = pl.ds(pl.multiple_of(lax.rem(place + r, count) * width, width), width)
        three_ref[at, :] = jnp.dot(third_ref[at, :], two_ref[...], preferred_element_type=F32).astype(BF16)
    for copy in fourths:
        copy.wait()
    matmul(fourth_ref, three_ref, four_ref)
    mine = pl.ds(pl.multiple_of(place * width, width), width)
    slab3_ref[...] = three_ref[mine, :]
    slab4_ref[...] = four_ref[mine, :]
    for copy in parts:
        copy.wait()
    drive_ref[...] = jnp.sum(parts_ref[...].astype(F32), axis=0)


def local_kernel(drive_ref, prior_ref, second_ref, third_ref, fourth_ref, four_ref, locals_ref, term_ref, mean_ref):
    local = joined(drive_ref[0:3, :])
    locals_ref[0:1, :] = local
    for j, map_ref in enumerate((second_ref, third_ref, fourth_ref)):
        local = times_t(local, map_ref[...]) + joined(drive_ref[3 * j + 3:3 * j + 6, :])
        locals_ref[j + 1:j + 2, :] = local
    term_ref[...] = split_rows(local)
    mean_ref[...] = local

    @pl.when(lax.axis_index("tm") == 0)
    def _():
        mean_ref[...] = times_t(prior_ref[...], four_ref[...]) + local


def first_kernel(mean_ref, own_ref, term_ref, value_ref):
    value_ref[...] = mean_ref[...]

    @pl.when(lax.axis_index("tm") == 1)
    def _():
        value_ref[...] = times_t(mean_ref[...], own_ref[...]) + joined(term_ref[...])


DIRECT = 3


def pair_kernel(half, own_ref, own_term_ref, other_ref, other_term_ref, turned_ref):
    rows = own_ref.shape[0] // 2
    at = slice(half * rows, (half + 1) * rows)

    @pl.when(jnp.logical_and(core_here() != 0, chip_here() >= DIRECT))
    def _():
        for i in range(2):
            out = jnp.dot(own_ref[i * rows:(i + 1) * rows, :], other_ref[:, at], preferred_element_type=F32)
            turned_ref[:rows, i * rows:(i + 1) * rows] = out.T.astype(BF16)
        if half == 1:
            term = times_t(joined(other_term_ref[...]), own_ref[...]) + joined(own_term_ref[...])
            turned_ref[rows:, :] = split_rows(term)


def applied(x, turned0_ref, turned1_ref):
    rows = turned0_ref.shape[0]
    return times(x, turned0_ref[...], turned1_ref[:rows, :]) + joined(turned1_ref[rows:, :])


def direct_kernel(turn, begin_ref, came_ref, own_ref, own_term_ref, other_ref, other_term_ref, held_ref, value_ref):
    held_ref[...] = begin_ref[...]
    value_ref[...] = begin_ref[...]

    @pl.when(lax.axis_index("tm") == 2 * turn + 1)
    def _():
        begin = came_ref[...]
        held_ref[...] = begin
        between = times_t(begin, other_ref[...]) + joined(other_term_ref[...])
        value_ref[...] = times_t(between, own_ref[...]) + joined(own_term_ref[...])


def hop_kernel(turn, begin_ref, came_ref, turned0_ref, turned1_ref, held_ref, value_ref):
    here = lax.axis_index("tm") == 2 * turn + 1

    @pl.when(here)
    def _():
        begin = came_ref[...]
        held_ref[...] = begin
        value_ref[...] = applied(begin, turned0_ref, turned1_ref)

    @pl.when(jnp.logical_not(here))
    def _():
        held_ref[...] = begin_ref[...]
        value_ref[...] = begin_ref[...]


def far_kernel(
    chip, begin_ref, came_ref, before_ref, map0_ref, map1_ref, turned0_ref, turned1_ref, held_ref, value_ref
):
    here = lax.axis_index("tm") == 2 * chip + 1

    @pl.when(here)
    def _():
        begin = applied(came_ref[...], map0_ref, map1_ref)
        held_ref[...] = begin
        value_ref[...] = applied(begin, turned0_ref, turned1_ref)

    @pl.when(jnp.logical_not(here))
    def _():
        held_ref[...] = begin_ref[...]
        value_ref[...] = before_ref[...]


def final_kernel(firsts, held_ref, handed_ref, begin_ref):
    chip = chip_here()
    handed = jnp.logical_and(chip >= firsts, lax.rem(chip, 2) == 0)
    begin_ref[...] = jnp.where(handed, handed_ref[...], held_ref[...])


def ready_kernel(other_ref, other_term_ref, locals_ref, after_ref, *refs):
    slabs, (maps_ref, terms_ref) = refs[:-2], refs[-2:]
    width, size = slabs[1].shape
    mine = pl.ds(pl.multiple_of(lax.axis_index("state") * width, width), width)

    plain = jnp.logical_or(core_here() == 0, chip_here() == 0)

    @pl.when(plain)
    def _():
        for j, slab_ref in enumerate(slabs):
            maps_ref[:, j * width:(j + 1) * width] = slab_ref[:width, :].astype(F32).T.astype(BF16)
            terms_ref[j:j + 1, :] = locals_ref[j:j + 1, mine]

    @pl.when(jnp.logical_not(plain))
    def _():
        for j, slab_ref in enumerate(slabs):
            at = slice(j * width, (j + 1) * width)
            out = jnp.dot(slab_ref[:width, :], other_ref[...], preferred_element_type=F32)
            maps_ref[:, at] = out.T.astype(BF16)
            term = times_t(joined(other_term_ref[...]), slab_ref[:width, :])
            terms_ref[j:j + 1, :] = term + locals_ref[j:j + 1, mine]


def out_kernel(prior_ref, mean_ref, begin_ref, got_ref, maps_ref, terms_ref, out_ref):
    steps, width = out_ref.shape
    first = jnp.where(core_here() == 0, prior_ref[...], mean_ref[...])
    begin = jnp.where(core_here() == 0, got_ref[...], begin_ref[...])
    begin = jnp.where(chip_here() == 0, first, begin)
    row = times(begin, maps_ref[...])
    for j in range(steps):
        out_ref[j:j + 1, :] = row[:, j * width:(j + 1) * width] + terms_ref[j:j + 1, :]


def call(kernel, out_shape, spaces, scratch=(), flops=0, moved=0, aliases={}):
    return pl.pallas_call(
        kernel,
        out_shape=out_shape,
        in_specs=[pl.BlockSpec(memory_space=s) for s in spaces],
        out_specs=jax.tree.map(lambda _: pl.BlockSpec(memory_space=pltpu.VMEM), out_shape),
        scratch_shapes=list(scratch),
        input_output_aliases=aliases,
        compiler_params=pltpu.CompilerParams(vmem_limit_bytes=VMEM_LIMIT),
        cost_estimate=pl.CostEstimate(flops=flops, bytes_accessed=moved, transcendentals=0),
    )


def after(value, *needed):
    return lax.optimization_barrier((value, needed))[0]


def ring_rounds(parts, axis, needed):
    count = lax.axis_size(axis)
    forward = [(i, (i + 1) % count) for i in range(count)]
    backward = [((i + 1) % count, i) for i in range(count)]
    half = count // 2
    found = [{0: part} for part in parts]
    for r in range(1, half + 1):
        for i, pieces in enumerate(found):
            left, right = pieces[(count - r + 1) % count], pieces[r - 1]
            more = needed(r, i, found)
            if more:
                left, right = after((left, right), *more)
            if r < half or i % 2 == 0:
                pieces[count - r] = lax.ppermute(left, axis, forward)
            if r < half or i % 2 == 1:
                pieces[r] = lax.ppermute(right, axis, backward)
    return [[pieces[r] for r in range(count)] for pieces in found]


def shards(observations, precisions, blocks, block_rows, block_cols, transition, prior):
    steps_here, width, size = transition.shape
    side = blocks.shape[2]
    count = lax.axis_size("state")
    blocks_of_time = lax.axis_size("tm")
    V, S, A = pltpu.VMEM, pltpu.SMEM, pl.ANY

    matrix = jax.ShapeDtypeStruct((size, size), BF16)
    slab = jax.ShapeDtypeStruct((width, size), BF16)
    rows = jax.ShapeDtypeStruct((16, size), BF16)
    steps = jax.ShapeDtypeStruct((steps_here, size), F32)
    row = jax.ShapeDtypeStruct((1, size), F32)
    whole = pltpu.VMEM((size, size), BF16)

    half = steps_here // 2
    pieces = observations.shape[1] // side
    packed = call(
        drive_kernel, jax.ShapeDtypeStruct((half * width + 16, size), BF16), [V] * 4 + [A],
        [
            pltpu.VMEM((pieces, steps_here, side), F32),
            pltpu.VMEM((16, size), F32),
            pltpu.SemaphoreType.DMA((half,)),
        ],
        flops=10 ** 7, moved=2 ** 21,
    )(block_rows, block_cols, (precisions * observations).astype(BF16), blocks, transition[half:])
    early, late = ring_rounds(
        [transition[:half].reshape(half * width, size), packed], "state",
        lambda r, i, found: (packed,) if (r, i) == (2, 0) else (),
    )
    two, slab2, second = call(
        functools.partial(two_kernel, count), (matrix, slab, matrix), [A] * count,
        [whole, pltpu.SemaphoreType.DMA((2 * count,))], flops=2 * size ** 3, moved=6 * size ** 2,
    )(*early)
    have = [r for r in range(count) if r not in (count // 2, count // 2 + 1)]
    three, third, fourth = call(
        functools.partial(three_kernel, count, have), (matrix, matrix, matrix), [V] + [A] * len(have),
        [pltpu.SemaphoreType.DMA((2 * len(have),))], flops=2 * size ** 3, moved=6 * size ** 2,
    )(two, *[late[r] for r in have])
    own, slab3, slab4, _, third, fourth, drive = call(
        functools.partial(four_kernel, count, have),
        (matrix, slab, slab, matrix, matrix, matrix, jax.ShapeDtypeStruct((16, size), F32)),
        [V] * 4 + [A] * count,
        [pltpu.VMEM((count, 16, size), BF16), pltpu.SemaphoreType.DMA((3 * count,))],
        flops=2 * size ** 3, moved=6 * size ** 2, aliases={1: 3, 2: 4, 3: 5},
    )(two, three, third, fourth, *late)
    pairs = [(i, i + 1) for i in range(0, blocks_of_time, 2)]
    other = lax.ppermute(own, "tm", pairs[1:])
    start = prior.reshape(1, size)
    locals_, own_term, mean = call(
        local_kernel, (steps, rows, row), [V] * 6, flops=128 * size ** 2, moved=8 * size ** 2
    )(drive, start, second, third, fourth, own)
    mean = lax.ppermute(mean, "tm", pairs[:1])
    other_term = lax.ppermute(own_term, "tm", pairs[1:])
    value = call(first_kernel, row, [V] * 3, flops=32 * size ** 2, moved=2 * size ** 2)(mean, own, own_term)
    came = lax.ppermute(value, "tm", [(1, 3)])

    chips = blocks_of_time // 2
    firsts = chips // 2
    part = jax.ShapeDtypeStruct((size // 2, size), BF16)
    longer = jax.ShapeDtypeStruct((size // 2 + 16, size), BF16)
    blocks_here = (own, own_term, other, other_term)
    pair_blocks = after(blocks_here, value)
    onward = [(2 * c + 1, 2 * c + 3) for c in range(firsts, chips, 2)]
    half_cost = dict(flops=size ** 3, moved=6 * size ** 2)
    turned0 = call(functools.partial(pair_kernel, 0), part, [V] * 4, **half_cost)(*pair_blocks)
    before0 = lax.ppermute(turned0, "tm", onward)
    turned1 = call(functools.partial(pair_kernel, 1), longer, [V] * 4, **half_cost)(*pair_blocks)
    before1 = lax.ppermute(turned1, "tm", onward)

    begin = start
    for turn in range(1, firsts):
        if turn < DIRECT:
            begin, value = call(
                functools.partial(direct_kernel, turn), (row, row), [V] * 6,
                flops=64 * size ** 2, moved=4 * size ** 2,
            )(begin, came, *blocks_here)
        else:
            begin, value = call(
                functools.partial(hop_kernel, turn), (row, row), [V] * 4,
                flops=32 * size ** 2, moved=2 * size ** 2,
            )(begin, came, turned0, turned1)
        came = lax.ppermute(value, "tm", [(2 * turn + 1, 2 * turn + (3 if turn + 1 < firsts else 5))])
        if turn == DIRECT:
            maps, terms = call(
                ready_kernel,
                (jax.ShapeDtypeStruct((size, steps_here * width), BF16), jax.ShapeDtypeStruct((steps_here, width), F32)),
                [V] * 8, flops=size ** 3, moved=4 * size ** 2,
            )(other, other_term, locals_, value, early[0], slab2, slab3, slab4)
        if turn == DIRECT + 1:
            came = after(came, maps)
    for chip in range(firsts + 1, chips, 2):
        begin, value = call(
            functools.partial(far_kernel, chip), (row, row), [V] * 7,
            flops=64 * size ** 2, moved=4 * size ** 2,
        )(begin, came, value, before0, before1, turned0, turned1)
        if chip < chips - 1:
            came = lax.ppermute(value, "tm", [(2 * chip + 1, 2 * chip + 5)])
    handed = lax.ppermute(value, "tm", [(2 * c - 1, 2 * c + 1) for c in range(firsts, chips, 2)])
    begin = call(functools.partial(final_kernel, firsts), row, [V, V])(begin, handed)
    got = lax.ppermute(begin, "tm", [(b, a) for a, b in pairs])
    return call(
        out_kernel, jax.ShapeDtypeStruct((steps_here, width), F32), [V] * 6,
        flops=16 * size ** 2, moved=size ** 2,
    )(start, mean, begin, got, maps, terms)


def solution(mesh):
    return jax.shard_map(
        shards,
        mesh=mesh,
        in_specs=(
            P("tm", None),
            P("tm", None),
            P("tm", "state", None, None),
            P("tm", "state"),
            P("tm", "state"),
            P("tm", "state", None),
            P(),
        ),
        out_specs=P("tm", "state"),
        check_vma=False,
    )
```

```python
import functools

import jax
import jax.numpy as jnp
from jax import lax
from jax.experimental import pallas as pl
from jax.experimental.pallas import tpu as pltpu
from jax.sharding import PartitionSpec as P

F32 = jnp.float32
BF16 = jnp.bfloat16
VMEM_LIMIT = 24 * 1024 * 1024
ROWS = 512


def three_parts(x):
    hi = x.astype(BF16).astype(F32)
    rest = x - hi
    mid = rest.astype(BF16).astype(F32)
    return hi, mid, rest - mid


def split_rows(x):
    hi, mid, lo = three_parts(x)
    row = lax.broadcasted_iota(jnp.int32, (16, x.shape[1]), 0)
    out = jnp.where(row == 0, hi, jnp.where(row == 1, mid, jnp.where(row == 2, lo, 0.0)))
    return out.astype(BF16)


def joined(rows):
    return jnp.sum(rows.astype(F32), axis=0, keepdims=True)


def times_t(x, *parts):
    left = split_rows(x)
    out = [
        joined(lax.dot_general(left, part, (((1,), (1,)), ((), ())), preferred_element_type=F32)) for part in parts
    ]
    return out[0] if len(out) == 1 else jnp.concatenate(out, axis=1)


def times(x, *parts):
    left = split_rows(x)
    return joined(product(left, *parts))


def product(left, *parts):
    rows = parts[0].shape[0]
    out = [
        jnp.dot(left[:, i * rows:(i + 1) * rows], part, preferred_element_type=F32) for i, part in enumerate(parts)
    ]
    return sum(out[1:], out[0])


def matmul(left_ref, right_ref, out_ref):
    def block(i, carry):
        at = pl.ds(pl.multiple_of(i * ROWS, ROWS), ROWS)
        out_ref[at, :] = jnp.dot(left_ref[at, :], right_ref[...], preferred_element_type=F32).astype(BF16)
        return carry

    lax.fori_loop(0, left_ref.shape[0] // ROWS, block, 0)


def core_here():
    return lax.rem(lax.axis_index("tm"), 2)


def chip_here():
    return lax.div(lax.axis_index("tm"), 2)


def drive_kernel(
    rows_ref, cols_ref, values_ref, blocks_ref, maps_ref, out_ref, weighted_ref, parts_ref, sems
):
    steps, count, side, _ = blocks_ref.shape
    later, width, size = maps_ref.shape
    copies = []
    for j in range(later):
        copies.append(pltpu.make_async_copy(maps_ref.at[j], out_ref.at[pl.ds(j * width, width), :], sems.at[j]))
        copies[j].start()
    weighted = values_ref[...].astype(F32)
    pieces = weighted_ref.shape[0]
    for r in range(pieces):
        weighted_ref[r] = weighted[:, r * side:(r + 1) * side]
    parts_ref[...] = jnp.zeros_like(parts_ref)
    piece = lax.broadcasted_iota(jnp.int32, (pieces, count), 0)
    column = lax.broadcasted_iota(jnp.int32, (size // side, count), 0)
    own = lax.broadcasted_iota(jnp.int32, (count, count * side), 0) == (
        lax.broadcasted_iota(jnp.int32, (count, count * side), 1) // side
    )
    for t in range(steps):
        chosen = (piece == rows_ref[t:t + 1, :]).astype(F32).astype(BF16)
        left = lax.dot_general(
            chosen, weighted_ref[:, t, :].astype(BF16), (((0,), (0,)), ((), ())), preferred_element_type=F32
        )
        left = jnp.concatenate([left] * count, axis=1)
        left = jnp.where(own, left, 0.0).astype(BF16)
        terms = jnp.dot(left, blocks_ref[t].reshape(count * side, side), preferred_element_type=F32)
        chosen = (column == cols_ref[t:t + 1, :]).astype(F32).astype(BF16)
        drive = sum(jnp.dot(chosen, part.astype(BF16), preferred_element_type=F32) for part in three_parts(terms))
        for i, part in enumerate(three_parts(drive)):
            for c in range(size // side):
                parts_ref[3 * t + i:3 * t + i + 1, c * side:(c + 1) * side] = part[c:c + 1, :]
    out_ref[later * width:, :] = parts_ref[...].astype(BF16)
    for copy in copies:
        copy.wait()


def fetched(count, place, pieces, j, whole_ref, sems, first):
    width = whole_ref.shape[0] // count
    copies = []
    for i, (r, piece) in enumerate(pieces):
        at = pl.multiple_of(lax.rem(place + r, count) * width, width)
        copy = pltpu.make_async_copy(
            piece.at[pl.ds(j * width, width), :], whole_ref.at[pl.ds(at, width), :], sems.at[first + i]
        )
        copy.start()
        copies.append(copy)
    return copies


def two_kernel(count, *refs):
    pieces, (two_ref, slab_ref, next_ref, one_ref, sems) = list(enumerate(refs[:count])), refs[count:]
    width = slab_ref.shape[0]
    place = lax.axis_index("state")
    ones = fetched(count, place, pieces, 0, one_ref, sems, 0)
    nexts = fetched(count, place, pieces, 1, next_ref, sems, count)
    for copy in ones + nexts:
        copy.wait()
    matmul(next_ref, one_ref, two_ref)
    slab_ref[...] = two_ref[pl.ds(pl.multiple_of(place * width, width), width), :]


def three_kernel(count, have, two_ref, *refs):
    pieces = list(zip(have, refs[:len(have)]))
    three_ref, third_ref, fourth_ref, sems = refs[len(have):]
    width = third_ref.shape[0] // count
    place = lax.axis_index("state")
    copies = fetched(count, place, pieces, 0, third_ref, sems, 0)
    copies += fetched(count, place, pieces, 1, fourth_ref, sems, len(have))
    for copy in copies:
        copy.wait()
    for r in have:
        at = pl.ds(pl.multiple_of(lax.rem(place + r, count) * width, width), width)
        three_ref[at, :] = jnp.dot(third_ref[at, :], two_ref[...], preferred_element_type=F32).astype(BF16)


def four_kernel(count, have, two_ref, threes_ref, thirds_ref, fourths_ref, *refs):
    missing = [(r, refs[r]) for r in range(count) if r not in have]
    four_ref, slab3_ref, slab4_ref, three_ref, third_ref, fourth_ref, drive_ref, parts_ref, sems = refs[count:]
    width = slab3_ref.shape[0]
    place = lax.axis_index("state")
    thirds = fetched(count, place, missing, 0, third_ref, sems, 0)
    fourths = fetched(count, place, missing, 1, fourth_ref, sems, len(missing))
    parts = []
    for r in range(count):
        at = 2 * len(missing) + r
        parts.append(pltpu.make_async_copy(refs[r].at[pl.ds(2 * width, 16), :], parts_ref.at[r], sems.at[at]))
        parts[r].start()
    for copy in thirds:
        copy.wait()
    for r, _ in missing:
        at = pl.ds(pl.multiple_of(lax.rem(place + r, count) * width, width), width)
        three_ref[at, :] = jnp.dot(third_ref[at, :], two_ref[...], preferred_element_type=F32).astype(BF16)
    for copy in fourths:
        copy.wait()
    matmul(fourth_ref, three_ref, four_ref)
    mine = pl.ds(pl.multiple_of(place * width, width), width)
    slab3_ref[...] = three_ref[mine, :]
    slab4_ref[...] = four_ref[mine, :]
    for copy in parts:
        copy.wait()
    drive_ref[...] = jnp.sum(parts_ref[...].astype(F32), axis=0)


def local_kernel(drive_ref, second_ref, third_ref, fourth_ref, locals_ref, term_ref):
    local = joined(drive_ref[0:3, :])
    locals_ref[0:1, :] = local
    for j, map_ref in enumerate((second_ref, third_ref, fourth_ref)):
        local = times_t(local, map_ref[...]) + joined(drive_ref[3 * j + 3:3 * j + 6, :])
        locals_ref[j + 1:j + 2, :] = local
    term_ref[...] = split_rows(local)


DIRECT = 2


def pair_kernel(half, own_ref, own_term_ref, other_ref, other_term_ref, turned_ref):
    rows = own_ref.shape[0] // 2
    at = slice(half * rows, (half + 1) * rows)

    @pl.when(jnp.logical_and(core_here() != 0, chip_here() >= DIRECT))
    def _():
        for i in range(2):
            out = jnp.dot(own_ref[i * rows:(i + 1) * rows, :], other_ref[:, at], preferred_element_type=F32)
            turned_ref[:rows, i * rows:(i + 1) * rows] = out.T.astype(BF16)
        if half == 1:
            term = times_t(joined(other_term_ref[...]), own_ref[...]) + joined(own_term_ref[...])
            turned_ref[rows:, :] = split_rows(term)


def applied(x, turned0_ref, turned1_ref):
    rows = turned0_ref.shape[0]
    return times(x, turned0_ref[...], turned1_ref[:rows, :]) + joined(turned1_ref[rows:, :])


def direct_kernel(turn, begin_ref, came_ref, own_ref, own_term_ref, other_ref, other_term_ref, held_ref, value_ref):
    held_ref[...] = begin_ref[...]
    value_ref[...] = begin_ref[...]

    @pl.when(lax.axis_index("tm") == 2 * turn + 1)
    def _():
        begin = came_ref[...]
        held_ref[...] = begin
        between = times_t(begin, other_ref[...]) + joined(other_term_ref[...])
        value_ref[...] = times_t(between, own_ref[...]) + joined(own_term_ref[...])


def hop_kernel(turn, begin_ref, came_ref, turned0_ref, turned1_ref, held_ref, value_ref):
    here = lax.axis_index("tm") == 2 * turn + 1

    @pl.when(here)
    def _():
        begin = came_ref[...]
        held_ref[...] = begin
        value_ref[...] = applied(begin, turned0_ref, turned1_ref)

    @pl.when(jnp.logical_not(here))
    def _():
        held_ref[...] = begin_ref[...]
        value_ref[...] = begin_ref[...]


def double_kernel(half, firsts, came_ref, turned0_ref, turned1_ref, double_ref):
    rows = turned0_ref.shape[0]
    chip = chip_here()

    @pl.when((core_here() != 0) & (chip > firsts) & (lax.rem(chip, 2) == 1) & (chip < 2 * firsts - 1))
    def _():
        double_ref[:rows, :] = product(came_ref[:rows, :], turned0_ref[...], turned1_ref[:rows, :]).astype(BF16)
        if half == 1:
            double_ref[rows:, :] = split_rows(applied(joined(came_ref[rows:, :]), turned0_ref, turned1_ref))


def far_kernel(chip, came_ref, before_ref, double0_ref, double1_ref, value_ref):
    here = lax.axis_index("tm") == 2 * chip + 1

    @pl.when(here)
    def _():
        value_ref[...] = applied(came_ref[...], double0_ref, double1_ref)

    @pl.when(jnp.logical_not(here))
    def _():
        value_ref[...] = before_ref[...]


def final_kernel(firsts, held_ref, handed_ref, map0_ref, map1_ref, *refs):
    cames, begin_ref = refs[:-1], refs[-1]
    chip = chip_here()
    handed = jnp.logical_and(chip >= firsts, lax.rem(chip, 2) == 0)
    begin_ref[...] = jnp.where(handed, handed_ref[...], held_ref[...])
    for i, came_ref in enumerate(cames):
        @pl.when(lax.axis_index("tm") == 2 * (firsts + 1 + 2 * i) + 1)
        def _():
            begin_ref[...] = applied(came_ref[...], map0_ref, map1_ref)


def ready_kernel(other_ref, other_term_ref, locals_ref, after_ref, *refs):
    slabs, (maps_ref, terms_ref) = refs[:-2], refs[-2:]
    width, size = slabs[1].shape
    mine = pl.ds(pl.multiple_of(lax.axis_index("state") * width, width), width)

    @pl.when(core_here() == 0)
    def _():
        for j, slab_ref in enumerate(slabs):
            maps_ref[:, j * width:(j + 1) * width] = slab_ref[:width, :].astype(F32).T.astype(BF16)
            terms_ref[j:j + 1, :] = locals_ref[j:j + 1, mine]

    @pl.when(core_here() != 0)
    def _():
        for j, slab_ref in enumerate(slabs):
            at = slice(j * width, (j + 1) * width)
            out = jnp.dot(slab_ref[:width, :], other_ref[...], preferred_element_type=F32)
            maps_ref[:, at] = out.T.astype(BF16)
            term = times_t(joined(other_term_ref[...]), slab_ref[:width, :])
            terms_ref[j:j + 1, :] = term + locals_ref[j:j + 1, mine]


def out_kernel(begin_ref, got_ref, maps_ref, terms_ref, out_ref):
    steps, width = out_ref.shape
    begin = jnp.where(core_here() == 0, got_ref[...], begin_ref[...])
    row = times(begin, maps_ref[...])
    for j in range(steps):
        out_ref[j:j + 1, :] = row[:, j * width:(j + 1) * width] + terms_ref[j:j + 1, :]


def call(kernel, out_shape, spaces, scratch=(), flops=0, moved=0, aliases={}):
    return pl.pallas_call(
        kernel,
        out_shape=out_shape,
        in_specs=[pl.BlockSpec(memory_space=s) for s in spaces],
        out_specs=jax.tree.map(lambda _: pl.BlockSpec(memory_space=pltpu.VMEM), out_shape),
        scratch_shapes=list(scratch),
        input_output_aliases=aliases,
        compiler_params=pltpu.CompilerParams(vmem_limit_bytes=VMEM_LIMIT),
        cost_estimate=pl.CostEstimate(flops=flops, bytes_accessed=moved, transcendentals=0),
    )


def after(value, *needed):
    return lax.optimization_barrier((value, needed))[0]


def ring_rounds(parts, axis, needed):
    count = lax.axis_size(axis)
    forward = [(i, (i + 1) % count) for i in range(count)]
    backward = [((i + 1) % count, i) for i in range(count)]
    half = count // 2
    found = [{0: part} for part in parts]
    for r in range(1, half + 1):
        for i, pieces in enumerate(found):
            left, right = pieces[(count - r + 1) % count], pieces[r - 1]
            more = needed(r, i, found)
            if more:
                left, right = after((left, right), *more)
            if r < half or i % 2 == 0:
                pieces[count - r] = lax.ppermute(left, axis, forward)
            if r < half or i % 2 == 1:
                pieces[r] = lax.ppermute(right, axis, backward)
    return [[pieces[r] for r in range(count)] for pieces in found]


def shards(observations, precisions, blocks, block_rows, block_cols, transition, prior):
    steps_here, width, size = transition.shape
    side = blocks.shape[2]
    count = lax.axis_size("state")
    blocks_of_time = lax.axis_size("tm")
    V, S, A = pltpu.VMEM, pltpu.SMEM, pl.ANY

    matrix = jax.ShapeDtypeStruct((size, size), BF16)
    slab = jax.ShapeDtypeStruct((width, size), BF16)
    rows = jax.ShapeDtypeStruct((16, size), BF16)
    steps = jax.ShapeDtypeStruct((steps_here, size), F32)
    row = jax.ShapeDtypeStruct((1, size), F32)
    whole = pltpu.VMEM((size, size), BF16)

    half = steps_here // 2
    pieces = observations.shape[1] // side
    packed = call(
        drive_kernel, jax.ShapeDtypeStruct((half * width + 16, size), BF16), [V] * 4 + [A],
        [
            pltpu.VMEM((pieces, steps_here, side), F32),
            pltpu.VMEM((16, size), F32),
            pltpu.SemaphoreType.DMA((half,)),
        ],
        flops=10 ** 7, moved=2 ** 21,
    )(block_rows, block_cols, (precisions * observations).astype(BF16), blocks, transition[half:])
    early, late = ring_rounds(
        [transition[:half].reshape(half * width, size), packed], "state",
        lambda r, i, found: (packed,) if (r, i) == (2, 0) else (),
    )
    two, slab2, second = call(
        functools.partial(two_kernel, count), (matrix, slab, matrix), [A] * count,
        [whole, pltpu.SemaphoreType.DMA((2 * count,))], flops=2 * size ** 3, moved=6 * size ** 2,
    )(*early)
    have = [r for r in range(count) if r not in (count // 2, count // 2 + 1)]
    three, third, fourth = call(
        functools.partial(three_kernel, count, have), (matrix, matrix, matrix), [V] + [A] * len(have),
        [pltpu.SemaphoreType.DMA((2 * len(have),))], flops=2 * size ** 3, moved=6 * size ** 2,
    )(two, *[late[r] for r in have])
    own, slab3, slab4, _, third, fourth, drive = call(
        functools.partial(four_kernel, count, have),
        (matrix, slab, slab, matrix, matrix, matrix, jax.ShapeDtypeStruct((16, size), F32)),
        [V] * 4 + [A] * count,
        [pltpu.VMEM((count, 16, size), BF16), pltpu.SemaphoreType.DMA((3 * count,))],
        flops=2 * size ** 3, moved=6 * size ** 2, aliases={1: 3, 2: 4, 3: 5},
    )(two, three, third, fourth, *late)
    pairs = [(i, i + 1) for i in range(0, blocks_of_time, 2)]
    other = lax.ppermute(own, "tm", pairs)
    locals_, own_term = call(
        local_kernel, (steps, rows), [V] * 4, flops=96 * size ** 2, moved=6 * size ** 2
    )(drive, second, third, fourth)
    other_term = lax.ppermute(own_term, "tm", pairs)

    chips = blocks_of_time // 2
    firsts = chips // 2
    part = jax.ShapeDtypeStruct((size // 2, size), BF16)
    longer = jax.ShapeDtypeStruct((size // 2 + 16, size), BF16)
    blocks_here = (own, own_term, other, other_term)
    onward = [(2 * c + 1, 2 * c + 3) for c in range(firsts, chips, 2)]
    half_cost = dict(flops=size ** 3, moved=6 * size ** 2)
    turned0 = call(functools.partial(pair_kernel, 0), part, [V] * 4, **half_cost)(*blocks_here)
    before0 = lax.ppermute(turned0, "tm", onward)
    turned1 = call(functools.partial(pair_kernel, 1), longer, [V] * 4, **half_cost)(*blocks_here)
    before1 = lax.ppermute(turned1, "tm", onward)

    begin = after(prior.reshape(1, size), turned1)
    came = begin
    for turn in range(firsts):
        if turn < DIRECT:
            begin, value = call(
                functools.partial(direct_kernel, turn), (row, row), [V] * 6,
                flops=64 * size ** 2, moved=4 * size ** 2,
            )(begin, came, *blocks_here)
        else:
            begin, value = call(
                functools.partial(hop_kernel, turn), (row, row), [V] * 4,
                flops=32 * size ** 2, moved=2 * size ** 2,
            )(begin, came, turned0, turned1)
        came = lax.ppermute(value, "tm", [(2 * turn + 1, 2 * turn + (3 if turn + 1 < firsts else 5))])
        if turn == 3:
            maps, terms = call(
                ready_kernel,
                (jax.ShapeDtypeStruct((size, steps_here * width), BF16), jax.ShapeDtypeStruct((steps_here, width), F32)),
                [V] * 8, flops=size ** 3, moved=4 * size ** 2,
            )(other, other_term, locals_, value, early[0], slab2, slab3, slab4)
        if turn == 4:
            came = after(came, maps)
    double0 = call(functools.partial(double_kernel, 0, firsts), part, [V] * 3, **half_cost)(before0, turned0, turned1)
    double1 = call(functools.partial(double_kernel, 1, firsts), longer, [V] * 3, **half_cost)(before1, turned0, turned1)
    cames = [came]
    for chip in range(firsts + 1, chips - 1, 2):
        value = call(
            functools.partial(far_kernel, chip), row, [V] * 4, flops=32 * size ** 2, moved=2 * size ** 2
        )(came, value, double0, double1)
        came = lax.ppermute(value, "tm", [(2 * chip + 1, 2 * chip + 5)])
        cames.append(came)
    handed = lax.ppermute(value, "tm", [(2 * c - 1, 2 * c + 1) for c in range(firsts, chips, 2)])
    begin = call(
        functools.partial(final_kernel, firsts), row, [V] * (4 + len(cames)), flops=32 * size ** 2, moved=2 * size ** 2
    )(begin, handed, before0, before1, *cames)
    got = lax.ppermute(begin, "tm", [(b, a) for a, b in pairs])
    return call(
        out_kernel, jax.ShapeDtypeStruct((steps_here, width), F32), [V] * 4,
        flops=16 * size ** 2, moved=size ** 2,
    )(begin, got, maps, terms)


def solution(mesh):
    return jax.shard_map(
        shards,
        mesh=mesh,
        in_specs=(
            P("tm", None),
            P("tm", None),
            P("tm", "state", None, None),
            P("tm", "state"),
            P("tm", "state"),
            P("tm", "state", None),
            P(),
        ),
        out_specs=P("tm", "state"),
        check_vma=False,
    )
```

```python
import functools

import jax
import jax.numpy as jnp
from jax import lax
from jax.experimental import pallas as pl
from jax.experimental.pallas import tpu as pltpu
from jax.sharding import PartitionSpec as P

F32 = jnp.float32
BF16 = jnp.bfloat16
VMEM_LIMIT = 24 * 1024 * 1024
ROWS = 512


def three_parts(x):
    hi = x.astype(BF16).astype(F32)
    rest = x - hi
    mid = rest.astype(BF16).astype(F32)
    return hi, mid, rest - mid


def split_rows(x):
    hi, mid, lo = three_parts(x)
    row = lax.broadcasted_iota(jnp.int32, (16, x.shape[1]), 0)
    out = jnp.where(row == 0, hi, jnp.where(row == 1, mid, jnp.where(row == 2, lo, 0.0)))
    return out.astype(BF16)


def joined(rows):
    return jnp.sum(rows.astype(F32), axis=0, keepdims=True)


def times_t(x, *parts):
    left = split_rows(x)
    out = [
        joined(lax.dot_general(left, part, (((1,), (1,)), ((), ())), preferred_element_type=F32)) for part in parts
    ]
    return out[0] if len(out) == 1 else jnp.concatenate(out, axis=1)


def times(x, *parts):
    left = split_rows(x)
    return joined(product(left, *parts))


def product(left, *parts):
    rows = parts[0].shape[0]
    out = [
        jnp.dot(left[:, i * rows:(i + 1) * rows], part, preferred_element_type=F32) for i, part in enumerate(parts)
    ]
    return sum(out[1:], out[0])


def matmul(left_ref, right_ref, out_ref):
    def block(i, carry):
        at = pl.ds(pl.multiple_of(i * ROWS, ROWS), ROWS)
        out_ref[at, :] = jnp.dot(left_ref[at, :], right_ref[...], preferred_element_type=F32).astype(BF16)
        return carry

    lax.fori_loop(0, left_ref.shape[0] // ROWS, block, 0)


def core_here():
    return lax.rem(lax.axis_index("tm"), 2)


def chip_here():
    return lax.div(lax.axis_index("tm"), 2)


def drive_kernel(
    rows_ref, cols_ref, values_ref, blocks_ref, maps_ref, out_ref, weighted_ref, parts_ref, sems
):
    steps, count, side, _ = blocks_ref.shape
    later, width, size = maps_ref.shape
    copies = []
    for j in range(later):
        copies.append(pltpu.make_async_copy(maps_ref.at[j], out_ref.at[pl.ds(j * width, width), :], sems.at[j]))
        copies[j].start()
    weighted = values_ref[...].astype(F32)
    pieces = weighted_ref.shape[0]
    for r in range(pieces):
        weighted_ref[r] = weighted[:, r * side:(r + 1) * side]
    parts_ref[...] = jnp.zeros_like(parts_ref)
    piece = lax.broadcasted_iota(jnp.int32, (pieces, count), 0)
    column = lax.broadcasted_iota(jnp.int32, (size // side, count), 0)
    own = lax.broadcasted_iota(jnp.int32, (count, count * side), 0) == (
        lax.broadcasted_iota(jnp.int32, (count, count * side), 1) // side
    )
    for t in range(steps):
        chosen = (piece == rows_ref[t:t + 1, :]).astype(F32).astype(BF16)
        left = lax.dot_general(
            chosen, weighted_ref[:, t, :].astype(BF16), (((0,), (0,)), ((), ())), preferred_element_type=F32
        )
        left = jnp.concatenate([left] * count, axis=1)
        left = jnp.where(own, left, 0.0).astype(BF16)
        terms = jnp.dot(left, blocks_ref[t].reshape(count * side, side), preferred_element_type=F32)
        chosen = (column == cols_ref[t:t + 1, :]).astype(F32).astype(BF16)
        drive = sum(jnp.dot(chosen, part.astype(BF16), preferred_element_type=F32) for part in three_parts(terms))
        for i, part in enumerate(three_parts(drive)):
            for c in range(size // side):
                parts_ref[3 * t + i:3 * t + i + 1, c * side:(c + 1) * side] = part[c:c + 1, :]
    out_ref[later * width:, :] = parts_ref[...].astype(BF16)
    for copy in copies:
        copy.wait()


def fetched(count, place, pieces, j, whole_ref, sems, first):
    width = whole_ref.shape[0] // count
    copies = []
    for i, (r, piece) in enumerate(pieces):
        at = pl.multiple_of(lax.rem(place + r, count) * width, width)
        copy = pltpu.make_async_copy(
            piece.at[pl.ds(j * width, width), :], whole_ref.at[pl.ds(at, width), :], sems.at[first + i]
        )
        copy.start()
        copies.append(copy)
    return copies


def two_kernel(count, *refs):
    pieces, (two_ref, slab_ref, one_ref, next_ref, sems) = list(enumerate(refs[:count])), refs[count:]
    width = slab_ref.shape[0]
    place = lax.axis_index("state")
    ones = fetched(count, place, pieces, 0, one_ref, sems, 0)
    nexts = fetched(count, place, pieces, 1, next_ref, sems, count)
    for copy in ones + nexts:
        copy.wait()
    matmul(next_ref, one_ref, two_ref)
    slab_ref[...] = two_ref[pl.ds(pl.multiple_of(place * width, width), width), :]


def three_kernel(count, have, two_ref, *refs):
    pieces = list(zip(have, refs[:len(have)]))
    three_ref, third_ref, fourth_ref, sems = refs[len(have):]
    width = third_ref.shape[0] // count
    place = lax.axis_index("state")
    copies = fetched(count, place, pieces, 0, third_ref, sems, 0)
    copies += fetched(count, place, pieces, 1, fourth_ref, sems, len(have))
    for copy in copies:
        copy.wait()
    for r in have:
        at = pl.ds(pl.multiple_of(lax.rem(place + r, count) * width, width), width)
        three_ref[at, :] = jnp.dot(third_ref[at, :], two_ref[...], preferred_element_type=F32).astype(BF16)


def stepped(x, drive_ref, *map_refs):
    for j, map_ref in enumerate(map_refs):
        x = times_t(x, map_ref[...]) + joined(drive_ref[3 * j:3 * j + 3, :])
    return x


def gather_kernel(count, have, prior_ref, first_ref, second_ref, thirds_ref, fourths_ref, *refs):
    missing = [(r, refs[r]) for r in range(count) if r not in have]
    third_ref, fourth_ref, drive_ref, mean_ref, parts_ref, sems = refs[count:]
    width = third_ref.shape[0] // count
    place = lax.axis_index("state")
    copies = fetched(count, place, missing, 0, third_ref, sems, 0)
    copies += fetched(count, place, missing, 1, fourth_ref, sems, len(missing))
    for r in range(count):
        at = 2 * len(missing) + r
        copies.append(pltpu.make_async_copy(refs[r].at[pl.ds(2 * width, 16), :], parts_ref.at[r], sems.at[at]))
        copies[at].start()
    for copy in copies:
        copy.wait()
    drive_ref[...] = jnp.sum(parts_ref[...].astype(F32), axis=0)
    mean_ref[...] = prior_ref[...]

    @pl.when(lax.axis_index("tm") == 0)
    def _():
        mean_ref[...] = stepped(prior_ref[...], drive_ref, first_ref, second_ref, third_ref, fourth_ref)


def first_kernel(mean_ref, drive_ref, first_ref, second_ref, third_ref, fourth_ref, value_ref):
    value_ref[...] = mean_ref[...]

    @pl.when(lax.axis_index("tm") == 1)
    def _():
        value_ref[...] = stepped(mean_ref[...], drive_ref, first_ref, second_ref, third_ref, fourth_ref)


def four_kernel(count, have, after_ref, two_ref, threes_ref, third_ref, fourth_ref, four_ref, slab3_ref, slab4_ref, three_ref):
    width = slab3_ref.shape[0]
    place = lax.axis_index("state")
    for r in range(count):
        if r not in have:
            at = pl.ds(pl.multiple_of(lax.rem(place + r, count) * width, width), width)
            three_ref[at, :] = jnp.dot(third_ref[at, :], two_ref[...], preferred_element_type=F32).astype(BF16)
    mine = pl.ds(pl.multiple_of(place * width, width), width)
    slab3_ref[...] = three_ref[mine, :]

    @pl.when(chip_here() == 0)
    def _():
        slab4_ref[...] = jnp.dot(fourth_ref[mine, :], three_ref[...], preferred_element_type=F32).astype(BF16)

    @pl.when(chip_here() != 0)
    def _():
        matmul(fourth_ref, three_ref, four_ref)
        slab4_ref[...] = four_ref[mine, :]


def local_kernel(late, drive_ref, after_ref, second_ref, third_ref, fourth_ref, locals_ref, term_ref):
    @pl.when((chip_here() == 0) == late)
    def _():
        local = joined(drive_ref[0:3, :])
        locals_ref[0:1, :] = local
        for j, map_ref in enumerate((second_ref, third_ref, fourth_ref)):
            local = times_t(local, map_ref[...]) + joined(drive_ref[3 * j + 3:3 * j + 6, :])
            locals_ref[j + 1:j + 2, :] = local
        term_ref[...] = split_rows(local)


DIRECT = 2


def pair_kernel(own_ref, own_term_ref, other_ref, other_term_ref, turned_ref):
    size = own_ref.shape[0]

    @pl.when(jnp.logical_and(core_here() != 0, chip_here() >= DIRECT))
    def _():
        def block(i, carry):
            at = pl.ds(pl.multiple_of(i * ROWS, ROWS), ROWS)
            out = jnp.dot(own_ref[at, :], other_ref[...], preferred_element_type=F32)
            turned_ref[:size, at] = out.T.astype(BF16)
            return carry

        lax.fori_loop(0, size // ROWS, block, 0)
        term = times_t(joined(other_term_ref[...]), own_ref[...]) + joined(own_term_ref[...])
        turned_ref[size:, :] = split_rows(term)


def applied(x, turned_ref):
    size = x.shape[1]
    return times(x, turned_ref[:size, :]) + joined(turned_ref[size:, :])


def direct_kernel(turn, begin_ref, came_ref, own_ref, own_term_ref, other_ref, other_term_ref, held_ref, value_ref):
    held_ref[...] = begin_ref[...]
    value_ref[...] = begin_ref[...]

    @pl.when(lax.axis_index("tm") == 2 * turn + 1)
    def _():
        begin = came_ref[...]
        held_ref[...] = begin
        between = times_t(begin, other_ref[...]) + joined(other_term_ref[...])
        value_ref[...] = times_t(between, own_ref[...]) + joined(own_term_ref[...])


def hop_kernel(turn, begin_ref, came_ref, turned_ref, held_ref, value_ref):
    here = lax.axis_index("tm") == 2 * turn + 1

    @pl.when(here)
    def _():
        begin = came_ref[...]
        held_ref[...] = begin
        value_ref[...] = applied(begin, turned_ref)

    @pl.when(jnp.logical_not(here))
    def _():
        held_ref[...] = begin_ref[...]
        value_ref[...] = begin_ref[...]


def double_kernel(firsts, came_ref, turned_ref, double_ref):
    size = turned_ref.shape[1]
    chip = chip_here()

    @pl.when((core_here() != 0) & (chip > firsts) & (lax.rem(chip, 2) == 1) & (chip < 2 * firsts - 1))
    def _():
        matmul(came_ref.at[:size, :], turned_ref.at[:size, :], double_ref)
        double_ref[size:, :] = split_rows(applied(joined(came_ref[size:, :]), turned_ref))


def far_kernel(chip, came_ref, before_ref, double_ref, value_ref):
    here = lax.axis_index("tm") == 2 * chip + 1

    @pl.when(here)
    def _():
        value_ref[...] = applied(came_ref[...], double_ref)

    @pl.when(jnp.logical_not(here))
    def _():
        value_ref[...] = before_ref[...]


def final_kernel(firsts, held_ref, handed_ref, map_ref, *refs):
    cames, begin_ref = refs[:-1], refs[-1]
    chip = chip_here()
    handed = jnp.logical_and(chip >= firsts, lax.rem(chip, 2) == 0)
    begin_ref[...] = jnp.where(handed, handed_ref[...], held_ref[...])
    for i, came_ref in enumerate(cames):
        @pl.when(lax.axis_index("tm") == 2 * (firsts + 1 + 2 * i) + 1)
        def _():
            begin_ref[...] = applied(came_ref[...], map_ref)


def ready_kernel(other_ref, other_term_ref, locals_ref, lates_ref, after_ref, *refs):
    slabs, (maps_ref, terms_ref) = refs[:-2], refs[-2:]
    width, size = slabs[1].shape
    mine = pl.ds(pl.multiple_of(lax.axis_index("state") * width, width), width)
    plain = jnp.logical_or(core_here() == 0, chip_here() == 0)
    terms_ref[...] = jnp.where(chip_here() == 0, lates_ref[:, mine], locals_ref[:, mine])

    @pl.when(plain)
    def _():
        for j, slab_ref in enumerate(slabs):
            maps_ref[:, j * width:(j + 1) * width] = slab_ref[:width, :].astype(F32).T.astype(BF16)

    @pl.when(jnp.logical_not(plain))
    def _():
        for j, slab_ref in enumerate(slabs):
            at = slice(j * width, (j + 1) * width)
            out = jnp.dot(slab_ref[:width, :], other_ref[...], preferred_element_type=F32)
            maps_ref[:, at] = out.T.astype(BF16)
            terms_ref[j:j + 1, :] += times_t(joined(other_term_ref[...]), slab_ref[:width, :])


def out_kernel(prior_ref, mean_ref, begin_ref, got_ref, maps_ref, terms_ref, out_ref):
    steps, width = out_ref.shape
    first = jnp.where(core_here() == 0, prior_ref[...], mean_ref[...])
    begin = jnp.where(core_here() == 0, got_ref[...], begin_ref[...])
    begin = jnp.where(chip_here() == 0, first, begin)
    row = times(begin, maps_ref[...])
    for j in range(steps):
        out_ref[j:j + 1, :] = row[:, j * width:(j + 1) * width] + terms_ref[j:j + 1, :]


def call(kernel, out_shape, spaces, scratch=(), flops=0, moved=0, aliases={}):
    return pl.pallas_call(
        kernel,
        out_shape=out_shape,
        in_specs=[pl.BlockSpec(memory_space=s) for s in spaces],
        out_specs=jax.tree.map(lambda _: pl.BlockSpec(memory_space=pltpu.VMEM), out_shape),
        scratch_shapes=list(scratch),
        input_output_aliases=aliases,
        compiler_params=pltpu.CompilerParams(vmem_limit_bytes=VMEM_LIMIT),
        cost_estimate=pl.CostEstimate(flops=flops, bytes_accessed=moved, transcendentals=0),
    )


def after(value, *needed):
    return lax.optimization_barrier((value, needed))[0]


def ring_rounds(parts, axis, needed):
    count = lax.axis_size(axis)
    forward = [(i, (i + 1) % count) for i in range(count)]
    backward = [((i + 1) % count, i) for i in range(count)]
    half = count // 2
    found = [{0: part} for part in parts]
    for r in range(1, half + 1):
        for i, pieces in enumerate(found):
            left, right = pieces[(count - r + 1) % count], pieces[r - 1]
            more = needed(r, i, found)
            if more:
                left, right = after((left, right), *more)
            if r < half or i % 2 == 0:
                pieces[count - r] = lax.ppermute(left, axis, forward)
            if r < half or i % 2 == 1:
                pieces[r] = lax.ppermute(right, axis, backward)
    return [[pieces[r] for r in range(count)] for pieces in found]


def shards(observations, precisions, blocks, block_rows, block_cols, transition, prior):
    steps_here, width, size = transition.shape
    side = blocks.shape[2]
    count = lax.axis_size("state")
    blocks_of_time = lax.axis_size("tm")
    V, S, A = pltpu.VMEM, pltpu.SMEM, pl.ANY

    matrix = jax.ShapeDtypeStruct((size, size), BF16)
    slab = jax.ShapeDtypeStruct((width, size), BF16)
    rows = jax.ShapeDtypeStruct((16, size), BF16)
    steps = jax.ShapeDtypeStruct((steps_here, size), F32)
    row = jax.ShapeDtypeStruct((1, size), F32)
    whole = pltpu.VMEM((size, size), BF16)

    half = steps_here // 2
    pieces = observations.shape[1] // side
    packed = call(
        drive_kernel, jax.ShapeDtypeStruct((half * width + 16, size), BF16), [V] * 4 + [A],
        [
            pltpu.VMEM((pieces, steps_here, side), F32),
            pltpu.VMEM((16, size), F32),
            pltpu.SemaphoreType.DMA((half,)),
        ],
        flops=10 ** 7, moved=2 ** 21,
    )(block_rows, block_cols, (precisions * observations).astype(BF16), blocks, transition[half:])
    early, late = ring_rounds(
        [transition[:half].reshape(half * width, size), packed], "state",
        lambda r, i, found: (packed,) if (r, i) == (2, 0) else (),
    )
    two, slab2, first, second = call(
        functools.partial(two_kernel, count), (matrix, slab, matrix, matrix), [A] * count,
        [pltpu.SemaphoreType.DMA((2 * count,))], flops=2 * size ** 3, moved=6 * size ** 2,
    )(*early)
    have = [r for r in range(count) if r not in (count // 2, count // 2 + 1)]
    three, third, fourth = call(
        functools.partial(three_kernel, count, have), (matrix, matrix, matrix), [V] + [A] * len(have),
        [pltpu.SemaphoreType.DMA((2 * len(have),))], flops=2 * size ** 3, moved=6 * size ** 2,
    )(two, *[late[r] for r in have])
    start = prior.reshape(1, size)
    third, fourth, drive, mean = call(
        functools.partial(gather_kernel, count, have),
        (matrix, matrix, jax.ShapeDtypeStruct((16, size), F32), row),
        [V] * 5 + [A] * count,
        [pltpu.VMEM((count, 16, size), BF16), pltpu.SemaphoreType.DMA((3 * count,))],
        flops=128 * size ** 2, moved=2 * size ** 2, aliases={3: 0, 4: 1},
    )(start, first, second, third, fourth, *late)
    pairs = [(i, i + 1) for i in range(0, blocks_of_time, 2)]
    mean = lax.ppermute(mean, "tm", pairs[:1])
    value = call(first_kernel, row, [V] * 6, flops=128 * size ** 2, moved=8 * size ** 2)(
        mean, drive, first, second, third, fourth
    )
    came = lax.ppermute(value, "tm", [(1, 3)])
    own, slab3, slab4, _ = call(
        functools.partial(four_kernel, count, have), (matrix, slab, slab, matrix), [V] * 5,
        flops=2 * size ** 3, moved=6 * size ** 2, aliases={2: 3},
    )(value, two, three, third, fourth)
    other = lax.ppermute(own, "tm", pairs[1:])

    def locals_of(is_late, needed):
        return call(
            functools.partial(local_kernel, is_late), (steps, rows), [V] * 5, flops=96 * size ** 2, moved=6 * size ** 2
        )(drive, needed, second, third, fourth)

    locals_, own_term = locals_of(False, value)
    other_term = lax.ppermute(own_term, "tm", pairs[1:])

    chips = blocks_of_time // 2
    firsts = chips // 2
    part = jax.ShapeDtypeStruct((size // 2, size), BF16)
    longer = jax.ShapeDtypeStruct((size + 16, size), BF16)
    blocks_here = (own, own_term, other, other_term)
    onward = [(2 * c + 1, 2 * c + 3) for c in range(firsts, chips, 2)]
    turned = call(pair_kernel, longer, [V] * 4, flops=2 * size ** 3, moved=6 * size ** 2)(*blocks_here)
    before = lax.ppermute(turned, "tm", onward)

    begin = after(start, turned)
    for turn in range(1, firsts):
        if turn < DIRECT:
            begin, value = call(
                functools.partial(direct_kernel, turn), (row, row), [V] * 6,
                flops=64 * size ** 2, moved=4 * size ** 2,
            )(begin, came, *blocks_here)
        else:
            begin, value = call(
                functools.partial(hop_kernel, turn), (row, row), [V] * 3,
                flops=32 * size ** 2, moved=2 * size ** 2,
            )(begin, came, turned)
        came = lax.ppermute(value, "tm", [(2 * turn + 1, 2 * turn + (3 if turn + 1 < firsts else 5))])
        if turn == 3:
            lates, _ = locals_of(True, value)
            maps, terms = call(
                ready_kernel,
                (jax.ShapeDtypeStruct((size, steps_here * width), BF16), jax.ShapeDtypeStruct((steps_here, width), F32)),
                [V] * 9, flops=size ** 3, moved=4 * size ** 2,
            )(other, other_term, locals_, lates, value, early[0], slab2, slab3, slab4)
        if turn == 4:
            came = after(came, maps)
    double = call(
        functools.partial(double_kernel, firsts), longer, [V, V], flops=2 * size ** 3, moved=6 * size ** 2
    )(before, turned)
    cames = [came]
    for chip in range(firsts + 1, chips - 1, 2):
        value = call(
            functools.partial(far_kernel, chip), row, [V] * 3, flops=32 * size ** 2, moved=2 * size ** 2
        )(came, value, double)
        came = lax.ppermute(value, "tm", [(2 * chip + 1, 2 * chip + 5)])
        cames.append(came)
    handed = lax.ppermute(value, "tm", [(2 * c - 1, 2 * c + 1) for c in range(firsts, chips, 2)])
    begin = call(
        functools.partial(final_kernel, firsts), row, [V] * (3 + len(cames)), flops=32 * size ** 2, moved=2 * size ** 2
    )(begin, handed, before, *cames)
    got = lax.ppermute(begin, "tm", [(b, a) for a, b in pairs])
    return call(
        out_kernel, jax.ShapeDtypeStruct((steps_here, width), F32), [V] * 6,
        flops=16 * size ** 2, moved=size ** 2,
    )(start, mean, begin, got, maps, terms)


def solution(mesh):
    return jax.shard_map(
        shards,
        mesh=mesh,
        in_specs=(
            P("tm", None),
            P("tm", None),
            P("tm", "state", None, None),
            P("tm", "state"),
            P("tm", "state"),
            P("tm", "state", None),
            P(),
        ),
        out_specs=P("tm", "state"),
        check_vma=False,
    )
```

```python
import functools

import jax
import jax.numpy as jnp
from jax import lax
from jax.experimental import pallas as pl
from jax.experimental.pallas import tpu as pltpu
from jax.sharding import PartitionSpec as P

F32 = jnp.float32
BF16 = jnp.bfloat16
VMEM_LIMIT = 24 * 1024 * 1024
ROWS = 512


def three_parts(x):
    hi = x.astype(BF16).astype(F32)
    rest = x - hi
    mid = rest.astype(BF16).astype(F32)
    return hi, mid, rest - mid


def split_rows(x):
    hi, mid, lo = three_parts(x)
    row = lax.broadcasted_iota(jnp.int32, (16, x.shape[1]), 0)
    out = jnp.where(row == 0, hi, jnp.where(row == 1, mid, jnp.where(row == 2, lo, 0.0)))
    return out.astype(BF16)


def joined(rows):
    return jnp.sum(rows.astype(F32), axis=0, keepdims=True)


def times_t(x, *parts):
    left = split_rows(x)
    out = [
        joined(lax.dot_general(left, part, (((1,), (1,)), ((), ())), preferred_element_type=F32)) for part in parts
    ]
    return out[0] if len(out) == 1 else jnp.concatenate(out, axis=1)


def times(x, *parts):
    left = split_rows(x)
    return joined(product(left, *parts))


def product(left, *parts):
    rows = parts[0].shape[0]
    out = [
        jnp.dot(left[:, i * rows:(i + 1) * rows], part, preferred_element_type=F32) for i, part in enumerate(parts)
    ]
    return sum(out[1:], out[0])


def matmul(left_ref, right_ref, out_ref):
    def block(i, carry):
        at = pl.ds(pl.multiple_of(i * ROWS, ROWS), ROWS)
        out_ref[at, :] = jnp.dot(left_ref[at, :], right_ref[...], preferred_element_type=F32).astype(BF16)
        return carry

    lax.fori_loop(0, left_ref.shape[0] // ROWS, block, 0)


def core_here():
    return lax.rem(lax.axis_index("tm"), 2)


def chip_here():
    return lax.div(lax.axis_index("tm"), 2)


def drive_kernel(
    rows_ref, cols_ref, values_ref, blocks_ref, maps_ref, out_ref, weighted_ref, parts_ref, sems
):
    steps, count, side, _ = blocks_ref.shape
    later, width, size = maps_ref.shape
    copies = []
    for j in range(later):
        copies.append(pltpu.make_async_copy(maps_ref.at[j], out_ref.at[pl.ds(j * width, width), :], sems.at[j]))
        copies[j].start()
    weighted = values_ref[...].astype(F32)
    pieces = weighted_ref.shape[0]
    for r in range(pieces):
        weighted_ref[r] = weighted[:, r * side:(r + 1) * side]
    parts_ref[...] = jnp.zeros_like(parts_ref)
    piece = lax.broadcasted_iota(jnp.int32, (pieces, count), 0)
    column = lax.broadcasted_iota(jnp.int32, (size // side, count), 0)
    own = lax.broadcasted_iota(jnp.int32, (count, count * side), 0) == (
        lax.broadcasted_iota(jnp.int32, (count, count * side), 1) // side
    )
    for t in range(steps):
        chosen = (piece == rows_ref[t:t + 1, :]).astype(F32).astype(BF16)
        left = lax.dot_general(
            chosen, weighted_ref[:, t, :].astype(BF16), (((0,), (0,)), ((), ())), preferred_element_type=F32
        )
        left = jnp.concatenate([left] * count, axis=1)
        left = jnp.where(own, left, 0.0).astype(BF16)
        terms = jnp.dot(left, blocks_ref[t].reshape(count * side, side), preferred_element_type=F32)
        chosen = (column == cols_ref[t:t + 1, :]).astype(F32).astype(BF16)
        drive = sum(jnp.dot(chosen, part.astype(BF16), preferred_element_type=F32) for part in three_parts(terms))
        for i, part in enumerate(three_parts(drive)):
            for c in range(size // side):
                parts_ref[3 * t + i:3 * t + i + 1, c * side:(c + 1) * side] = part[c:c + 1, :]
    out_ref[later * width:, :] = parts_ref[...].astype(BF16)
    for copy in copies:
        copy.wait()


def rows_of(r, width, count):
    owner = lax.rem(lax.axis_index("state") + r + core_here() * (count - 2 * r), count)
    return pl.ds(pl.multiple_of(owner * width, width), width)


def fetched(count, pieces, j, whole_ref, sems, first):
    width = whole_ref.shape[0] // count
    copies = []
    for i, (r, piece) in enumerate(pieces):
        copy = pltpu.make_async_copy(
            piece.at[pl.ds(j * width, width), :], whole_ref.at[rows_of(r, width, count), :], sems.at[first + i]
        )
        copy.start()
        copies.append(copy)
    return copies


def two_kernel(count, *refs):
    pieces, (two_ref, slab_ref, next_ref, one_ref, sems) = list(enumerate(refs[:count])), refs[count:]
    width = slab_ref.shape[0]
    place = lax.axis_index("state")
    ones = fetched(count, pieces, 0, one_ref, sems, 0)
    nexts = fetched(count, pieces, 1, next_ref, sems, count)
    for copy in ones + nexts:
        copy.wait()
    matmul(next_ref, one_ref, two_ref)
    slab_ref[...] = two_ref[pl.ds(pl.multiple_of(place * width, width), width), :]


def three_kernel(count, have, two_ref, *refs):
    pieces = list(zip(have, refs[:len(have)]))
    three_ref, third_ref, fourth_ref, sems = refs[len(have):]
    width = third_ref.shape[0] // count
    copies = fetched(count, pieces, 0, third_ref, sems, 0)
    copies += fetched(count, pieces, 1, fourth_ref, sems, len(have))
    for copy in copies:
        copy.wait()
    for r in have:
        at = rows_of(r, width, count)
        three_ref[at, :] = jnp.dot(third_ref[at, :], two_ref[...], preferred_element_type=F32).astype(BF16)


def four_kernel(count, have, two_ref, threes_ref, thirds_ref, fourths_ref, *refs):
    pieces = refs[:count]
    four_ref, slab3_ref, slab4_ref, three_ref, third_ref, fourth_ref, drive_ref, parts_ref, sems = refs[count:]
    width = slab3_ref.shape[0]
    parts = []
    for i, r in enumerate(have):
        parts.append(pltpu.make_async_copy(pieces[r].at[pl.ds(2 * width, 16), :], parts_ref.at[i], sems.at[i]))
        parts[i].start()
    drive = jnp.zeros(drive_ref.shape, F32)
    for r in range(count):
        if r not in have:
            at = rows_of(r, width, count)
            third_ref[at, :] = pieces[r][:width, :]
            fourth_ref[at, :] = pieces[r][width:2 * width, :]
            three_ref[at, :] = jnp.dot(pieces[r][:width, :], two_ref[...], preferred_element_type=F32).astype(BF16)
            drive += pieces[r][2 * width:, :].astype(F32)
    matmul(fourth_ref, three_ref, four_ref)
    mine = pl.ds(pl.multiple_of(lax.axis_index("state") * width, width), width)
    slab3_ref[...] = three_ref[mine, :]
    slab4_ref[...] = four_ref[mine, :]
    for copy in parts:
        copy.wait()
    drive_ref[...] = drive + jnp.sum(parts_ref[...].astype(F32), axis=0)


def local_kernel(drive_ref, second_ref, third_ref, fourth_ref, locals_ref, term_ref):
    local = joined(drive_ref[0:3, :])
    locals_ref[0:1, :] = local
    for j, map_ref in enumerate((second_ref, third_ref, fourth_ref)):
        local = times_t(local, map_ref[...]) + joined(drive_ref[3 * j + 3:3 * j + 6, :])
        locals_ref[j + 1:j + 2, :] = local
    term_ref[...] = split_rows(local)


DIRECT = 2


def pair_kernel(half, own_ref, own_term_ref, other_ref, other_term_ref, turned_ref):
    rows = own_ref.shape[0] // 2
    at = slice(half * rows, (half + 1) * rows)

    @pl.when(jnp.logical_and(core_here() != 0, chip_here() >= DIRECT))
    def _():
        for i in range(2):
            out = jnp.dot(own_ref[i * rows:(i + 1) * rows, :], other_ref[:, at], preferred_element_type=F32)
            turned_ref[:rows, i * rows:(i + 1) * rows] = out.T.astype(BF16)
        if half == 1:
            term = times_t(joined(other_term_ref[...]), own_ref[...]) + joined(own_term_ref[...])
            turned_ref[rows:, :] = split_rows(term)


def applied(x, turned0_ref, turned1_ref):
    rows = turned0_ref.shape[0]
    return times(x, turned0_ref[...], turned1_ref[:rows, :]) + joined(turned1_ref[rows:, :])


def direct_kernel(turn, begin_ref, came_ref, own_ref, own_term_ref, other_ref, other_term_ref, held_ref, value_ref):
    held_ref[...] = begin_ref[...]
    value_ref[...] = begin_ref[...]

    @pl.when(lax.axis_index("tm") == 2 * turn + 1)
    def _():
        begin = came_ref[...]
        held_ref[...] = begin
        between = times_t(begin, other_ref[...]) + joined(other_term_ref[...])
        value_ref[...] = times_t(between, own_ref[...]) + joined(own_term_ref[...])


def hop_kernel(turn, begin_ref, came_ref, turned0_ref, turned1_ref, held_ref, value_ref):
    here = lax.axis_index("tm") == 2 * turn + 1

    @pl.when(here)
    def _():
        begin = came_ref[...]
        held_ref[...] = begin
        value_ref[...] = applied(begin, turned0_ref, turned1_ref)

    @pl.when(jnp.logical_not(here))
    def _():
        held_ref[...] = begin_ref[...]
        value_ref[...] = begin_ref[...]


def double_kernel(half, firsts, came_ref, turned0_ref, turned1_ref, double_ref):
    rows = turned0_ref.shape[0]
    chip = chip_here()

    @pl.when((core_here() != 0) & (chip > firsts) & (lax.rem(chip, 2) == 1) & (chip < 2 * firsts - 1))
    def _():
        double_ref[:rows, :] = product(came_ref[:rows, :], turned0_ref[...], turned1_ref[:rows, :]).astype(BF16)
        if half == 1:
            double_ref[rows:, :] = split_rows(applied(joined(came_ref[rows:, :]), turned0_ref, turned1_ref))


def far_kernel(chip, came_ref, before_ref, double0_ref, double1_ref, value_ref):
    here = lax.axis_index("tm") == 2 * chip + 1

    @pl.when(here)
    def _():
        value_ref[...] = applied(came_ref[...], double0_ref, double1_ref)

    @pl.when(jnp.logical_not(here))
    def _():
        value_ref[...] = before_ref[...]


def final_kernel(firsts, held_ref, handed_ref, map0_ref, map1_ref, *refs):
    cames, begin_ref = refs[:-1], refs[-1]
    chip = chip_here()
    handed = jnp.logical_and(chip >= firsts, lax.rem(chip, 2) == 0)
    begin_ref[...] = jnp.where(handed, handed_ref[...], held_ref[...])
    for i, came_ref in enumerate(cames):
        @pl.when(lax.axis_index("tm") == 2 * (firsts + 1 + 2 * i) + 1)
        def _():
            begin_ref[...] = applied(came_ref[...], map0_ref, map1_ref)


def ready_kernel(other_ref, other_term_ref, locals_ref, after_ref, *refs):
    slabs, (maps_ref, terms_ref) = refs[:-2], refs[-2:]
    width, size = slabs[1].shape
    mine = pl.ds(pl.multiple_of(lax.axis_index("state") * width, width), width)

    @pl.when(core_here() == 0)
    def _():
        for j, slab_ref in enumerate(slabs):
            maps_ref[:, j * width:(j + 1) * width] = slab_ref[:width, :].astype(F32).T.astype(BF16)
            terms_ref[j:j + 1, :] = locals_ref[j:j + 1, mine]

    @pl.when(core_here() != 0)
    def _():
        for j, slab_ref in enumerate(slabs):
            at = slice(j * width, (j + 1) * width)
            out = jnp.dot(slab_ref[:width, :], other_ref[...], preferred_element_type=F32)
            maps_ref[:, at] = out.T.astype(BF16)
            term = times_t(joined(other_term_ref[...]), slab_ref[:width, :])
            terms_ref[j:j + 1, :] = term + locals_ref[j:j + 1, mine]


def out_kernel(begin_ref, got_ref, maps_ref, terms_ref, out_ref):
    steps, width = out_ref.shape
    begin = jnp.where(core_here() == 0, got_ref[...], begin_ref[...])
    row = times(begin, maps_ref[...])
    for j in range(steps):
        out_ref[j:j + 1, :] = row[:, j * width:(j + 1) * width] + terms_ref[j:j + 1, :]


def call(kernel, out_shape, spaces, scratch=(), flops=0, moved=0, aliases={}):
    return pl.pallas_call(
        kernel,
        out_shape=out_shape,
        in_specs=[pl.BlockSpec(memory_space=s) for s in spaces],
        out_specs=jax.tree.map(lambda _: pl.BlockSpec(memory_space=pltpu.VMEM), out_shape),
        scratch_shapes=list(scratch),
        input_output_aliases=aliases,
        compiler_params=pltpu.CompilerParams(vmem_limit_bytes=VMEM_LIMIT),
        cost_estimate=pl.CostEstimate(flops=flops, bytes_accessed=moved, transcendentals=0),
    )


def after(value, *needed):
    return lax.optimization_barrier((value, needed))[0]


def ring_rounds(parts, needed):
    lines, count = lax.axis_size("tm"), lax.axis_size("state")
    forward = [(b * count + i, b * count + (i + 1 - 2 * (b % 2)) % count) for b in range(lines) for i in range(count)]
    backward = [(there, here) for here, there in forward]
    half = count // 2
    found = [{0: part} for part in parts]
    for r in range(1, half + 1):
        for i, pieces in enumerate(found):
            left, right = pieces[(count - r + 1) % count], pieces[r - 1]
            more = needed(r, i, found)
            if more:
                left, right = after((left, right), *more)
            if r < half or i % 2 == 0:
                pieces[count - r] = lax.ppermute(left, ("tm", "state"), forward)
            if r < half or i % 2 == 1:
                pieces[r] = lax.ppermute(right, ("tm", "state"), backward)
    return [[pieces[r] for r in range(count)] for pieces in found]


def shards(observations, precisions, blocks, block_rows, block_cols, transition, prior):
    steps_here, width, size = transition.shape
    side = blocks.shape[2]
    count = lax.axis_size("state")
    blocks_of_time = lax.axis_size("tm")
    V, S, A = pltpu.VMEM, pltpu.SMEM, pl.ANY

    matrix = jax.ShapeDtypeStruct((size, size), BF16)
    slab = jax.ShapeDtypeStruct((width, size), BF16)
    rows = jax.ShapeDtypeStruct((16, size), BF16)
    steps = jax.ShapeDtypeStruct((steps_here, size), F32)
    row = jax.ShapeDtypeStruct((1, size), F32)
    whole = pltpu.VMEM((size, size), BF16)

    half = steps_here // 2
    pieces = observations.shape[1] // side
    packed = call(
        drive_kernel, jax.ShapeDtypeStruct((half * width + 16, size), BF16), [V] * 4 + [A],
        [
            pltpu.VMEM((pieces, steps_here, side), F32),
            pltpu.VMEM((16, size), F32),
            pltpu.SemaphoreType.DMA((half,)),
        ],
        flops=10 ** 7, moved=2 ** 21,
    )(block_rows, block_cols, (precisions * observations).astype(BF16), blocks, transition[half:])
    early, late = ring_rounds(
        [transition[:half].reshape(half * width, size), packed],
        lambda r, i, found: (packed,) if (r, i) == (2, 0) else (),
    )
    two, slab2, second = call(
        functools.partial(two_kernel, count), (matrix, slab, matrix), [A] * count,
        [whole, pltpu.SemaphoreType.DMA((2 * count,))], flops=2 * size ** 3, moved=6 * size ** 2,
    )(*early)
    have = [r for r in range(count) if r not in (count // 2, count // 2 + 1)]
    three, third, fourth = call(
        functools.partial(three_kernel, count, have), (matrix, matrix, matrix), [V] + [A] * len(have),
        [pltpu.SemaphoreType.DMA((2 * len(have),))], flops=2 * size ** 3, moved=6 * size ** 2,
    )(two, *[late[r] for r in have])
    own, slab3, slab4, _, third, fourth, drive = call(
        functools.partial(four_kernel, count, have),
        (matrix, slab, slab, matrix, matrix, matrix, jax.ShapeDtypeStruct((16, size), F32)),
        [V] * 4 + [A if r in have else V for r in range(count)],
        [pltpu.VMEM((len(have), 16, size), BF16), pltpu.SemaphoreType.DMA((len(have),))],
        flops=2 * size ** 3, moved=6 * size ** 2, aliases={1: 3, 2: 4, 3: 5},
    )(two, three, third, fourth, *late)
    pairs = [(i, i + 1) for i in range(0, blocks_of_time, 2)]
    other = lax.ppermute(own, "tm", pairs)
    locals_, own_term = call(
        local_kernel, (steps, rows), [V] * 4, flops=96 * size ** 2, moved=6 * size ** 2
    )(drive, second, third, fourth)
    other_term = lax.ppermute(own_term, "tm", pairs)

    chips = blocks_of_time // 2
    firsts = chips // 2
    part = jax.ShapeDtypeStruct((size // 2, size), BF16)
    longer = jax.ShapeDtypeStruct((size // 2 + 16, size), BF16)
    blocks_here = (own, own_term, other, other_term)
    onward = [(2 * c + 1, 2 * c + 3) for c in range(firsts, chips, 2)]
    half_cost = dict(flops=size ** 3, moved=6 * size ** 2)
    begin = prior.reshape(1, size)
    came = begin
    for turn in range(firsts):
        if turn < DIRECT:
            begin, value = call(
                functools.partial(direct_kernel, turn), (row, row), [V] * 6,
                flops=64 * size ** 2, moved=4 * size ** 2,
            )(begin, came, *blocks_here)
        else:
            begin, value = call(
                functools.partial(hop_kernel, turn), (row, row), [V] * 4,
                flops=32 * size ** 2, moved=2 * size ** 2,
            )(begin, came, turned0, turned1)
        came = lax.ppermute(value, "tm", [(2 * turn + 1, 2 * turn + (3 if turn + 1 < firsts else 5))])
        if turn == 1:
            pair_blocks = after(blocks_here, value)
            turned0 = call(functools.partial(pair_kernel, 0), part, [V] * 4, **half_cost)(*pair_blocks)
            before0 = lax.ppermute(turned0, "tm", onward)
            turned1 = call(functools.partial(pair_kernel, 1), longer, [V] * 4, **half_cost)(*pair_blocks)
            before1 = lax.ppermute(turned1, "tm", onward)
        if turn == 3:
            maps, terms = call(
                ready_kernel,
                (jax.ShapeDtypeStruct((size, steps_here * width), BF16), jax.ShapeDtypeStruct((steps_here, width), F32)),
                [V] * 8, flops=size ** 3, moved=4 * size ** 2,
            )(other, other_term, locals_, value, early[0], slab2, slab3, slab4)
        if turn == 4:
            came = after(came, maps)
    double0 = call(functools.partial(double_kernel, 0, firsts), part, [V] * 3, **half_cost)(before0, turned0, turned1)
    double1 = call(functools.partial(double_kernel, 1, firsts), longer, [V] * 3, **half_cost)(before1, turned0, turned1)
    cames = [came]
    for chip in range(firsts + 1, chips - 1, 2):
        value = call(
            functools.partial(far_kernel, chip), row, [V] * 4, flops=32 * size ** 2, moved=2 * size ** 2
        )(came, value, double0, double1)
        came = lax.ppermute(value, "tm", [(2 * chip + 1, 2 * chip + 5)])
        cames.append(came)
    handed = lax.ppermute(value, "tm", [(2 * c - 1, 2 * c + 1) for c in range(firsts, chips, 2)])
    begin = call(
        functools.partial(final_kernel, firsts), row, [V] * (4 + len(cames)), flops=32 * size ** 2, moved=2 * size ** 2
    )(begin, handed, before0, before1, *cames)
    got = lax.ppermute(begin, "tm", [(b, a) for a, b in pairs])
    return call(
        out_kernel, jax.ShapeDtypeStruct((steps_here, width), F32), [V] * 4,
        flops=16 * size ** 2, moved=size ** 2,
    )(begin, got, maps, terms)


def solution(mesh):
    return jax.shard_map(
        shards,
        mesh=mesh,
        in_specs=(
            P("tm", None),
            P("tm", None),
            P("tm", "state", None, None),
            P("tm", "state"),
            P("tm", "state"),
            P("tm", "state", None),
            P(),
        ),
        out_specs=P("tm", "state"),
        check_vma=False,
    )
```

```python
import functools

import jax
import jax.numpy as jnp
from jax import lax
from jax.experimental import pallas as pl
from jax.experimental.pallas import tpu as pltpu
from jax.sharding import PartitionSpec as P

F32 = jnp.float32
BF16 = jnp.bfloat16
VMEM_LIMIT = 24 * 1024 * 1024
ROWS = 512


def three_parts(x):
    hi = x.astype(BF16).astype(F32)
    rest = x - hi
    mid = rest.astype(BF16).astype(F32)
    return hi, mid, rest - mid


def split_rows(x):
    hi, mid, lo = three_parts(x)
    row = lax.broadcasted_iota(jnp.int32, (16, x.shape[1]), 0)
    out = jnp.where(row == 0, hi, jnp.where(row == 1, mid, jnp.where(row == 2, lo, 0.0)))
    return out.astype(BF16)


def joined(rows):
    return jnp.sum(rows.astype(F32), axis=0, keepdims=True)


def times_t(x, *parts):
    left = split_rows(x)
    out = [
        joined(lax.dot_general(left, part, (((1,), (1,)), ((), ())), preferred_element_type=F32)) for part in parts
    ]
    return out[0] if len(out) == 1 else jnp.concatenate(out, axis=1)


def times(x, *parts):
    left = split_rows(x)
    return joined(product(left, *parts))


def product(left, *parts):
    rows = parts[0].shape[0]
    out = [
        jnp.dot(left[:, i * rows:(i + 1) * rows], part, preferred_element_type=F32) for i, part in enumerate(parts)
    ]
    return sum(out[1:], out[0])


def matmul(left_ref, right_ref, out_ref):
    def block(i, carry):
        at = pl.ds(pl.multiple_of(i * ROWS, ROWS), ROWS)
        out_ref[at, :] = jnp.dot(left_ref[at, :], right_ref[...], preferred_element_type=F32).astype(BF16)
        return carry

    lax.fori_loop(0, left_ref.shape[0] // ROWS, block, 0)


def core_here():
    return lax.rem(lax.axis_index("tm"), 2)


def chip_here():
    return lax.div(lax.axis_index("tm"), 2)


def drive_kernel(
    rows_ref, cols_ref, values_ref, blocks_ref, maps_ref, out_ref, weighted_ref, parts_ref, sems
):
    steps, count, side, _ = blocks_ref.shape
    later, width, size = maps_ref.shape
    copies = []
    for j in range(later):
        copies.append(pltpu.make_async_copy(maps_ref.at[j], out_ref.at[pl.ds(j * width, width), :], sems.at[j]))
        copies[j].start()
    weighted = values_ref[...].astype(F32)
    pieces = weighted_ref.shape[0]
    for r in range(pieces):
        weighted_ref[r] = weighted[:, r * side:(r + 1) * side]
    parts_ref[...] = jnp.zeros_like(parts_ref)
    piece = lax.broadcasted_iota(jnp.int32, (pieces, count), 0)
    column = lax.broadcasted_iota(jnp.int32, (size // side, count), 0)
    own = lax.broadcasted_iota(jnp.int32, (count, count * side), 0) == (
        lax.broadcasted_iota(jnp.int32, (count, count * side), 1) // side
    )
    for t in range(steps):
        chosen = (piece == rows_ref[t:t + 1, :]).astype(F32).astype(BF16)
        left = lax.dot_general(
            chosen, weighted_ref[:, t, :].astype(BF16), (((0,), (0,)), ((), ())), preferred_element_type=F32
        )
        left = jnp.concatenate([left] * count, axis=1)
        left = jnp.where(own, left, 0.0).astype(BF16)
        terms = jnp.dot(left, blocks_ref[t].reshape(count * side, side), preferred_element_type=F32)
        chosen = (column == cols_ref[t:t + 1, :]).astype(F32).astype(BF16)
        drive = sum(jnp.dot(chosen, part.astype(BF16), preferred_element_type=F32) for part in three_parts(terms))
        for i, part in enumerate(three_parts(drive)):
            for c in range(size // side):
                parts_ref[3 * t + i:3 * t + i + 1, c * side:(c + 1) * side] = part[c:c + 1, :]
    out_ref[later * width:, :] = parts_ref[...].astype(BF16)
    for copy in copies:
        copy.wait()


def rows_of(r, width, count):
    owner = lax.rem(lax.axis_index("state") + r + core_here() * (count - 2 * r), count)
    return pl.ds(pl.multiple_of(owner * width, width), width)


def fetched(count, pieces, j, whole_ref, sems, first):
    width = whole_ref.shape[0] // count
    copies = []
    for i, (r, piece) in enumerate(pieces):
        copy = pltpu.make_async_copy(
            piece.at[pl.ds(j * width, width), :], whole_ref.at[rows_of(r, width, count), :], sems.at[first + i]
        )
        copy.start()
        copies.append(copy)
    return copies


def two_kernel(count, *refs):
    pieces, (two_ref, slab_ref, next_ref, one_ref, sems) = list(enumerate(refs[:count])), refs[count:]
    width = slab_ref.shape[0]
    place = lax.axis_index("state")
    ones = fetched(count, pieces, 0, one_ref, sems, 0)
    nexts = fetched(count, pieces, 1, next_ref, sems, count)
    for copy in ones + nexts:
        copy.wait()
    matmul(next_ref, one_ref, two_ref)
    slab_ref[...] = two_ref[pl.ds(pl.multiple_of(place * width, width), width), :]


def three_kernel(count, have, two_ref, *refs):
    pieces = list(zip(have, refs[:len(have)]))
    three_ref, third_ref, fourth_ref, sems = refs[len(have):]
    width = third_ref.shape[0] // count
    copies = fetched(count, pieces, 0, third_ref, sems, 0)
    copies += fetched(count, pieces, 1, fourth_ref, sems, len(have))
    for copy in copies:
        copy.wait()
    for r in have:
        at = rows_of(r, width, count)
        three_ref[at, :] = jnp.dot(third_ref[at, :], two_ref[...], preferred_element_type=F32).astype(BF16)


def four_kernel(count, have, two_ref, threes_ref, thirds_ref, fourths_ref, *refs):
    pieces = refs[:count]
    four_ref, slab3_ref, slab4_ref, three_ref, third_ref, fourth_ref, drive_ref, parts_ref, sems = refs[count:]
    width = slab3_ref.shape[0]
    parts = []
    for i, r in enumerate(have):
        parts.append(pltpu.make_async_copy(pieces[r].at[pl.ds(2 * width, 16), :], parts_ref.at[i], sems.at[i]))
        parts[i].start()
    drive = jnp.zeros(drive_ref.shape, F32)
    for r in range(count):
        if r not in have:
            at = rows_of(r, width, count)
            third_ref[at, :] = pieces[r][:width, :]
            fourth_ref[at, :] = pieces[r][width:2 * width, :]
            three_ref[at, :] = jnp.dot(pieces[r][:width, :], two_ref[...], preferred_element_type=F32).astype(BF16)
            drive += pieces[r][2 * width:, :].astype(F32)
    matmul(fourth_ref, three_ref, four_ref)
    mine = pl.ds(pl.multiple_of(lax.axis_index("state") * width, width), width)
    slab3_ref[...] = three_ref[mine, :]
    slab4_ref[...] = four_ref[mine, :]
    for copy in parts:
        copy.wait()
    drive_ref[...] = drive + jnp.sum(parts_ref[...].astype(F32), axis=0)


def local_kernel(drive_ref, second_ref, third_ref, fourth_ref, locals_ref, term_ref):
    local = joined(drive_ref[0:3, :])
    locals_ref[0:1, :] = local
    for j, map_ref in enumerate((second_ref, third_ref, fourth_ref)):
        local = times_t(local, map_ref[...]) + joined(drive_ref[3 * j + 3:3 * j + 6, :])
        locals_ref[j + 1:j + 2, :] = local
    term_ref[...] = split_rows(local)


DIRECT = 2


def pair_kernel(half, own_ref, own_term_ref, other_ref, other_term_ref, turned_ref):
    rows = own_ref.shape[0] // 2
    at = slice(half * rows, (half + 1) * rows)

    @pl.when(jnp.logical_and(core_here() != 0, chip_here() >= DIRECT))
    def _():
        for i in range(2):
            out = jnp.dot(own_ref[i * rows:(i + 1) * rows, :], other_ref[:, at], preferred_element_type=F32)
            turned_ref[:rows, i * rows:(i + 1) * rows] = out.T.astype(BF16)
        if half == 1:
            term = times_t(joined(other_term_ref[...]), own_ref[...]) + joined(own_term_ref[...])
            turned_ref[rows:, :] = split_rows(term)


def applied(x, turned0_ref, turned1_ref):
    rows = turned0_ref.shape[0]
    return times(x, turned0_ref[...], turned1_ref[:rows, :]) + joined(turned1_ref[rows:, :])


def direct_kernel(turn, begin_ref, came_ref, own_ref, own_term_ref, other_ref, other_term_ref, held_ref, value_ref):
    held_ref[...] = begin_ref[...]
    value_ref[...] = begin_ref[...]

    @pl.when(lax.axis_index("tm") == 2 * turn + 1)
    def _():
        begin = came_ref[...]
        held_ref[...] = begin
        between = times_t(begin, other_ref[...]) + joined(other_term_ref[...])
        value_ref[...] = times_t(between, own_ref[...]) + joined(own_term_ref[...])


def hop_kernel(turn, begin_ref, came_ref, turned0_ref, turned1_ref, held_ref, value_ref):
    here = lax.axis_index("tm") == 2 * turn + 1

    @pl.when(here)
    def _():
        begin = came_ref[...]
        held_ref[...] = begin
        value_ref[...] = applied(begin, turned0_ref, turned1_ref)

    @pl.when(jnp.logical_not(here))
    def _():
        held_ref[...] = begin_ref[...]
        value_ref[...] = begin_ref[...]


def double_kernel(half, firsts, came_ref, turned0_ref, turned1_ref, double_ref):
    rows = turned0_ref.shape[0]
    chip = chip_here()

    @pl.when((core_here() != 0) & (chip > firsts) & (lax.rem(chip, 2) == 1) & (chip < 2 * firsts - 1))
    def _():
        double_ref[:rows, :] = product(came_ref[:rows, :], turned0_ref[...], turned1_ref[:rows, :]).astype(BF16)
        if half == 1:
            double_ref[rows:, :] = split_rows(applied(joined(came_ref[rows:, :]), turned0_ref, turned1_ref))


def far_kernel(chip, came_ref, before_ref, double0_ref, double1_ref, value_ref):
    here = lax.axis_index("tm") == 2 * chip + 1

    @pl.when(here)
    def _():
        value_ref[...] = applied(came_ref[...], double0_ref, double1_ref)

    @pl.when(jnp.logical_not(here))
    def _():
        value_ref[...] = before_ref[...]


def final_kernel(firsts, held_ref, handed_ref, map0_ref, map1_ref, *refs):
    cames, begin_ref = refs[:-1], refs[-1]
    chip = chip_here()
    handed = jnp.logical_and(chip >= firsts, lax.rem(chip, 2) == 0)
    begin_ref[...] = jnp.where(handed, handed_ref[...], held_ref[...])
    for i, came_ref in enumerate(cames):
        @pl.when(lax.axis_index("tm") == 2 * (firsts + 1 + 2 * i) + 1)
        def _():
            begin_ref[...] = applied(came_ref[...], map0_ref, map1_ref)


def ready_kernel(other_ref, other_term_ref, locals_ref, after_ref, *refs):
    slabs, (maps_ref, terms_ref) = refs[:-2], refs[-2:]
    width, size = slabs[1].shape
    mine = pl.ds(pl.multiple_of(lax.axis_index("state") * width, width), width)

    @pl.when(core_here() == 0)
    def _():
        for j, slab_ref in enumerate(slabs):
            maps_ref[:, j * width:(j + 1) * width] = slab_ref[:width, :].astype(F32).T.astype(BF16)
            terms_ref[j:j + 1, :] = locals_ref[j:j + 1, mine]

    @pl.when(core_here() != 0)
    def _():
        for j, slab_ref in enumerate(slabs):
            at = slice(j * width, (j + 1) * width)
            out = jnp.dot(slab_ref[:width, :], other_ref[...], preferred_element_type=F32)
            maps_ref[:, at] = out.T.astype(BF16)
            term = times_t(joined(other_term_ref[...]), slab_ref[:width, :])
            terms_ref[j:j + 1, :] = term + locals_ref[j:j + 1, mine]


def out_kernel(begin_ref, got_ref, maps_ref, terms_ref, out_ref):
    steps, width = out_ref.shape
    begin = jnp.where(core_here() == 0, got_ref[...], begin_ref[...])
    row = times(begin, maps_ref[...])
    for j in range(steps):
        out_ref[j:j + 1, :] = row[:, j * width:(j + 1) * width] + terms_ref[j:j + 1, :]


def call(kernel, out_shape, spaces, scratch=(), flops=0, moved=0, aliases={}):
    return pl.pallas_call(
        kernel,
        out_shape=out_shape,
        in_specs=[pl.BlockSpec(memory_space=s) for s in spaces],
        out_specs=jax.tree.map(lambda _: pl.BlockSpec(memory_space=pltpu.VMEM), out_shape),
        scratch_shapes=list(scratch),
        input_output_aliases=aliases,
        compiler_params=pltpu.CompilerParams(vmem_limit_bytes=VMEM_LIMIT),
        cost_estimate=pl.CostEstimate(flops=flops, bytes_accessed=moved, transcendentals=0),
    )


def after(value, *needed):
    return lax.optimization_barrier((value, needed))[0]


def ring_rounds(parts, needed):
    lines, count = lax.axis_size("tm"), lax.axis_size("state")
    forward = [(b * count + i, b * count + (i + 1 - 2 * (b % 2)) % count) for b in range(lines) for i in range(count)]
    backward = [(there, here) for here, there in forward]
    half = count // 2
    found = [{0: part} for part in parts]
    for r in range(1, half + 1):
        for i, pieces in enumerate(found):
            left, right = pieces[(count - r + 1) % count], pieces[r - 1]
            more = needed(r, i, found)
            if more:
                left, right = after((left, right), *more)
            if r < half or i % 2 == 0:
                pieces[count - r] = lax.ppermute(left, ("tm", "state"), forward)
            if r < half or i % 2 == 1:
                pieces[r] = lax.ppermute(right, ("tm", "state"), backward)
    return [[pieces[r] for r in range(count)] for pieces in found]


def shards(observations, precisions, blocks, block_rows, block_cols, transition, prior):
    steps_here, width, size = transition.shape
    side = blocks.shape[2]
    count = lax.axis_size("state")
    blocks_of_time = lax.axis_size("tm")
    V, S, A = pltpu.VMEM, pltpu.SMEM, pl.ANY

    matrix = jax.ShapeDtypeStruct((size, size), BF16)
    slab = jax.ShapeDtypeStruct((width, size), BF16)
    rows = jax.ShapeDtypeStruct((16, size), BF16)
    steps = jax.ShapeDtypeStruct((steps_here, size), F32)
    row = jax.ShapeDtypeStruct((1, size), F32)
    whole = pltpu.VMEM((size, size), BF16)

    half = steps_here // 2
    pieces = observations.shape[1] // side
    packed = call(
        drive_kernel, jax.ShapeDtypeStruct((half * width + 16, size), BF16), [V] * 4 + [A],
        [
            pltpu.VMEM((pieces, steps_here, side), F32),
            pltpu.VMEM((16, size), F32),
            pltpu.SemaphoreType.DMA((half,)),
        ],
        flops=10 ** 7, moved=2 ** 21,
    )(block_rows, block_cols, (precisions * observations).astype(BF16), blocks, transition[half:])
    early, late = ring_rounds(
        [transition[:half].reshape(half * width, size), packed],
        lambda r, i, found: (packed,) if (r, i) == (2, 0) else (),
    )
    two, slab2, second = call(
        functools.partial(two_kernel, count), (matrix, slab, matrix), [A] * count,
        [whole, pltpu.SemaphoreType.DMA((2 * count,))], flops=2 * size ** 3, moved=6 * size ** 2,
    )(*early)
    have = [r for r in range(count) if r not in (count // 2, count // 2 + 1)]
    three, third, fourth = call(
        functools.partial(three_kernel, count, have), (matrix, matrix, matrix), [V] + [A] * len(have),
        [pltpu.SemaphoreType.DMA((2 * len(have),))], flops=2 * size ** 3, moved=6 * size ** 2,
    )(two, *[late[r] for r in have])
    own, slab3, slab4, _, third, fourth, drive = call(
        functools.partial(four_kernel, count, have),
        (matrix, slab, slab, matrix, matrix, matrix, jax.ShapeDtypeStruct((16, size), F32)),
        [V] * 4 + [A if r in have else V for r in range(count)],
        [pltpu.VMEM((len(have), 16, size), BF16), pltpu.SemaphoreType.DMA((len(have),))],
        flops=2 * size ** 3, moved=6 * size ** 2, aliases={1: 3, 2: 4, 3: 5},
    )(two, three, third, fourth, *late)
    pairs = [(i, i + 1) for i in range(0, blocks_of_time, 2)]
    other = lax.ppermute(own, "tm", pairs)
    locals_, own_term = call(
        local_kernel, (steps, rows), [V] * 4, flops=96 * size ** 2, moved=6 * size ** 2
    )(drive, second, third, fourth)
    other_term = lax.ppermute(own_term, "tm", pairs)

    chips = blocks_of_time // 2
    firsts = chips // 2
    part = jax.ShapeDtypeStruct((size // 2, size), BF16)
    longer = jax.ShapeDtypeStruct((size // 2 + 16, size), BF16)
    blocks_here = (own, own_term, other, other_term)
    onward = [(2 * c + 1, 2 * c + 3) for c in range(firsts, chips, 2)]
    half_cost = dict(flops=size ** 3, moved=6 * size ** 2)
    turned0 = call(functools.partial(pair_kernel, 0), part, [V] * 4, **half_cost)(*blocks_here)
    before0 = lax.ppermute(turned0, "tm", onward)
    turned1 = call(functools.partial(pair_kernel, 1), longer, [V] * 4, **half_cost)(*blocks_here)
    before1 = lax.ppermute(turned1, "tm", onward)

    begin = after(prior.reshape(1, size), turned1)
    came = begin
    for turn in range(firsts):
        if turn < DIRECT:
            begin, value = call(
                functools.partial(direct_kernel, turn), (row, row), [V] * 6,
                flops=64 * size ** 2, moved=4 * size ** 2,
            )(begin, came, *blocks_here)
        else:
            begin, value = call(
                functools.partial(hop_kernel, turn), (row, row), [V] * 4,
                flops=32 * size ** 2, moved=2 * size ** 2,
            )(begin, came, turned0, turned1)
        came = lax.ppermute(value, "tm", [(2 * turn + 1, 2 * turn + (3 if turn + 1 < firsts else 5))])
        if turn == 3:
            maps, terms = call(
                ready_kernel,
                (jax.ShapeDtypeStruct((size, steps_here * width), BF16), jax.ShapeDtypeStruct((steps_here, width), F32)),
                [V] * 8, flops=size ** 3, moved=4 * size ** 2,
            )(other, other_term, locals_, value, early[0], slab2, slab3, slab4)
        if turn == 4:
            came = after(came, maps)
    double0 = call(functools.partial(double_kernel, 0, firsts), part, [V] * 3, **half_cost)(before0, turned0, turned1)
    double1 = call(functools.partial(double_kernel, 1, firsts), longer, [V] * 3, **half_cost)(before1, turned0, turned1)
    cames = [came]
    for chip in range(firsts + 1, chips - 1, 2):
        value = call(
            functools.partial(far_kernel, chip), row, [V] * 4, flops=32 * size ** 2, moved=2 * size ** 2
        )(came, value, double0, double1)
        came = lax.ppermute(value, "tm", [(2 * chip + 1, 2 * chip + 5)])
        cames.append(came)
    handed = lax.ppermute(value, "tm", [(2 * c - 1, 2 * c + 1) for c in range(firsts, chips, 2)])
    begin = call(
        functools.partial(final_kernel, firsts), row, [V] * (4 + len(cames)), flops=32 * size ** 2, moved=2 * size ** 2
    )(begin, handed, before0, before1, *cames)
    got = lax.ppermute(begin, "tm", [(b, a) for a, b in pairs])
    return call(
        out_kernel, jax.ShapeDtypeStruct((steps_here, width), F32), [V] * 4,
        flops=16 * size ** 2, moved=size ** 2,
    )(begin, got, maps, terms)


def solution(mesh):
    return jax.shard_map(
        shards,
        mesh=mesh,
        in_specs=(
            P("tm", None),
            P("tm", None),
            P("tm", "state", None, None),
            P("tm", "state"),
            P("tm", "state"),
            P("tm", "state", None),
            P(),
        ),
        out_specs=P("tm", "state"),
        check_vma=False,
    )
```

```python
import functools

import jax
import jax.numpy as jnp
from jax import lax
from jax.experimental import pallas as pl
from jax.experimental.pallas import tpu as pltpu
from jax.sharding import PartitionSpec as P

F32 = jnp.float32
BF16 = jnp.bfloat16
VMEM_LIMIT = 24 * 1024 * 1024
ROWS = 512


def three_parts(x):
    hi = x.astype(BF16).astype(F32)
    rest = x - hi
    mid = rest.astype(BF16).astype(F32)
    return hi, mid, rest - mid


def split_rows(x):
    hi, mid, lo = three_parts(x)
    row = lax.broadcasted_iota(jnp.int32, (16, x.shape[1]), 0)
    out = jnp.where(row == 0, hi, jnp.where(row == 1, mid, jnp.where(row == 2, lo, 0.0)))
    return out.astype(BF16)


def joined(rows):
    return jnp.sum(rows.astype(F32), axis=0, keepdims=True)


def times_t(x, *parts):
    left = split_rows(x)
    out = [
        joined(lax.dot_general(left, part, (((1,), (1,)), ((), ())), preferred_element_type=F32)) for part in parts
    ]
    return out[0] if len(out) == 1 else jnp.concatenate(out, axis=1)


def times(x, *parts):
    left = split_rows(x)
    return joined(product(left, *parts))


def product(left, *parts):
    rows = parts[0].shape[0]
    out = [
        jnp.dot(left[:, i * rows:(i + 1) * rows], part, preferred_element_type=F32) for i, part in enumerate(parts)
    ]
    return sum(out[1:], out[0])


def matmul(left_ref, right_ref, out_ref):
    def block(i, carry):
        at = pl.ds(pl.multiple_of(i * ROWS, ROWS), ROWS)
        out_ref[at, :] = jnp.dot(left_ref[at, :], right_ref[...], preferred_element_type=F32).astype(BF16)
        return carry

    lax.fori_loop(0, left_ref.shape[0] // ROWS, block, 0)


def core_here():
    return lax.rem(lax.axis_index("tm"), 2)


def chip_here():
    return lax.div(lax.axis_index("tm"), 2)


def drive_kernel(
    rows_ref, cols_ref, values_ref, blocks_ref, maps_ref, out_ref, weighted_ref, parts_ref, sems
):
    steps, count, side, _ = blocks_ref.shape
    later, width, size = maps_ref.shape
    copies = []
    for j in range(later):
        copies.append(pltpu.make_async_copy(maps_ref.at[j], out_ref.at[pl.ds(j * width, width), :], sems.at[j]))
        copies[j].start()
    weighted = values_ref[...].astype(F32)
    pieces = weighted_ref.shape[0]
    for r in range(pieces):
        weighted_ref[r] = weighted[:, r * side:(r + 1) * side]
    parts_ref[...] = jnp.zeros_like(parts_ref)
    piece = lax.broadcasted_iota(jnp.int32, (pieces, count), 0)
    column = lax.broadcasted_iota(jnp.int32, (size // side, count), 0)
    own = lax.broadcasted_iota(jnp.int32, (count, count * side), 0) == (
        lax.broadcasted_iota(jnp.int32, (count, count * side), 1) // side
    )
    for t in range(steps):
        chosen = (piece == rows_ref[t:t + 1, :]).astype(F32).astype(BF16)
        left = lax.dot_general(
            chosen, weighted_ref[:, t, :].astype(BF16), (((0,), (0,)), ((), ())), preferred_element_type=F32
        )
        left = jnp.concatenate([left] * count, axis=1)
        left = jnp.where(own, left, 0.0).astype(BF16)
        terms = jnp.dot(left, blocks_ref[t].reshape(count * side, side), preferred_element_type=F32)
        chosen = (column == cols_ref[t:t + 1, :]).astype(F32).astype(BF16)
        drive = sum(jnp.dot(chosen, part.astype(BF16), preferred_element_type=F32) for part in three_parts(terms))
        for i, part in enumerate(three_parts(drive)):
            for c in range(size // side):
                parts_ref[3 * t + i:3 * t + i + 1, c * side:(c + 1) * side] = part[c:c + 1, :]
    out_ref[later * width:, :] = parts_ref[...].astype(BF16)
    for copy in copies:
        copy.wait()


def rows_of(r, width, count):
    owner = lax.rem(lax.axis_index("state") + r + core_here() * (count - 2 * r), count)
    return pl.ds(pl.multiple_of(owner * width, width), width)


def fetched(count, pieces, j, whole_ref, sems, first):
    width = whole_ref.shape[0] // count
    copies = []
    for i, (r, piece) in enumerate(pieces):
        copy = pltpu.make_async_copy(
            piece.at[pl.ds(j * width, width), :], whole_ref.at[rows_of(r, width, count), :], sems.at[first + i]
        )
        copy.start()
        copies.append(copy)
    return copies


def two_kernel(count, *refs):
    pieces, (two_ref, slab_ref, next_ref, one_ref, sems) = list(enumerate(refs[:count])), refs[count:]
    width = slab_ref.shape[0]
    place = lax.axis_index("state")
    ones = fetched(count, pieces, 0, one_ref, sems, 0)
    nexts = fetched(count, pieces, 1, next_ref, sems, count)
    for copy in ones + nexts:
        copy.wait()
    matmul(next_ref, one_ref, two_ref)
    slab_ref[...] = two_ref[pl.ds(pl.multiple_of(place * width, width), width), :]


def three_kernel(count, have, two_ref, *refs):
    pieces = list(zip(have, refs[:len(have)]))
    three_ref, third_ref, fourth_ref, sems = refs[len(have):]
    width = third_ref.shape[0] // count
    copies = fetched(count, pieces, 0, third_ref, sems, 0)
    copies += fetched(count, pieces, 1, fourth_ref, sems, len(have))
    for copy in copies:
        copy.wait()
    for r in have:
        at = rows_of(r, width, count)
        three_ref[at, :] = jnp.dot(third_ref[at, :], two_ref[...], preferred_element_type=F32).astype(BF16)


def four_kernel(count, have, two_ref, threes_ref, thirds_ref, fourths_ref, *refs):
    pieces = refs[:count]
    four_ref, slab3_ref, slab4_ref, three_ref, third_ref, fourth_ref, drive_ref, parts_ref, sems = refs[count:]
    width = slab3_ref.shape[0]
    parts = []
    for i, r in enumerate(have):
        parts.append(pltpu.make_async_copy(pieces[r].at[pl.ds(2 * width, 16), :], parts_ref.at[i], sems.at[i]))
        parts[i].start()
    drive = jnp.zeros(drive_ref.shape, F32)
    for r in range(count):
        if r not in have:
            at = rows_of(r, width, count)
            third_ref[at, :] = pieces[r][:width, :]
            fourth_ref[at, :] = pieces[r][width:2 * width, :]
            three_ref[at, :] = jnp.dot(pieces[r][:width, :], two_ref[...], preferred_element_type=F32).astype(BF16)
            drive += pieces[r][2 * width:, :].astype(F32)
    mine = pl.ds(pl.multiple_of(lax.axis_index("state") * width, width), width)
    slab3_ref[...] = three_ref[mine, :]

    @pl.when(core_here() == 0)
    def _():
        matmul(fourth_ref, three_ref, four_ref)
        slab4_ref[...] = four_ref[mine, :]

    for copy in parts:
        copy.wait()
    drive_ref[...] = drive + jnp.sum(parts_ref[...].astype(F32), axis=0)


def second_kernel(three_ref, fourth_ref, four_ref, slab4_ref):
    width = slab4_ref.shape[0]

    @pl.when(core_here() != 0)
    def _():
        matmul(fourth_ref, three_ref, four_ref)
        slab4_ref[...] = four_ref[pl.ds(pl.multiple_of(lax.axis_index("state") * width, width), width), :]


def local_kernel(drive_ref, second_ref, third_ref, fourth_ref, locals_ref, term_ref):
    local = joined(drive_ref[0:3, :])
    locals_ref[0:1, :] = local
    for j, map_ref in enumerate((second_ref, third_ref, fourth_ref)):
        local = times_t(local, map_ref[...]) + joined(drive_ref[3 * j + 3:3 * j + 6, :])
        locals_ref[j + 1:j + 2, :] = local
    term_ref[...] = split_rows(local)


DIRECT = 2


def pair_kernel(half, own_ref, own_term_ref, other_ref, other_term_ref, turned_ref):
    rows = own_ref.shape[0] // 2
    at = slice(half * rows, (half + 1) * rows)

    @pl.when(jnp.logical_and(core_here() != 0, chip_here() >= DIRECT))
    def _():
        for i in range(2):
            out = jnp.dot(own_ref[i * rows:(i + 1) * rows, :], other_ref[:, at], preferred_element_type=F32)
            turned_ref[:rows, i * rows:(i + 1) * rows] = out.T.astype(BF16)
        if half == 1:
            term = times_t(joined(other_term_ref[...]), own_ref[...]) + joined(own_term_ref[...])
            turned_ref[rows:, :] = split_rows(term)


def applied(x, turned0_ref, turned1_ref):
    rows = turned0_ref.shape[0]
    return times(x, turned0_ref[...], turned1_ref[:rows, :]) + joined(turned1_ref[rows:, :])


def direct_kernel(turn, begin_ref, came_ref, own_ref, own_term_ref, other_ref, other_term_ref, held_ref, value_ref):
    held_ref[...] = begin_ref[...]
    value_ref[...] = begin_ref[...]

    @pl.when(lax.axis_index("tm") == 2 * turn + 1)
    def _():
        begin = came_ref[...]
        held_ref[...] = begin
        between = times_t(begin, other_ref[...]) + joined(other_term_ref[...])
        value_ref[...] = times_t(between, own_ref[...]) + joined(own_term_ref[...])


def hop_kernel(turn, begin_ref, came_ref, turned0_ref, turned1_ref, held_ref, value_ref):
    here = lax.axis_index("tm") == 2 * turn + 1

    @pl.when(here)
    def _():
        begin = came_ref[...]
        held_ref[...] = begin
        value_ref[...] = applied(begin, turned0_ref, turned1_ref)

    @pl.when(jnp.logical_not(here))
    def _():
        held_ref[...] = begin_ref[...]
        value_ref[...] = begin_ref[...]


def double_kernel(half, firsts, came_ref, turned0_ref, turned1_ref, double_ref):
    rows = turned0_ref.shape[0]
    chip = chip_here()

    @pl.when((core_here() != 0) & (chip > firsts) & (lax.rem(chip, 2) == 1) & (chip < 2 * firsts - 1))
    def _():
        double_ref[:rows, :] = product(came_ref[:rows, :], turned0_ref[...], turned1_ref[:rows, :]).astype(BF16)
        if half == 1:
            double_ref[rows:, :] = split_rows(applied(joined(came_ref[rows:, :]), turned0_ref, turned1_ref))


def far_kernel(chip, came_ref, before_ref, double0_ref, double1_ref, value_ref):
    here = lax.axis_index("tm") == 2 * chip + 1

    @pl.when(here)
    def _():
        value_ref[...] = applied(came_ref[...], double0_ref, double1_ref)

    @pl.when(jnp.logical_not(here))
    def _():
        value_ref[...] = before_ref[...]


def final_kernel(firsts, held_ref, handed_ref, map0_ref, map1_ref, *refs):
    cames, begin_ref = refs[:-1], refs[-1]
    chip = chip_here()
    handed = jnp.logical_and(chip >= firsts, lax.rem(chip, 2) == 0)
    begin_ref[...] = jnp.where(handed, handed_ref[...], held_ref[...])
    for i, came_ref in enumerate(cames):
        @pl.when(lax.axis_index("tm") == 2 * (firsts + 1 + 2 * i) + 1)
        def _():
            begin_ref[...] = applied(came_ref[...], map0_ref, map1_ref)


def ready_kernel(other_ref, other_term_ref, locals_ref, after_ref, *refs):
    slabs, (second_ref, maps_ref, terms_ref) = refs[:-3], refs[-3:]
    width, size = slabs[1].shape
    mine = pl.ds(pl.multiple_of(lax.axis_index("state") * width, width), width)

    @pl.when(core_here() == 0)
    def _():
        for j, slab_ref in enumerate(slabs):
            maps_ref[:, j * width:(j + 1) * width] = slab_ref[:width, :].astype(F32).T.astype(BF16)
            terms_ref[j:j + 1, :] = locals_ref[j:j + 1, mine]

    @pl.when(core_here() != 0)
    def _():
        for j, slab_ref in enumerate(slabs[:-1] + (second_ref,)):
            at = slice(j * width, (j + 1) * width)
            out = jnp.dot(slab_ref[:width, :], other_ref[...], preferred_element_type=F32)
            maps_ref[:, at] = out.T.astype(BF16)
            term = times_t(joined(other_term_ref[...]), slab_ref[:width, :])
            terms_ref[j:j + 1, :] = term + locals_ref[j:j + 1, mine]


def out_kernel(begin_ref, got_ref, maps_ref, terms_ref, out_ref):
    steps, width = out_ref.shape
    begin = jnp.where(core_here() == 0, got_ref[...], begin_ref[...])
    row = times(begin, maps_ref[...])
    for j in range(steps):
        out_ref[j:j + 1, :] = row[:, j * width:(j + 1) * width] + terms_ref[j:j + 1, :]


def call(kernel, out_shape, spaces, scratch=(), flops=0, moved=0, aliases={}):
    return pl.pallas_call(
        kernel,
        out_shape=out_shape,
        in_specs=[pl.BlockSpec(memory_space=s) for s in spaces],
        out_specs=jax.tree.map(lambda _: pl.BlockSpec(memory_space=pltpu.VMEM), out_shape),
        scratch_shapes=list(scratch),
        input_output_aliases=aliases,
        compiler_params=pltpu.CompilerParams(vmem_limit_bytes=VMEM_LIMIT),
        cost_estimate=pl.CostEstimate(flops=flops, bytes_accessed=moved, transcendentals=0),
    )


def after(value, *needed):
    return lax.optimization_barrier((value, needed))[0]


def ring_rounds(parts, needed):
    lines, count = lax.axis_size("tm"), lax.axis_size("state")
    forward = [(b * count + i, b * count + (i + 1 - 2 * (b % 2)) % count) for b in range(lines) for i in range(count)]
    backward = [(there, here) for here, there in forward]
    half = count // 2
    found = [{0: part} for part in parts]
    for r in range(1, half + 1):
        for i, pieces in enumerate(found):
            left, right = pieces[(count - r + 1) % count], pieces[r - 1]
            more = needed(r, i, found)
            if more:
                left, right = after((left, right), *more)
            if r < half or i % 2 == 0:
                pieces[count - r] = lax.ppermute(left, ("tm", "state"), forward)
            if r < half or i % 2 == 1:
                pieces[r] = lax.ppermute(right, ("tm", "state"), backward)
    return [[pieces[r] for r in range(count)] for pieces in found]


def shards(observations, precisions, blocks, block_rows, block_cols, transition, prior):
    steps_here, width, size = transition.shape
    side = blocks.shape[2]
    count = lax.axis_size("state")
    blocks_of_time = lax.axis_size("tm")
    V, S, A = pltpu.VMEM, pltpu.SMEM, pl.ANY

    matrix = jax.ShapeDtypeStruct((size, size), BF16)
    slab = jax.ShapeDtypeStruct((width, size), BF16)
    rows = jax.ShapeDtypeStruct((16, size), BF16)
    steps = jax.ShapeDtypeStruct((steps_here, size), F32)
    row = jax.ShapeDtypeStruct((1, size), F32)
    whole = pltpu.VMEM((size, size), BF16)

    half = steps_here // 2
    pieces = observations.shape[1] // side
    packed = call(
        drive_kernel, jax.ShapeDtypeStruct((half * width + 16, size), BF16), [V] * 4 + [A],
        [
            pltpu.VMEM((pieces, steps_here, side), F32),
            pltpu.VMEM((16, size), F32),
            pltpu.SemaphoreType.DMA((half,)),
        ],
        flops=10 ** 7, moved=2 ** 21,
    )(block_rows, block_cols, (precisions * observations).astype(BF16), blocks, transition[half:])
    early, late = ring_rounds(
        [transition[:half].reshape(half * width, size), packed],
        lambda r, i, found: (packed,) if (r, i) == (2, 0) else (),
    )
    two, slab2, second = call(
        functools.partial(two_kernel, count), (matrix, slab, matrix), [A] * count,
        [whole, pltpu.SemaphoreType.DMA((2 * count,))], flops=2 * size ** 3, moved=6 * size ** 2,
    )(*early)
    have = [r for r in range(count) if r not in (count // 2, count // 2 + 1)]
    three, third, fourth = call(
        functools.partial(three_kernel, count, have), (matrix, matrix, matrix), [V] + [A] * len(have),
        [pltpu.SemaphoreType.DMA((2 * len(have),))], flops=2 * size ** 3, moved=6 * size ** 2,
    )(two, *[late[r] for r in have])
    sent, slab3, slab4, three, third, fourth, drive = call(
        functools.partial(four_kernel, count, have),
        (matrix, slab, slab, matrix, matrix, matrix, jax.ShapeDtypeStruct((16, size), F32)),
        [V] * 4 + [A if r in have else V for r in range(count)],
        [pltpu.VMEM((len(have), 16, size), BF16), pltpu.SemaphoreType.DMA((len(have),))],
        flops=2 * size ** 3, moved=6 * size ** 2, aliases={1: 3, 2: 4, 3: 5},
    )(two, three, third, fourth, *late)
    pairs = [(i, i + 1) for i in range(0, blocks_of_time, 2)]
    other = lax.ppermute(sent, "tm", pairs)
    own, slab5 = call(second_kernel, (matrix, slab), [V] * 2, flops=2 * size ** 3, moved=6 * size ** 2)(three, fourth)
    locals_, own_term = call(
        local_kernel, (steps, rows), [V] * 4, flops=96 * size ** 2, moved=6 * size ** 2
    )(drive, second, third, fourth)
    other_term = lax.ppermute(own_term, "tm", pairs)

    chips = blocks_of_time // 2
    firsts = chips // 2
    part = jax.ShapeDtypeStruct((size // 2, size), BF16)
    longer = jax.ShapeDtypeStruct((size // 2 + 16, size), BF16)
    blocks_here = (own, own_term, other, other_term)
    onward = [(2 * c + 1, 2 * c + 3) for c in range(firsts, chips, 2)]
    half_cost = dict(flops=size ** 3, moved=6 * size ** 2)
    turned0 = call(functools.partial(pair_kernel, 0), part, [V] * 4, **half_cost)(*blocks_here)
    before0 = lax.ppermute(turned0, "tm", onward)
    turned1 = call(functools.partial(pair_kernel, 1), longer, [V] * 4, **half_cost)(*blocks_here)
    before1 = lax.ppermute(turned1, "tm", onward)

    begin = after(prior.reshape(1, size), turned1)
    came = begin
    for turn in range(firsts):
        if turn < DIRECT:
            begin, value = call(
                functools.partial(direct_kernel, turn), (row, row), [V] * 6,
                flops=64 * size ** 2, moved=4 * size ** 2,
            )(begin, came, *blocks_here)
        else:
            begin, value = call(
                functools.partial(hop_kernel, turn), (row, row), [V] * 4,
                flops=32 * size ** 2, moved=2 * size ** 2,
            )(begin, came, turned0, turned1)
        came = lax.ppermute(value, "tm", [(2 * turn + 1, 2 * turn + (3 if turn + 1 < firsts else 5))])
        if turn == 3:
            maps, terms = call(
                ready_kernel,
                (jax.ShapeDtypeStruct((size, steps_here * width), BF16), jax.ShapeDtypeStruct((steps_here, width), F32)),
                [V] * 9, flops=size ** 3, moved=4 * size ** 2,
            )(other, other_term, locals_, value, early[0], slab2, slab3, slab4, slab5)
        if turn == 4:
            came = after(came, maps)
    double0 = call(functools.partial(double_kernel, 0, firsts), part, [V] * 3, **half_cost)(before0, turned0, turned1)
    double1 = call(functools.partial(double_kernel, 1, firsts), longer, [V] * 3, **half_cost)(before1, turned0, turned1)
    cames = [came]
    for chip in range(firsts + 1, chips - 1, 2):
        value = call(
            functools.partial(far_kernel, chip), row, [V] * 4, flops=32 * size ** 2, moved=2 * size ** 2
        )(came, value, double0, double1)
        came = lax.ppermute(value, "tm", [(2 * chip + 1, 2 * chip + 5)])
        cames.append(came)
    handed = lax.ppermute(value, "tm", [(2 * c - 1, 2 * c + 1) for c in range(firsts, chips, 2)])
    begin = call(
        functools.partial(final_kernel, firsts), row, [V] * (4 + len(cames)), flops=32 * size ** 2, moved=2 * size ** 2
    )(begin, handed, before0, before1, *cames)
    got = lax.ppermute(begin, "tm", [(b, a) for a, b in pairs])
    return call(
        out_kernel, jax.ShapeDtypeStruct((steps_here, width), F32), [V] * 4,
        flops=16 * size ** 2, moved=size ** 2,
    )(begin, got, maps, terms)


def solution(mesh):
    return jax.shard_map(
        shards,
        mesh=mesh,
        in_specs=(
            P("tm", None),
            P("tm", None),
            P("tm", "state", None, None),
            P("tm", "state"),
            P("tm", "state"),
            P("tm", "state", None),
            P(),
        ),
        out_specs=P("tm", "state"),
        check_vma=False,
    )
```

```python
import functools

import jax
import jax.numpy as jnp
from jax import lax
from jax.experimental import pallas as pl
from jax.experimental.pallas import tpu as pltpu
from jax.sharding import PartitionSpec as P

F32 = jnp.float32
BF16 = jnp.bfloat16
VMEM_LIMIT = 24 * 1024 * 1024
ROWS = 512


def three_parts(x):
    hi = x.astype(BF16).astype(F32)
    rest = x - hi
    mid = rest.astype(BF16).astype(F32)
    return hi, mid, rest - mid


def split_rows(x):
    hi, mid, lo = three_parts(x)
    row = lax.broadcasted_iota(jnp.int32, (16, x.shape[1]), 0)
    out = jnp.where(row == 0, hi, jnp.where(row == 1, mid, jnp.where(row == 2, lo, 0.0)))
    return out.astype(BF16)


def joined(rows):
    return jnp.sum(rows.astype(F32), axis=0, keepdims=True)


def times_t(x, *parts):
    left = split_rows(x)
    out = [
        joined(lax.dot_general(left, part, (((1,), (1,)), ((), ())), preferred_element_type=F32)) for part in parts
    ]
    return out[0] if len(out) == 1 else jnp.concatenate(out, axis=1)


def times(x, *parts):
    left = split_rows(x)
    return joined(product(left, *parts))


def product(left, *parts):
    rows = parts[0].shape[0]
    out = [
        jnp.dot(left[:, i * rows:(i + 1) * rows], part, preferred_element_type=F32) for i, part in enumerate(parts)
    ]
    return sum(out[1:], out[0])


def matmul(left_ref, right_ref, out_ref):
    def block(i, carry):
        at = pl.ds(pl.multiple_of(i * ROWS, ROWS), ROWS)
        out_ref[at, :] = jnp.dot(left_ref[at, :], right_ref[...], preferred_element_type=F32).astype(BF16)
        return carry

    lax.fori_loop(0, left_ref.shape[0] // ROWS, block, 0)


def core_here():
    return lax.rem(lax.axis_index("tm"), 2)


def chip_here():
    return lax.div(lax.axis_index("tm"), 2)


def drive_kernel(
    rows_ref, cols_ref, values_ref, blocks_ref, maps_ref, out_ref, weighted_ref, parts_ref, sems
):
    steps, count, side, _ = blocks_ref.shape
    later, width, size = maps_ref.shape
    copies = []
    for j in range(later):
        copies.append(pltpu.make_async_copy(maps_ref.at[j], out_ref.at[pl.ds(j * width, width), :], sems.at[j]))
        copies[j].start()
    weighted = values_ref[...].astype(F32)
    pieces = weighted_ref.shape[0]
    for r in range(pieces):
        weighted_ref[r] = weighted[:, r * side:(r + 1) * side]
    parts_ref[...] = jnp.zeros_like(parts_ref)
    piece = lax.broadcasted_iota(jnp.int32, (pieces, count), 0)
    column = lax.broadcasted_iota(jnp.int32, (size // side, count), 0)
    own = lax.broadcasted_iota(jnp.int32, (count, count * side), 0) == (
        lax.broadcasted_iota(jnp.int32, (count, count * side), 1) // side
    )
    for t in range(steps):
        chosen = (piece == rows_ref[t:t + 1, :]).astype(F32).astype(BF16)
        left = lax.dot_general(
            chosen, weighted_ref[:, t, :].astype(BF16), (((0,), (0,)), ((), ())), preferred_element_type=F32
        )
        left = jnp.concatenate([left] * count, axis=1)
        left = jnp.where(own, left, 0.0).astype(BF16)
        terms = jnp.dot(left, blocks_ref[t].reshape(count * side, side), preferred_element_type=F32)
        chosen = (column == cols_ref[t:t + 1, :]).astype(F32).astype(BF16)
        drive = sum(jnp.dot(chosen, part.astype(BF16), preferred_element_type=F32) for part in three_parts(terms))
        for i, part in enumerate(three_parts(drive)):
            for c in range(size // side):
                parts_ref[3 * t + i:3 * t + i + 1, c * side:(c + 1) * side] = part[c:c + 1, :]
    out_ref[later * width:, :] = parts_ref[...].astype(BF16)
    for copy in copies:
        copy.wait()


def rows_of(r, width, count):
    owner = lax.rem(lax.axis_index("state") + r + core_here() * (count - 2 * r), count)
    return pl.ds(pl.multiple_of(owner * width, width), width)


def fetched(count, pieces, j, whole_ref, sems, first):
    width = whole_ref.shape[0] // count
    copies = []
    for i, (r, piece) in enumerate(pieces):
        copy = pltpu.make_async_copy(
            piece.at[pl.ds(j * width, width), :], whole_ref.at[rows_of(r, width, count), :], sems.at[first + i]
        )
        copy.start()
        copies.append(copy)
    return copies


def two_kernel(count, *refs):
    pieces, (two_ref, slab_ref, next_ref, one_ref, sems) = list(enumerate(refs[:count])), refs[count:]
    width = slab_ref.shape[0]
    place = lax.axis_index("state")
    ones = fetched(count, pieces, 0, one_ref, sems, 0)
    nexts = fetched(count, pieces, 1, next_ref, sems, count)
    for copy in ones + nexts:
        copy.wait()
    matmul(next_ref, one_ref, two_ref)
    slab_ref[...] = two_ref[pl.ds(pl.multiple_of(place * width, width), width), :]


def three_kernel(count, have, two_ref, *refs):
    pieces = list(zip(have, refs[:len(have)]))
    three_ref, third_ref, fourth_ref, sems = refs[len(have):]
    width = third_ref.shape[0] // count
    copies = fetched(count, pieces, 0, third_ref, sems, 0)
    copies += fetched(count, pieces, 1, fourth_ref, sems, len(have))
    for copy in copies:
        copy.wait()
    for r in have:
        at = rows_of(r, width, count)
        three_ref[at, :] = jnp.dot(third_ref[at, :], two_ref[...], preferred_element_type=F32).astype(BF16)


def four_kernel(count, have, two_ref, threes_ref, thirds_ref, fourths_ref, *refs):
    pieces = refs[:count]
    four_ref, slab3_ref, slab4_ref, three_ref, third_ref, fourth_ref, drive_ref, parts_ref, sems = refs[count:]
    width = slab3_ref.shape[0]
    parts = []
    for i, r in enumerate(have):
        parts.append(pltpu.make_async_copy(pieces[r].at[pl.ds(2 * width, 16), :], parts_ref.at[i], sems.at[i]))
        parts[i].start()
    drive = jnp.zeros(drive_ref.shape, F32)
    for r in range(count):
        if r not in have:
            at = rows_of(r, width, count)
            third_ref[at, :] = pieces[r][:width, :]
            fourth_ref[at, :] = pieces[r][width:2 * width, :]
            three_ref[at, :] = jnp.dot(pieces[r][:width, :], two_ref[...], preferred_element_type=F32).astype(BF16)
            drive += pieces[r][2 * width:, :].astype(F32)
    mine = pl.ds(pl.multiple_of(lax.axis_index("state") * width, width), width)
    slab3_ref[...] = three_ref[mine, :]

    @pl.when(core_here() == 0)
    def _():
        matmul(fourth_ref, three_ref, four_ref)
        slab4_ref[...] = four_ref[mine, :]

    for copy in parts:
        copy.wait()
    drive_ref[...] = drive + jnp.sum(parts_ref[...].astype(F32), axis=0)


def second_kernel(three_ref, fourth_ref, four_ref, slab4_ref):
    width, size = slab4_ref.shape
    mine = pl.ds(pl.multiple_of(lax.axis_index("state") * width, width), width)
    turned = chip_here() < DIRECT

    @pl.when(jnp.logical_and(core_here() != 0, turned))
    def _():
        def block(i, carry):
            at = pl.ds(pl.multiple_of(i * ROWS, ROWS), ROWS)
            out = jnp.dot(fourth_ref[at, :], three_ref[...], preferred_element_type=F32)
            four_ref[:, at] = out.T.astype(BF16)
            return carry

        lax.fori_loop(0, size // ROWS, block, 0)
        slab4_ref[...] = four_ref[:, mine].astype(F32).T.astype(BF16)

    @pl.when(jnp.logical_and(core_here() != 0, jnp.logical_not(turned)))
    def _():
        matmul(fourth_ref, three_ref, four_ref)
        slab4_ref[...] = four_ref[mine, :]


def local_kernel(drive_ref, second_ref, third_ref, fourth_ref, locals_ref, term_ref):
    local = joined(drive_ref[0:3, :])
    locals_ref[0:1, :] = local
    for j, map_ref in enumerate((second_ref, third_ref, fourth_ref)):
        local = times_t(local, map_ref[...]) + joined(drive_ref[3 * j + 3:3 * j + 6, :])
        locals_ref[j + 1:j + 2, :] = local
    term_ref[...] = split_rows(local)


DIRECT = 2


def pair_kernel(half, own_ref, own_term_ref, other_ref, other_term_ref, turned_ref):
    rows = own_ref.shape[0] // 2
    at = slice(half * rows, (half + 1) * rows)

    @pl.when(jnp.logical_and(core_here() != 0, chip_here() >= DIRECT))
    def _():
        for i in range(2):
            out = jnp.dot(own_ref[i * rows:(i + 1) * rows, :], other_ref[:, at], preferred_element_type=F32)
            turned_ref[:rows, i * rows:(i + 1) * rows] = out.T.astype(BF16)
        if half == 1:
            term = times_t(joined(other_term_ref[...]), own_ref[...]) + joined(own_term_ref[...])
            turned_ref[rows:, :] = split_rows(term)


def applied(x, turned0_ref, turned1_ref):
    rows = turned0_ref.shape[0]
    return times(x, turned0_ref[...], turned1_ref[:rows, :]) + joined(turned1_ref[rows:, :])


def direct_kernel(turn, begin_ref, came_ref, own_ref, own_term_ref, other_ref, other_term_ref, held_ref, value_ref):
    held_ref[...] = begin_ref[...]
    value_ref[...] = begin_ref[...]

    @pl.when(lax.axis_index("tm") == 2 * turn + 1)
    def _():
        begin = came_ref[...]
        held_ref[...] = begin
        between = times_t(begin, other_ref[...]) + joined(other_term_ref[...])
        value_ref[...] = times(between, own_ref[...]) + joined(own_term_ref[...])


def hop_kernel(turn, begin_ref, came_ref, turned0_ref, turned1_ref, held_ref, value_ref):
    here = lax.axis_index("tm") == 2 * turn + 1

    @pl.when(here)
    def _():
        begin = came_ref[...]
        held_ref[...] = begin
        value_ref[...] = applied(begin, turned0_ref, turned1_ref)

    @pl.when(jnp.logical_not(here))
    def _():
        held_ref[...] = begin_ref[...]
        value_ref[...] = begin_ref[...]


def double_kernel(half, firsts, came_ref, turned0_ref, turned1_ref, double_ref):
    rows = turned0_ref.shape[0]
    chip = chip_here()

    @pl.when((core_here() != 0) & (chip > firsts) & (lax.rem(chip, 2) == 1) & (chip < 2 * firsts - 1))
    def _():
        double_ref[:rows, :] = product(came_ref[:rows, :], turned0_ref[...], turned1_ref[:rows, :]).astype(BF16)
        if half == 1:
            double_ref[rows:, :] = split_rows(applied(joined(came_ref[rows:, :]), turned0_ref, turned1_ref))


def far_kernel(chip, came_ref, before_ref, double0_ref, double1_ref, value_ref):
    here = lax.axis_index("tm") == 2 * chip + 1

    @pl.when(here)
    def _():
        value_ref[...] = applied(came_ref[...], double0_ref, double1_ref)

    @pl.when(jnp.logical_not(here))
    def _():
        value_ref[...] = before_ref[...]


def final_kernel(firsts, held_ref, handed_ref, map0_ref, map1_ref, *refs):
    cames, begin_ref = refs[:-1], refs[-1]
    chip = chip_here()
    handed = jnp.logical_and(chip >= firsts, lax.rem(chip, 2) == 0)
    begin_ref[...] = jnp.where(handed, handed_ref[...], held_ref[...])
    for i, came_ref in enumerate(cames):
        @pl.when(lax.axis_index("tm") == 2 * (firsts + 1 + 2 * i) + 1)
        def _():
            begin_ref[...] = applied(came_ref[...], map0_ref, map1_ref)


def ready_kernel(other_ref, other_term_ref, locals_ref, after_ref, *refs):
    slabs, (second_ref, maps_ref, terms_ref) = refs[:-3], refs[-3:]
    width, size = slabs[1].shape
    mine = pl.ds(pl.multiple_of(lax.axis_index("state") * width, width), width)

    @pl.when(core_here() == 0)
    def _():
        for j, slab_ref in enumerate(slabs):
            maps_ref[:, j * width:(j + 1) * width] = slab_ref[:width, :].astype(F32).T.astype(BF16)
            terms_ref[j:j + 1, :] = locals_ref[j:j + 1, mine]

    @pl.when(core_here() != 0)
    def _():
        for j, slab_ref in enumerate(slabs[:-1] + (second_ref,)):
            at = slice(j * width, (j + 1) * width)
            out = jnp.dot(slab_ref[:width, :], other_ref[...], preferred_element_type=F32)
            maps_ref[:, at] = out.T.astype(BF16)
            term = times_t(joined(other_term_ref[...]), slab_ref[:width, :])
            terms_ref[j:j + 1, :] = term + locals_ref[j:j + 1, mine]


def out_kernel(begin_ref, got_ref, maps_ref, terms_ref, out_ref):
    steps, width = out_ref.shape
    begin = jnp.where(core_here() == 0, got_ref[...], begin_ref[...])
    row = times(begin, maps_ref[...])
    for j in range(steps):
        out_ref[j:j + 1, :] = row[:, j * width:(j + 1) * width] + terms_ref[j:j + 1, :]


def call(kernel, out_shape, spaces, scratch=(), flops=0, moved=0, aliases={}):
    return pl.pallas_call(
        kernel,
        out_shape=out_shape,
        in_specs=[pl.BlockSpec(memory_space=s) for s in spaces],
        out_specs=jax.tree.map(lambda _: pl.BlockSpec(memory_space=pltpu.VMEM), out_shape),
        scratch_shapes=list(scratch),
        input_output_aliases=aliases,
        compiler_params=pltpu.CompilerParams(vmem_limit_bytes=VMEM_LIMIT),
        cost_estimate=pl.CostEstimate(flops=flops, bytes_accessed=moved, transcendentals=0),
    )


def after(value, *needed):
    return lax.optimization_barrier((value, needed))[0]


def ring_rounds(parts, needed):
    lines, count = lax.axis_size("tm"), lax.axis_size("state")
    forward = [(b * count + i, b * count + (i + 1 - 2 * (b % 2)) % count) for b in range(lines) for i in range(count)]
    backward = [(there, here) for here, there in forward]
    half = count // 2
    found = [{0: part} for part in parts]
    for r in range(1, half + 1):
        for i, pieces in enumerate(found):
            left, right = pieces[(count - r + 1) % count], pieces[r - 1]
            more = needed(r, i, found)
            if more:
                left, right = after((left, right), *more)
            if r < half or i % 2 == 0:
                pieces[count - r] = lax.ppermute(left, ("tm", "state"), forward)
            if r < half or i % 2 == 1:
                pieces[r] = lax.ppermute(right, ("tm", "state"), backward)
    return [[pieces[r] for r in range(count)] for pieces in found]


def shards(observations, precisions, blocks, block_rows, block_cols, transition, prior):
    steps_here, width, size = transition.shape
    side = blocks.shape[2]
    count = lax.axis_size("state")
    blocks_of_time = lax.axis_size("tm")
    V, S, A = pltpu.VMEM, pltpu.SMEM, pl.ANY

    matrix = jax.ShapeDtypeStruct((size, size), BF16)
    slab = jax.ShapeDtypeStruct((width, size), BF16)
    rows = jax.ShapeDtypeStruct((16, size), BF16)
    steps = jax.ShapeDtypeStruct((steps_here, size), F32)
    row = jax.ShapeDtypeStruct((1, size), F32)
    whole = pltpu.VMEM((size, size), BF16)

    half = steps_here // 2
    pieces = observations.shape[1] // side
    packed = call(
        drive_kernel, jax.ShapeDtypeStruct((half * width + 16, size), BF16), [V] * 4 + [A],
        [
            pltpu.VMEM((pieces, steps_here, side), F32),
            pltpu.VMEM((16, size), F32),
            pltpu.SemaphoreType.DMA((half,)),
        ],
        flops=10 ** 7, moved=2 ** 21,
    )(block_rows, block_cols, (precisions * observations).astype(BF16), blocks, transition[half:])
    early, late = ring_rounds(
        [transition[:half].reshape(half * width, size), packed],
        lambda r, i, found: (packed,) if (r, i) == (2, 0) else (),
    )
    two, slab2, second = call(
        functools.partial(two_kernel, count), (matrix, slab, matrix), [A] * count,
        [whole, pltpu.SemaphoreType.DMA((2 * count,))], flops=2 * size ** 3, moved=6 * size ** 2,
    )(*early)
    have = [r for r in range(count) if r not in (count // 2, count // 2 + 1)]
    three, third, fourth = call(
        functools.partial(three_kernel, count, have), (matrix, matrix, matrix), [V] + [A] * len(have),
        [pltpu.SemaphoreType.DMA((2 * len(have),))], flops=2 * size ** 3, moved=6 * size ** 2,
    )(two, *[late[r] for r in have])
    sent, slab3, slab4, three, third, fourth, drive = call(
        functools.partial(four_kernel, count, have),
        (matrix, slab, slab, matrix, matrix, matrix, jax.ShapeDtypeStruct((16, size), F32)),
        [V] * 4 + [A if r in have else V for r in range(count)],
        [pltpu.VMEM((len(have), 16, size), BF16), pltpu.SemaphoreType.DMA((len(have),))],
        flops=2 * size ** 3, moved=6 * size ** 2, aliases={1: 3, 2: 4, 3: 5},
    )(two, three, third, fourth, *late)
    pairs = [(i, i + 1) for i in range(0, blocks_of_time, 2)]
    other = lax.ppermute(sent, "tm", pairs)
    own, slab5 = call(second_kernel, (matrix, slab), [V] * 2, flops=2 * size ** 3, moved=6 * size ** 2)(three, fourth)
    locals_, own_term = call(
        local_kernel, (steps, rows), [V] * 4, flops=96 * size ** 2, moved=6 * size ** 2
    )(drive, second, third, fourth)
    other_term = lax.ppermute(own_term, "tm", pairs)

    chips = blocks_of_time // 2
    firsts = chips // 2
    part = jax.ShapeDtypeStruct((size // 2, size), BF16)
    longer = jax.ShapeDtypeStruct((size // 2 + 16, size), BF16)
    blocks_here = (own, own_term, other, other_term)
    onward = [(2 * c + 1, 2 * c + 3) for c in range(firsts, chips, 2)]
    half_cost = dict(flops=size ** 3, moved=6 * size ** 2)
    turned0 = call(functools.partial(pair_kernel, 0), part, [V] * 4, **half_cost)(*blocks_here)
    before0 = lax.ppermute(turned0, "tm", onward)
    turned1 = call(functools.partial(pair_kernel, 1), longer, [V] * 4, **half_cost)(*blocks_here)
    before1 = lax.ppermute(turned1, "tm", onward)

    begin = after(prior.reshape(1, size), turned1)
    came = begin
    for turn in range(firsts):
        if turn < DIRECT:
            begin, value = call(
                functools.partial(direct_kernel, turn), (row, row), [V] * 6,
                flops=64 * size ** 2, moved=4 * size ** 2,
            )(begin, came, *blocks_here)
        else:
            begin, value = call(
                functools.partial(hop_kernel, turn), (row, row), [V] * 4,
                flops=32 * size ** 2, moved=2 * size ** 2,
            )(begin, came, turned0, turned1)
        came = lax.ppermute(value, "tm", [(2 * turn + 1, 2 * turn + (3 if turn + 1 < firsts else 5))])
        if turn == 3:
            maps, terms = call(
                ready_kernel,
                (jax.ShapeDtypeStruct((size, steps_here * width), BF16), jax.ShapeDtypeStruct((steps_here, width), F32)),
                [V] * 9, flops=size ** 3, moved=4 * size ** 2,
            )(other, other_term, locals_, value, early[0], slab2, slab3, slab4, slab5)
        if turn == 4:
            came = after(came, maps)
    double0 = call(functools.partial(double_kernel, 0, firsts), part, [V] * 3, **half_cost)(before0, turned0, turned1)
    double1 = call(functools.partial(double_kernel, 1, firsts), longer, [V] * 3, **half_cost)(before1, turned0, turned1)
    cames = [came]
    for chip in range(firsts + 1, chips - 1, 2):
        value = call(
            functools.partial(far_kernel, chip), row, [V] * 4, flops=32 * size ** 2, moved=2 * size ** 2
        )(came, value, double0, double1)
        came = lax.ppermute(value, "tm", [(2 * chip + 1, 2 * chip + 5)])
        cames.append(came)
    handed = lax.ppermute(value, "tm", [(2 * c - 1, 2 * c + 1) for c in range(firsts, chips, 2)])
    begin = call(
        functools.partial(final_kernel, firsts), row, [V] * (4 + len(cames)), flops=32 * size ** 2, moved=2 * size ** 2
    )(begin, handed, before0, before1, *cames)
    got = lax.ppermute(begin, "tm", [(b, a) for a, b in pairs])
    return call(
        out_kernel, jax.ShapeDtypeStruct((steps_here, width), F32), [V] * 4,
        flops=16 * size ** 2, moved=size ** 2,
    )(begin, got, maps, terms)


def solution(mesh):
    return jax.shard_map(
        shards,
        mesh=mesh,
        in_specs=(
            P("tm", None),
            P("tm", None),
            P("tm", "state", None, None),
            P("tm", "state"),
            P("tm", "state"),
            P("tm", "state", None),
            P(),
        ),
        out_specs=P("tm", "state"),
        check_vma=False,
    )
```

```python
import functools

import jax
import jax.numpy as jnp
from jax import lax
from jax.experimental import pallas as pl
from jax.experimental.pallas import tpu as pltpu
from jax.sharding import PartitionSpec as P

F32 = jnp.float32
BF16 = jnp.bfloat16
VMEM_LIMIT = 24 * 1024 * 1024
ROWS = 1024


def three_parts(x):
    hi = x.astype(BF16).astype(F32)
    rest = x - hi
    mid = rest.astype(BF16).astype(F32)
    return hi, mid, rest - mid


def split_rows(x):
    hi, mid, lo = three_parts(x)
    row = lax.broadcasted_iota(jnp.int32, (16, x.shape[1]), 0)
    out = jnp.where(row == 0, hi, jnp.where(row == 1, mid, jnp.where(row == 2, lo, 0.0)))
    return out.astype(BF16)


def joined(rows):
    return jnp.sum(rows.astype(F32), axis=0, keepdims=True)


def times_t(x, *parts):
    left = split_rows(x)
    out = [
        joined(lax.dot_general(left, part, (((1,), (1,)), ((), ())), preferred_element_type=F32)) for part in parts
    ]
    return out[0] if len(out) == 1 else jnp.concatenate(out, axis=1)


def times(x, *parts):
    left = split_rows(x)
    return joined(product(left, *parts))


def product(left, *parts):
    rows = parts[0].shape[0]
    out = [
        jnp.dot(left[:, i * rows:(i + 1) * rows], part, preferred_element_type=F32) for i, part in enumerate(parts)
    ]
    return sum(out[1:], out[0])


def matmul(left_ref, right_ref, out_ref):
    def block(i, carry):
        at = pl.ds(pl.multiple_of(i * ROWS, ROWS), ROWS)
        out_ref[at, :] = jnp.dot(left_ref[at, :], right_ref[...], preferred_element_type=F32).astype(BF16)
        return carry

    lax.fori_loop(0, left_ref.shape[0] // ROWS, block, 0)


def core_here():
    return lax.rem(lax.axis_index("tm"), 2)


def chip_here():
    return lax.div(lax.axis_index("tm"), 2)


def drive_kernel(
    rows_ref, cols_ref, values_ref, blocks_ref, maps_ref, out_ref, weighted_ref, parts_ref, sems
):
    steps, count, side, _ = blocks_ref.shape
    later, width, size = maps_ref.shape
    copies = []
    for j in range(later):
        copies.append(pltpu.make_async_copy(maps_ref.at[j], out_ref.at[pl.ds(j * width, width), :], sems.at[j]))
        copies[j].start()
    weighted = values_ref[...].astype(F32)
    pieces = weighted_ref.shape[0]
    for r in range(pieces):
        weighted_ref[r] = weighted[:, r * side:(r + 1) * side]
    parts_ref[...] = jnp.zeros_like(parts_ref)
    piece = lax.broadcasted_iota(jnp.int32, (pieces, count), 0)
    column = lax.broadcasted_iota(jnp.int32, (size // side, count), 0)
    own = lax.broadcasted_iota(jnp.int32, (count, count * side), 0) == (
        lax.broadcasted_iota(jnp.int32, (count, count * side), 1) // side
    )
    for t in range(steps):
        chosen = (piece == rows_ref[t:t + 1, :]).astype(F32).astype(BF16)
        left = lax.dot_general(
            chosen, weighted_ref[:, t, :].astype(BF16), (((0,), (0,)), ((), ())), preferred_element_type=F32
        )
        left = jnp.concatenate([left] * count, axis=1)
        left = jnp.where(own, left, 0.0).astype(BF16)
        terms = jnp.dot(left, blocks_ref[t].reshape(count * side, side), preferred_element_type=F32)
        chosen = (column == cols_ref[t:t + 1, :]).astype(F32).astype(BF16)
        drive = sum(jnp.dot(chosen, part.astype(BF16), preferred_element_type=F32) for part in three_parts(terms))
        for i, part in enumerate(three_parts(drive)):
            for c in range(size // side):
                parts_ref[3 * t + i:3 * t + i + 1, c * side:(c + 1) * side] = part[c:c + 1, :]
    out_ref[later * width:, :] = parts_ref[...].astype(BF16)
    for copy in copies:
        copy.wait()


def rows_of(r, width, count):
    owner = lax.rem(lax.axis_index("state") + r + core_here() * (count - 2 * r), count)
    return pl.ds(pl.multiple_of(owner * width, width), width)


def fetched(count, pieces, j, whole_ref, sems, first):
    width = whole_ref.shape[0] // count
    copies = []
    for i, (r, piece) in enumerate(pieces):
        copy = pltpu.make_async_copy(
            piece.at[pl.ds(j * width, width), :], whole_ref.at[rows_of(r, width, count), :], sems.at[first + i]
        )
        copy.start()
        copies.append(copy)
    return copies


def two_kernel(count, *refs):
    pieces, (two_ref, slab_ref, next_ref, one_ref, sems) = list(enumerate(refs[:count])), refs[count:]
    width = slab_ref.shape[0]
    place = lax.axis_index("state")
    ones = fetched(count, pieces, 0, one_ref, sems, 0)
    nexts = fetched(count, pieces, 1, next_ref, sems, count)
    for copy in ones + nexts:
        copy.wait()
    matmul(next_ref, one_ref, two_ref)
    slab_ref[...] = two_ref[pl.ds(pl.multiple_of(place * width, width), width), :]


def three_kernel(count, have, two_ref, *refs):
    pieces = list(zip(have, refs[:len(have)]))
    three_ref, third_ref, fourth_ref, sems = refs[len(have):]
    width = third_ref.shape[0] // count
    copies = fetched(count, pieces, 0, third_ref, sems, 0)
    copies += fetched(count, pieces, 1, fourth_ref, sems, len(have))
    for copy in copies:
        copy.wait()
    for r in have:
        at = rows_of(r, width, count)
        three_ref[at, :] = jnp.dot(third_ref[at, :], two_ref[...], preferred_element_type=F32).astype(BF16)


def four_kernel(count, have, two_ref, threes_ref, thirds_ref, fourths_ref, *refs):
    pieces = refs[:count]
    four_ref, slab3_ref, slab4_ref, three_ref, third_ref, fourth_ref, drive_ref, parts_ref, sems = refs[count:]
    width = slab3_ref.shape[0]
    parts = []
    for i, r in enumerate(have):
        parts.append(pltpu.make_async_copy(pieces[r].at[pl.ds(2 * width, 16), :], parts_ref.at[i], sems.at[i]))
        parts[i].start()
    drive = jnp.zeros(drive_ref.shape, F32)
    for r in range(count):
        if r not in have:
            at = rows_of(r, width, count)
            third_ref[at, :] = pieces[r][:width, :]
            fourth_ref[at, :] = pieces[r][width:2 * width, :]
            three_ref[at, :] = jnp.dot(pieces[r][:width, :], two_ref[...], preferred_element_type=F32).astype(BF16)
            drive += pieces[r][2 * width:, :].astype(F32)
    mine = pl.ds(pl.multiple_of(lax.axis_index("state") * width, width), width)
    slab3_ref[...] = three_ref[mine, :]

    @pl.when(core_here() == 0)
    def _():
        matmul(fourth_ref, three_ref, four_ref)
        slab4_ref[...] = four_ref[mine, :]

    for copy in parts:
        copy.wait()
    drive_ref[...] = drive + jnp.sum(parts_ref[...].astype(F32), axis=0)


def second_kernel(three_ref, fourth_ref, four_ref, slab4_ref):
    width, size = slab4_ref.shape
    mine = pl.ds(pl.multiple_of(lax.axis_index("state") * width, width), width)
    turned = chip_here() < DIRECT

    @pl.when(jnp.logical_and(core_here() != 0, turned))
    def _():
        def block(i, carry):
            at = pl.ds(pl.multiple_of(i * ROWS, ROWS), ROWS)
            out = jnp.dot(fourth_ref[at, :], three_ref[...], preferred_element_type=F32)
            four_ref[:, at] = out.T.astype(BF16)
            return carry

        lax.fori_loop(0, size // ROWS, block, 0)
        slab4_ref[...] = four_ref[:, mine].astype(F32).T.astype(BF16)

    @pl.when(jnp.logical_and(core_here() != 0, jnp.logical_not(turned)))
    def _():
        matmul(fourth_ref, three_ref, four_ref)
        slab4_ref[...] = four_ref[mine, :]


def local_kernel(drive_ref, second_ref, third_ref, fourth_ref, locals_ref, term_ref):
    local = joined(drive_ref[0:3, :])
    locals_ref[0:1, :] = local
    for j, map_ref in enumerate((second_ref, third_ref, fourth_ref)):
        local = times_t(local, map_ref[...]) + joined(drive_ref[3 * j + 3:3 * j + 6, :])
        locals_ref[j + 1:j + 2, :] = local
    term_ref[...] = split_rows(local)


DIRECT = 2


def pair_kernel(half, own_ref, own_term_ref, other_ref, other_term_ref, turned_ref):
    rows = own_ref.shape[0] // 2
    at = slice(half * rows, (half + 1) * rows)

    @pl.when(jnp.logical_and(core_here() != 0, chip_here() >= DIRECT))
    def _():
        for i in range(2):
            out = jnp.dot(own_ref[i * rows:(i + 1) * rows, :], other_ref[:, at], preferred_element_type=F32)
            turned_ref[:rows, i * rows:(i + 1) * rows] = out.T.astype(BF16)
        if half == 1:
            term = times_t(joined(other_term_ref[...]), own_ref[...]) + joined(own_term_ref[...])
            turned_ref[rows:, :] = split_rows(term)


def applied(x, turned0_ref, turned1_ref):
    rows = turned0_ref.shape[0]
    return times(x, turned0_ref[...], turned1_ref[:rows, :]) + joined(turned1_ref[rows:, :])


def direct_kernel(turn, begin_ref, came_ref, own_ref, own_term_ref, other_ref, other_term_ref, held_ref, value_ref):
    held_ref[...] = begin_ref[...]
    value_ref[...] = begin_ref[...]

    @pl.when(lax.axis_index("tm") == 2 * turn + 1)
    def _():
        begin = came_ref[...]
        held_ref[...] = begin
        between = times_t(begin, other_ref[...]) + joined(other_term_ref[...])
        value_ref[...] = times(between, own_ref[...]) + joined(own_term_ref[...])


def hop_kernel(turn, begin_ref, came_ref, turned0_ref, turned1_ref, held_ref, value_ref):
    here = lax.axis_index("tm") == 2 * turn + 1

    @pl.when(here)
    def _():
        begin = came_ref[...]
        held_ref[...] = begin
        value_ref[...] = applied(begin, turned0_ref, turned1_ref)

    @pl.when(jnp.logical_not(here))
    def _():
        held_ref[...] = begin_ref[...]
        value_ref[...] = begin_ref[...]


def double_kernel(half, firsts, came_ref, turned0_ref, turned1_ref, double_ref):
    rows = turned0_ref.shape[0]
    chip = chip_here()

    @pl.when((core_here() != 0) & (chip > firsts) & (lax.rem(chip, 2) == 1) & (chip < 2 * firsts - 1))
    def _():
        double_ref[:rows, :] = product(came_ref[:rows, :], turned0_ref[...], turned1_ref[:rows, :]).astype(BF16)
        if half == 1:
            double_ref[rows:, :] = split_rows(applied(joined(came_ref[rows:, :]), turned0_ref, turned1_ref))


def far_kernel(chip, came_ref, before_ref, double0_ref, double1_ref, value_ref):
    here = lax.axis_index("tm") == 2 * chip + 1

    @pl.when(here)
    def _():
        value_ref[...] = applied(came_ref[...], double0_ref, double1_ref)

    @pl.when(jnp.logical_not(here))
    def _():
        value_ref[...] = before_ref[...]


def final_kernel(firsts, held_ref, handed_ref, map0_ref, map1_ref, *refs):
    cames, begin_ref = refs[:-1], refs[-1]
    chip = chip_here()
    handed = jnp.logical_and(chip >= firsts, lax.rem(chip, 2) == 0)
    begin_ref[...] = jnp.where(handed, handed_ref[...], held_ref[...])
    for i, came_ref in enumerate(cames):
        @pl.when(lax.axis_index("tm") == 2 * (firsts + 1 + 2 * i) + 1)
        def _():
            begin_ref[...] = applied(came_ref[...], map0_ref, map1_ref)


def ready_kernel(other_ref, other_term_ref, locals_ref, after_ref, *refs):
    slabs, (second_ref, maps_ref, terms_ref) = refs[:-3], refs[-3:]
    width, size = slabs[1].shape
    mine = pl.ds(pl.multiple_of(lax.axis_index("state") * width, width), width)

    @pl.when(core_here() == 0)
    def _():
        for j, slab_ref in enumerate(slabs):
            maps_ref[:, j * width:(j + 1) * width] = slab_ref[:width, :].astype(F32).T.astype(BF16)
            terms_ref[j:j + 1, :] = locals_ref[j:j + 1, mine]

    @pl.when(core_here() != 0)
    def _():
        for j, slab_ref in enumerate(slabs[:-1] + (second_ref,)):
            at = slice(j * width, (j + 1) * width)
            out = jnp.dot(slab_ref[:width, :], other_ref[...], preferred_element_type=F32)
            maps_ref[:, at] = out.T.astype(BF16)
            term = times_t(joined(other_term_ref[...]), slab_ref[:width, :])
            terms_ref[j:j + 1, :] = term + locals_ref[j:j + 1, mine]


def out_kernel(begin_ref, got_ref, maps_ref, terms_ref, out_ref):
    steps, width = out_ref.shape
    begin = jnp.where(core_here() == 0, got_ref[...], begin_ref[...])
    row = times(begin, maps_ref[...])
    for j in range(steps):
        out_ref[j:j + 1, :] = row[:, j * width:(j + 1) * width] + terms_ref[j:j + 1, :]


def call(kernel, out_shape, spaces, scratch=(), flops=0, moved=0, aliases={}):
    return pl.pallas_call(
        kernel,
        out_shape=out_shape,
        in_specs=[pl.BlockSpec(memory_space=s) for s in spaces],
        out_specs=jax.tree.map(lambda _: pl.BlockSpec(memory_space=pltpu.VMEM), out_shape),
        scratch_shapes=list(scratch),
        input_output_aliases=aliases,
        compiler_params=pltpu.CompilerParams(vmem_limit_bytes=VMEM_LIMIT),
        cost_estimate=pl.CostEstimate(flops=flops, bytes_accessed=moved, transcendentals=0),
    )


def after(value, *needed):
    return lax.optimization_barrier((value, needed))[0]


def ring_rounds(parts, needed):
    lines, count = lax.axis_size("tm"), lax.axis_size("state")
    forward = [(b * count + i, b * count + (i + 1 - 2 * (b % 2)) % count) for b in range(lines) for i in range(count)]
    backward = [(there, here) for here, there in forward]
    half = count // 2
    found = [{0: part} for part in parts]
    for r in range(1, half + 1):
        for i, pieces in enumerate(found):
            left, right = pieces[(count - r + 1) % count], pieces[r - 1]
            more = needed(r, i, found)
            if more:
                left, right = after((left, right), *more)
            if r < half or i % 2 == 0:
                pieces[count - r] = lax.ppermute(left, ("tm", "state"), forward)
            if r < half or i % 2 == 1:
                pieces[r] = lax.ppermute(right, ("tm", "state"), backward)
    return [[pieces[r] for r in range(count)] for pieces in found]


def shards(observations, precisions, blocks, block_rows, block_cols, transition, prior):
    steps_here, width, size = transition.shape
    side = blocks.shape[2]
    count = lax.axis_size("state")
    blocks_of_time = lax.axis_size("tm")
    V, S, A = pltpu.VMEM, pltpu.SMEM, pl.ANY

    matrix = jax.ShapeDtypeStruct((size, size), BF16)
    slab = jax.ShapeDtypeStruct((width, size), BF16)
    rows = jax.ShapeDtypeStruct((16, size), BF16)
    steps = jax.ShapeDtypeStruct((steps_here, size), F32)
    row = jax.ShapeDtypeStruct((1, size), F32)
    whole = pltpu.VMEM((size, size), BF16)

    half = steps_here // 2
    pieces = observations.shape[1] // side
    packed = call(
        drive_kernel, jax.ShapeDtypeStruct((half * width + 16, size), BF16), [V] * 4 + [A],
        [
            pltpu.VMEM((pieces, steps_here, side), F32),
            pltpu.VMEM((16, size), F32),
            pltpu.SemaphoreType.DMA((half,)),
        ],
        flops=10 ** 7, moved=2 ** 21,
    )(block_rows, block_cols, (precisions * observations).astype(BF16), blocks, transition[half:])
    early, late = ring_rounds(
        [transition[:half].reshape(half * width, size), packed],
        lambda r, i, found: (packed,) if (r, i) == (2, 0) else (),
    )
    two, slab2, second = call(
        functools.partial(two_kernel, count), (matrix, slab, matrix), [A] * count,
        [whole, pltpu.SemaphoreType.DMA((2 * count,))], flops=2 * size ** 3, moved=6 * size ** 2,
    )(*early)
    have = [r for r in range(count) if r not in (count // 2, count // 2 + 1)]
    three, third, fourth = call(
        functools.partial(three_kernel, count, have), (matrix, matrix, matrix), [V] + [A] * len(have),
        [pltpu.SemaphoreType.DMA((2 * len(have),))], flops=2 * size ** 3, moved=6 * size ** 2,
    )(two, *[late[r] for r in have])
    sent, slab3, slab4, three, third, fourth, drive = call(
        functools.partial(four_kernel, count, have),
        (matrix, slab, slab, matrix, matrix, matrix, jax.ShapeDtypeStruct((16, size), F32)),
        [V] * 4 + [A if r in have else V for r in range(count)],
        [pltpu.VMEM((len(have), 16, size), BF16), pltpu.SemaphoreType.DMA((len(have),))],
        flops=2 * size ** 3, moved=6 * size ** 2, aliases={1: 3, 2: 4, 3: 5},
    )(two, three, third, fourth, *late)
    pairs = [(i, i + 1) for i in range(0, blocks_of_time, 2)]
    other = lax.ppermute(sent, "tm", pairs)
    own, slab5 = call(second_kernel, (matrix, slab), [V] * 2, flops=2 * size ** 3, moved=6 * size ** 2)(three, fourth)
    locals_, own_term = call(
        local_kernel, (steps, rows), [V] * 4, flops=96 * size ** 2, moved=6 * size ** 2
    )(drive, second, third, fourth)
    other_term = lax.ppermute(own_term, "tm", pairs)

    chips = blocks_of_time // 2
    firsts = chips // 2
    part = jax.ShapeDtypeStruct((size // 2, size), BF16)
    longer = jax.ShapeDtypeStruct((size // 2 + 16, size), BF16)
    blocks_here = (own, own_term, other, other_term)
    onward = [(2 * c + 1, 2 * c + 3) for c in range(firsts, chips, 2)]
    half_cost = dict(flops=size ** 3, moved=6 * size ** 2)
    turned0 = call(functools.partial(pair_kernel, 0), part, [V] * 4, **half_cost)(*blocks_here)
    before0 = lax.ppermute(turned0, "tm", onward)
    turned1 = call(functools.partial(pair_kernel, 1), longer, [V] * 4, **half_cost)(*blocks_here)
    before1 = lax.ppermute(turned1, "tm", onward)

    begin = after(prior.reshape(1, size), turned1)
    came = begin
    for turn in range(firsts):
        if turn < DIRECT:
            begin, value = call(
                functools.partial(direct_kernel, turn), (row, row), [V] * 6,
                flops=64 * size ** 2, moved=4 * size ** 2,
            )(begin, came, *blocks_here)
        else:
            begin, value = call(
                functools.partial(hop_kernel, turn), (row, row), [V] * 4,
                flops=32 * size ** 2, moved=2 * size ** 2,
            )(begin, came, turned0, turned1)
        came = lax.ppermute(value, "tm", [(2 * turn + 1, 2 * turn + (3 if turn + 1 < firsts else 5))])
        if turn == 3:
            maps, terms = call(
                ready_kernel,
                (jax.ShapeDtypeStruct((size, steps_here * width), BF16), jax.ShapeDtypeStruct((steps_here, width), F32)),
                [V] * 9, flops=size ** 3, moved=4 * size ** 2,
            )(other, other_term, locals_, value, early[0], slab2, slab3, slab4, slab5)
        if turn == 4:
            came = after(came, maps)
    double0 = call(functools.partial(double_kernel, 0, firsts), part, [V] * 3, **half_cost)(before0, turned0, turned1)
    double1 = call(functools.partial(double_kernel, 1, firsts), longer, [V] * 3, **half_cost)(before1, turned0, turned1)
    cames = [came]
    for chip in range(firsts + 1, chips - 1, 2):
        value = call(
            functools.partial(far_kernel, chip), row, [V] * 4, flops=32 * size ** 2, moved=2 * size ** 2
        )(came, value, double0, double1)
        came = lax.ppermute(value, "tm", [(2 * chip + 1, 2 * chip + 5)])
        cames.append(came)
    handed = lax.ppermute(value, "tm", [(2 * c - 1, 2 * c + 1) for c in range(firsts, chips, 2)])
    begin = call(
        functools.partial(final_kernel, firsts), row, [V] * (4 + len(cames)), flops=32 * size ** 2, moved=2 * size ** 2
    )(begin, handed, before0, before1, *cames)
    got = lax.ppermute(begin, "tm", [(b, a) for a, b in pairs])
    return call(
        out_kernel, jax.ShapeDtypeStruct((steps_here, width), F32), [V] * 4,
        flops=16 * size ** 2, moved=size ** 2,
    )(begin, got, maps, terms)


def solution(mesh):
    return jax.shard_map(
        shards,
        mesh=mesh,
        in_specs=(
            P("tm", None),
            P("tm", None),
            P("tm", "state", None, None),
            P("tm", "state"),
            P("tm", "state"),
            P("tm", "state", None),
            P(),
        ),
        out_specs=P("tm", "state"),
        check_vma=False,
    )
```
